32 devices in a mesh: section: 4 (over y, x), ctx: 4 (over z), tp: 2 (over core).
Axes of the slice: x: 2, y: 2, z: 4, core: 2. Of those that a mesh axis runs over, the one named last changes fastest.
Arguments:
- hidden: bfloat16 [4, 512, 8192], P('section', 'ctx', 'tp')
- gain: bfloat16 [4, 8192], P('section', 'tp'), may hold values from 0.5 to 1.5
- queries: bfloat16 [4, 512, 32, 128], P('section', 'ctx', 'tp')
- key_value_weight: bfloat16 [4, 8192, 4, 2, 128], P('section', 'ctx', 'tp')
- adapt_down: bfloat16 [4, 16, 4096], P('section', None, 'tp'), may hold values from -1 to 1
- adapt_up: bfloat16 [4, 16, 8192], P('section', None, 'tp'), may hold values from -0.75 to 0.75
- out_grad: bfloat16 [4, 512, 8192], P('section', 'ctx', 'tp'), may hold values from -6 to 6
- doc_ids: int32 [512], P('ctx'), may hold values from 0 to 7, never falling along the last dimension, each value on 1 to 384 neighbouring positions
Outputs:
- attention_out: bfloat16 [4, 512, 4096], P('section', 'ctx', 'tp')
- adapter_out: bfloat16 [4, 512, 8192], P('section', 'ctx', 'tp')
- grad_down: float32 [4, 16, 4096], P('section', None, 'tp')
- grad_up: float32 [4, 16, 8192], P('section', None, 'tp')
The draws below stay inside these ranges and needn't reach their ends.
Inputs may be any that keep to these rules, and one draw needn't show every extreme that they name: doc_ids never falls along the sequence; a document spans at most three quarters of 512 tokens, and one spans exactly that.
All inputs are finite; a program needn't handle non-finite values.
Results may differ from the reference program's by a relative error of at most 0.022.
Values may be sent and summed in bfloat16 or wider, within the bound.
No kernel may reach another device: no remote copies, remote signals or barrier semaphores. Data moves between devices by JAX's collectives and lax.ppermute only.
A program may use at most 128 MiB of HBM per device.

```python
import math
import jax
import jax.numpy as jnp
import numpy as np
from jax import lax

MODEL_WIDTH = 8192
HEAD_SIZE = 128
GROUP = 8
R = 16
LAYER_SECTIONS = 4
SEQUENCE_TOKENS = 512
KEYVALUE_HEADS = 4
HQ = 32
QW = 4096
DOCS = 8


def spike_plan(key):
    random_seed_key = jax.random.fold_in(key, 4242)
    pair_count = max(2, SEQUENCE_TOKENS // 512)
    column = jax.random.randint(jax.random.fold_in(random_seed_key, 1), (), 0, MODEL_WIDTH)
    pair_starts = jax.random.randint(jax.random.fold_in(random_seed_key, 2), (LAYER_SECTIONS, pair_count), 0, SEQUENCE_TOKENS - 1)
    lift_size = jax.random.uniform(jax.random.fold_in(random_seed_key, 3), (LAYER_SECTIONS, pair_count), minval=2.0, maxval=3.0)
    pair_step = jax.random.uniform(jax.random.fold_in(random_seed_key, 4), (LAYER_SECTIONS, pair_count), minval=0.02, maxval=0.08)
    strength = jax.random.uniform(jax.random.fold_in(random_seed_key, 5), (LAYER_SECTIONS, pair_count), minval=2.0, maxval=4.0)
    sign_flags = jax.random.randint(jax.random.fold_in(random_seed_key, 6), (KEYVALUE_HEADS, HEAD_SIZE), 0, 2)
    half_width = HEAD_SIZE // 2
    dim_index = jnp.arange(HEAD_SIZE)
    planted = dim_index % half_width >= half_width - 4
    sign_table = jnp.where(planted[None, :], 2.0 * sign_flags.astype(jnp.float32) - 1.0, 0.0)
    row_index = jnp.arange(SEQUENCE_TOKENS)
    first_rows = row_index[None, None, :] == pair_starts[:, :, None]
    second_rows = row_index[None, None, :] == pair_starts[:, :, None] + 1
    either_rows = first_rows | second_rows
    lifted = jnp.max(jnp.where(first_rows, lift_size[:, :, None], jnp.where(second_rows, (lift_size * (1.0 + pair_step))[:, :, None], 0.0)), axis=1)
    marked = jnp.any(either_rows, axis=1)
    pushed = jnp.max(jnp.where(either_rows, strength[:, :, None], 0.0), axis=1)
    return (column, marked, lifted, pushed, planted, sign_table)


def draw_hidden(key, part):
    column, marked, lifted, pushed, planted, sign_table = spike_plan(key)
    noise_key = jax.random.fold_in(key, 11)
    noise_field = jax.random.truncated_normal(noise_key, -6.0, 6.0, (LAYER_SECTIONS, SEQUENCE_TOKENS, MODEL_WIDTH))
    spike_hit = (jnp.arange(MODEL_WIDTH) == column)[None, None, :] & marked[:, :, None]
    spike_value = lifted * MODEL_WIDTH ** 0.5
    return jnp.where(spike_hit, spike_value[:, :, None], noise_field).astype(jnp.bfloat16)


def draw_queries(key, part):
    column, marked, lifted, pushed, planted, sign_table = spike_plan(key)
    noise_key = jax.random.fold_in(key, 21)
    noise_field = jax.random.truncated_normal(noise_key, -6.0, 6.0, (LAYER_SECTIONS, SEQUENCE_TOKENS, HQ, HEAD_SIZE))
    head_signs = jnp.repeat(sign_table, GROUP, axis=0)
    boost = (pushed * HEAD_SIZE ** 0.5)[:, :, None, None] * head_signs[None, None, :, :]
    return (noise_field + boost).astype(jnp.bfloat16)


def draw_key_value_weight(key, part):
    column, marked, lifted, pushed, planted, sign_table = spike_plan(key)
    weight_scale = MODEL_WIDTH ** (-0.5)
    noise_key = jax.random.fold_in(key, 31)
    complete_shape = (LAYER_SECTIONS, MODEL_WIDTH, KEYVALUE_HEADS, 2, HEAD_SIZE)
    noise_field = jax.random.truncated_normal(noise_key, -4.0, 4.0, complete_shape) * weight_scale
    spike_hit = (jnp.arange(MODEL_WIDTH) == column)[None, :, None, None, None] & (jnp.arange(2) == 0)[None, None, None, :, None] & planted[None, None, None, None, :]
    planted_value = 16.0 * weight_scale * sign_table[None, None, :, None, :]
    return jnp.where(spike_hit, planted_value, noise_field).astype(jnp.bfloat16)


def levels(own_key, dims, split, least, high):
    factor_of = 1.0
    for position, parts in split:
        steps = jax.random.uniform(jax.random.fold_in(jax.random.fold_in(own_key, 6), position), (parts,), jnp.float32, least / len(split), high / len(split))
        factor_of = factor_of * jnp.repeat(jnp.exp(steps), dims[position] // parts).reshape((-1,) + (1,) * (len(dims) - 1 - position))
    return factor_of


def length_profile(count, total, most, skew):
    loads = [(1 << 20) // math.isqrt(standing ** skew) + 1 for standing in range(2, count + 1)]
    surplus, counts = total - most - (count - 1), [1] * (count - 1)
    while surplus > 0:
        free = [i for i in range(count - 1) if counts[i] < most]
        pool, budget = sum([loads[i] for i in free]), surplus
        for i in free:
            extra = min(most - counts[i], max(1, budget * loads[i] // pool), surplus)
            counts[i] = counts[i] + extra
            surplus = surplus - extra
    return np.array([most] + counts)


def uneven(rng, number_of, total, reach, slope):
    if number_of == 2:
        one = jax.random.randint(rng, (), max(1, total - reach), min(reach, total - 1) + 1)
        return jnp.stack([one, total - one])
    tallies = jnp.asarray(length_profile(number_of, total, reach, slope), jnp.int32)
    couples = (number_of - 1) // 2
    giver, taker = tallies[1:1 + 2 * couples:2], tallies[2:2 + 2 * couples:2]
    slack = jnp.minimum(giver - 1, reach - taker)
    shifted = jax.random.randint(jax.random.fold_in(rng, 1), (couples,), 0, 1 << 20) % (slack + 1)
    tallies = tallies.at[1:1 + 2 * couples:2].set(giver - shifted).at[2:2 + 2 * couples:2].set(taker + shifted)
    return tallies[jax.random.permutation(jax.random.fold_in(rng, 2), number_of)]


def normal_values(stream_key, shape, spread, most, shards=(), kind=jnp.bfloat16):
    loudness = levels(stream_key, shape, shards, -0.22, 0.18) if shards else 1.0
    drawn = jax.random.normal(stream_key, shape, jnp.float32) * spread * loudness
    return jnp.minimum(jnp.maximum(drawn, -most), most).astype(kind)


def setup_inputs(seed: int = 0) -> dict:
    arg_keys = jax.random.split(jax.random.key(seed), 9)
    return {
        "hidden": draw_hidden(jax.random.fold_in(arg_keys[8], 71), 0),
        "gain": jnp.clip(1.0 + 0.1 * jax.random.normal(arg_keys[1], (LAYER_SECTIONS, MODEL_WIDTH), jnp.float32), 0.5, 1.5).astype(jnp.bfloat16),
        "queries": draw_queries(jax.random.fold_in(arg_keys[8], 71), 0),
        "key_value_weight": draw_key_value_weight(jax.random.fold_in(arg_keys[8], 71), 0),
        "adapt_down": normal_values(arg_keys[4], (LAYER_SECTIONS, R, QW), (2 * R) ** -0.5, 1.0, ((0, 4), (2, 2))),
        "adapt_up": normal_values(arg_keys[5], (LAYER_SECTIONS, R, MODEL_WIDTH), (4 * R) ** -0.5, 0.75, ((0, 4), (2, 2))),
        "out_grad": normal_values(arg_keys[6], (LAYER_SECTIONS, SEQUENCE_TOKENS, MODEL_WIDTH), 1.0, 6.0, ((0, 4), (1, 4), (2, 2))),
        "doc_ids": jnp.searchsorted(jnp.cumsum(uneven(arg_keys[7], DOCS, SEQUENCE_TOKENS, (3 * SEQUENCE_TOKENS) // 4, 1)), jnp.arange(SEQUENCE_TOKENS), side="right").astype(jnp.int32),
    }


def rotate(head_values, positions):
    half_width = head_values.shape[-1] // 2
    freqs = 1000000.0 ** (-jnp.arange(half_width, dtype=jnp.float32) * 2.0 / head_values.shape[-1])
    angles = positions.astype(jnp.float32)[:, None] * freqs[None, :]
    cosine = jnp.cos(angles)[:, None, :]
    sine_table = jnp.sin(angles)[:, None, :]
    first_half = head_values[..., :half_width]
    second_half = head_values[..., half_width:]
    return jnp.concatenate([first_half * cosine - second_half * sine_table, second_half * cosine + first_half * sine_table], axis=-1)

def one_section(hidden, gain, queries, key_value_weight, adapt_down, adapt_up, out_grad, doc_ids):
    widened = hidden.astype(jnp.float32)
    normalized_rows = (widened * lax.rsqrt(lax.optimization_barrier(jnp.mean(widened * widened, axis=1, keepdims=True)) + 1e-06) * gain.astype(jnp.float32)).astype(jnp.bfloat16)
    positions = jnp.arange(SEQUENCE_TOKENS, dtype=jnp.int32)
    rotated_query = rotate(queries.astype(jnp.float32), positions).astype(jnp.bfloat16)
    key_value_rows = jnp.dot(normalized_rows, key_value_weight.reshape(MODEL_WIDTH, KEYVALUE_HEADS * 2 * HEAD_SIZE), preferred_element_type=jnp.float32).reshape(SEQUENCE_TOKENS, KEYVALUE_HEADS, 2, HEAD_SIZE)
    rotated_keys = rotate(key_value_rows[:, :, 0], positions).astype(jnp.bfloat16)
    value_rows = key_value_rows[:, :, 1].astype(jnp.bfloat16)
    allowed = (positions[None, :] <= positions[:, None]) & (doc_ids[None, :] == doc_ids[:, None])
    query_heads = rotated_query.transpose(1, 0, 2)
    key_heads = jnp.repeat(rotated_keys.transpose(1, 0, 2), GROUP, axis=0)
    value_heads = jnp.repeat(value_rows.transpose(1, 0, 2), GROUP, axis=0)

    def attend_head(items):
        head_query, head_keys, head_values = items
        scores = jnp.dot(head_query, head_keys.T, preferred_element_type=jnp.float32) * HEAD_SIZE ** (-0.5)
        scores = jnp.where(allowed, scores, -1e+30)
        row_top = lax.optimization_barrier(jnp.max(scores, axis=1, keepdims=True))
        weights = jnp.where(allowed, jnp.exp(scores - row_top), 0.0)
        weight_sum = lax.optimization_barrier(jnp.sum(weights, axis=1, keepdims=True))
        return jnp.dot(weights.astype(jnp.bfloat16), head_values, preferred_element_type=jnp.float32) / weight_sum
    heads_out = lax.map(attend_head, (query_heads, key_heads, value_heads))
    attended = heads_out.transpose(1, 0, 2).reshape(SEQUENCE_TOKENS, QW).astype(jnp.bfloat16)
    low_rows = jnp.dot(attended, adapt_down.T, preferred_element_type=jnp.float32).astype(jnp.bfloat16)
    adapter_rows = jnp.dot(low_rows, adapt_up, preferred_element_type=jnp.float32).astype(jnp.bfloat16)
    back_rows = jnp.dot(out_grad, adapt_up.T, preferred_element_type=jnp.float32).astype(jnp.bfloat16)
    up_raw = jnp.dot(low_rows.T, out_grad, preferred_element_type=jnp.float32)
    down_raw = jnp.dot(back_rows.T, attended, preferred_element_type=jnp.float32)
    return (attended, adapter_rows, down_raw, up_raw)

def reference(hidden, gain, queries, key_value_weight, adapt_down, adapt_up, out_grad, doc_ids):
    attended_all = []
    adapter_all = []
    downs = []
    uppers = []
    for section_index in range(LAYER_SECTIONS):
        attended, adapter_rows, down_raw, up_raw = one_section(hidden[section_index], gain[section_index], queries[section_index], key_value_weight[section_index], adapt_down[section_index], adapt_up[section_index], out_grad[section_index], doc_ids)
        attended_all.append(attended)
        adapter_all.append(adapter_rows)
        downs.append(down_raw)
        uppers.append(up_raw)
    down_all = jnp.stack(downs)
    up_all = jnp.stack(uppers)
    squares = jnp.sum(down_all * down_all) + jnp.sum(up_all * up_all)
    ceiling = 0.5 * math.sqrt(LAYER_SECTIONS * R * (QW + MODEL_WIDTH))
    factor = jnp.minimum(1.0, ceiling / (jnp.sqrt(squares) + 1e-06))
    return (jnp.stack(attended_all), jnp.stack(adapter_all), down_all * factor, up_all * factor)
```

```python
import math

import jax
import jax.numpy as jnp
from jax import lax
from jax.sharding import PartitionSpec as P


def rotate(head_values, positions):
    half_width = head_values.shape[-1] // 2
    freqs = 1000000.0 ** (-jnp.arange(half_width, dtype=jnp.float32) * 2.0 / head_values.shape[-1])
    angles = positions.astype(jnp.float32)[:, None] * freqs[None, :]
    cosine = jnp.cos(angles)[:, None, :]
    sine_table = jnp.sin(angles)[:, None, :]
    first_half = head_values[..., :half_width]
    second_half = head_values[..., half_width:]
    return jnp.concatenate(
        [
            first_half * cosine - second_half * sine_table,
            second_half * cosine + first_half * sine_table,
        ],
        axis=-1,
    )


def gathered_weights(hidden, gain, queries, key_value_weight, adapt_down, adapt_up, out_grad, doc_ids):
    tp_count = lax.axis_size("tp")
    row_count = hidden.shape[1]
    local_width = hidden.shape[2]
    head_dim = key_value_weight.shape[-1]
    kv_count = key_value_weight.shape[2]
    head_count = queries.shape[2]
    group_size = head_count // kv_count
    local_query = head_count * head_dim
    rank_size = adapt_down.shape[1]
    key_block = 1024
    full_rows, full_gain = (
        lax.all_gather(hidden, "tp", axis=2, tiled=True),
        lax.all_gather(gain, "tp", axis=1, tiled=True),
    )
    widened = full_rows[0].astype(jnp.float32)
    normalized_rows = (
        widened
        * lax.rsqrt(jnp.mean(widened * widened, axis=1, keepdims=True) + 1e-06)
        * full_gain[0].astype(jnp.float32)
    ).astype(jnp.bfloat16)
    kv_local = key_value_weight.reshape(1, key_value_weight.shape[1], kv_count * 2 * head_dim)
    keyval_raw = jnp.dot(
        normalized_rows,
        lax.all_gather(kv_local, "ctx", axis=1, tiled=True)[0],
        preferred_element_type=jnp.float32,
    )
    positions = lax.axis_index("ctx") * row_count + jnp.arange(row_count, dtype=jnp.int32)
    key_value_rows = keyval_raw.reshape(row_count, kv_count, 2, head_dim)
    rotated_keys = rotate(key_value_rows[:, :, 0], positions).astype(jnp.bfloat16)
    value_rows = key_value_rows[:, :, 1].astype(jnp.bfloat16)
    rotated_query = rotate(queries[0].astype(jnp.float32), positions).astype(jnp.bfloat16)
    stacked = (
        rotated_query.reshape(row_count, kv_count, group_size, head_dim)
        .transpose(1, 2, 0, 3)
        .reshape(kv_count, group_size * row_count, head_dim)
    )
    query_pos = jnp.tile(positions, group_size)
    query_doc = jnp.tile(doc_ids, group_size).astype(jnp.float32)
    score_scale = head_dim ** (-0.5)
    start_state = (
        jnp.full((kv_count, group_size * row_count), -1e30, jnp.float32),
        jnp.zeros((kv_count, group_size * row_count), jnp.float32),
        jnp.zeros((kv_count, group_size * row_count, head_dim), jnp.float32),
    )
    carried = start_state
    first_row = jnp.int32(0)
    piece_keys = lax.all_gather(rotated_keys, "ctx", axis=0, tiled=True)
    piece_values = lax.all_gather(value_rows, "ctx", axis=0, tiled=True)
    piece_docs = lax.all_gather(doc_ids.astype(jnp.bfloat16), "ctx", axis=0, tiled=True)
    key_total = piece_keys.shape[0]
    for block_start in range(0, key_total, key_block):
        block_stop = min(key_total, block_start + key_block)
        block_keys = piece_keys[block_start:block_stop]
        block_values = piece_values[block_start:block_stop]
        key_pos = first_row + block_start + jnp.arange(block_keys.shape[0], dtype=jnp.int32)
        key_doc = piece_docs[block_start:block_stop].astype(jnp.float32)
        running_top, running_sum, running_acc = carried
        scores = (
            jnp.einsum("gqd,kgd->gqk", stacked, block_keys, preferred_element_type=jnp.float32)
            * score_scale
        )
        allowed = (
            (key_pos[None, :] <= query_pos[:, None]) & (key_doc[None, :] == query_doc[:, None])
        )[None]
        scores = jnp.where(allowed, scores, -1e30)
        new_top = jnp.maximum(running_top, jnp.max(scores, axis=2))
        weights = jnp.where(allowed, jnp.exp(scores - new_top[:, :, None]), 0.0)
        shrink = jnp.exp(running_top - new_top)
        new_acc = running_acc * shrink[:, :, None] + jnp.einsum(
            "gqk,kgd->gqd",
            weights.astype(jnp.bfloat16),
            block_values,
            preferred_element_type=jnp.float32,
        )
        carried = (new_top, running_sum * shrink + jnp.sum(weights, axis=2), new_acc)
    final_top, final_sum, final_acc = carried
    attended = (
        (final_acc / final_sum[:, :, None])
        .reshape(kv_count, group_size, row_count, head_dim)
        .transpose(2, 0, 1, 3)
        .reshape(row_count, local_query)
        .astype(jnp.bfloat16)
    )
    low_part = jnp.dot(attended, adapt_down[0].T, preferred_element_type=jnp.float32)
    back_part = jnp.dot(out_grad[0], adapt_up[0].T, preferred_element_type=jnp.float32)
    low_sum, back_sum = lax.psum((low_part, back_part), "tp")
    low_rows = low_sum.astype(jnp.bfloat16)
    back_rows = back_sum.astype(jnp.bfloat16)
    adapter_rows = jnp.dot(low_rows, adapt_up[0], preferred_element_type=jnp.float32).astype(
        jnp.bfloat16
    )
    up_part = jnp.dot(low_rows.T, out_grad[0], preferred_element_type=jnp.float32)
    down_part = jnp.dot(back_rows.T, attended, preferred_element_type=jnp.float32)
    ceiling = 0.5 * math.sqrt(
        lax.axis_size("section") * rank_size * (local_query + local_width) * tp_count
    )
    up_total, down_total = (
        lax.psum(up_part.astype(jnp.bfloat16), "ctx").astype(jnp.float32),
        lax.psum(down_part.astype(jnp.bfloat16), "ctx").astype(jnp.float32),
    )
    local_squares = jnp.sum(up_total * up_total) + jnp.sum(down_total * down_total)
    squares = lax.psum(local_squares, ("section", "tp"))
    factor = jnp.minimum(1.0, ceiling / (jnp.sqrt(squares) + 1e-06))
    grad_up = up_total * factor
    grad_down = down_total * factor
    return (attended[None], adapter_rows[None], grad_down[None], grad_up[None])


def swap(value, axis, distance):
    count = lax.axis_size(axis)
    return lax.ppermute(value, axis, [(i, i ^ distance) for i in range(count)])


def send(value, axis, pairs):
    return lax.ppermute(value, axis, pairs)


def split_model_width(
    hidden, gain, queries, key_value_weight, adapt_down, adapt_up, out_grad, doc_ids
):
    f32, bf16 = jnp.float32, jnp.bfloat16
    place = lax.axis_index("ctx")
    core = lax.axis_index("tp")
    row_count = hidden.shape[1]
    local_width = hidden.shape[2]
    slice_width = key_value_weight.shape[1]
    kv_count, head_dim = key_value_weight.shape[2], key_value_weight.shape[-1]
    head_count = queries.shape[2]
    group_size = head_count // kv_count
    local_query = head_count * head_dim
    rank_size = adapt_down.shape[1]
    kv_width = kv_count * 2 * head_dim

    widened = hidden[0].astype(f32)
    part_square = jnp.sum(widened * widened, axis=1)
    mean_square = (part_square + swap(part_square, "tp", 1)) / (2 * local_width)
    normed = (
        widened * lax.rsqrt(mean_square + 1e-06)[:, None] * gain[0].astype(f32)
    ).astype(bf16)

    home = place // 2 == core
    parity = place % 2
    even_half = lax.dynamic_slice_in_dim(normed, parity * slice_width, slice_width, 1)
    odd_half = lax.dynamic_slice_in_dim(normed, (1 - parity) * slice_width, slice_width, 1)

    def device(chip, which):
        return chip * 2 + which

    axes = ("ctx", "tp")
    pairs_1 = [(device(a, a // 2), device(a ^ 1, 1 - a // 2)) for a in range(4)]
    pairs_3 = [(device(a, 1 - a // 2), device(a ^ 3, a // 2)) for a in range(4)]
    pairs_2 = [(device(a, 1 - a // 2), device(a ^ 2, 1 - a // 2)) for a in range(4)]
    home_to_away = [(device(a, a // 2), device(a, 1 - a // 2)) for a in range(4)]
    away_to_home = [(j, i) for i, j in home_to_away]
    got_1 = send(odd_half, axes, pairs_1)
    got_3 = send(odd_half, axes, pairs_3)
    got_2 = send(even_half, axes, pairs_2)
    weight = key_value_weight[0].reshape(slice_width, kv_width)
    near = jnp.where(home, even_half, got_1)
    near_other = swap(near, "tp", 1)
    far_3 = send(got_3, axes, away_to_home)
    far_2 = send(got_2, axes, home_to_away)

    def project(rows):
        return jnp.dot(rows, weight, preferred_element_type=f32)

    near_mine, near_theirs = project(near), project(near_other)
    part_0 = jnp.where(home, near_mine, near_theirs)
    part_1 = jnp.where(home, near_theirs, near_mine)
    part_3 = project(jnp.where(home, far_3, got_3))
    part_2 = project(jnp.where(home, got_2, far_2))

    def pack(value):
        heads = value.reshape(row_count, kv_count, 2, head_dim)
        keys, values = heads[:, :, 0], heads[:, :, 1]
        high = lax.reduce_precision(keys, 8, 7)
        pieces = (high.astype(bf16), (keys - high).astype(bf16), values.astype(bf16))
        return jnp.concatenate([p.reshape(row_count, -1) for p in pieces], axis=1)

    def unpack(sent):
        high, low, values = [
            p.astype(f32).reshape(row_count, kv_count, head_dim) for p in jnp.split(sent, 3, axis=1)
        ]
        return jnp.stack([high + low, values], axis=2).reshape(row_count, kv_width)

    def finish(value, d):
        heads = value.reshape(row_count, kv_count, 2, head_dim)
        where = (place ^ d) * row_count + jnp.arange(row_count, dtype=jnp.int32)
        return jnp.concatenate(
            [rotate(heads[:, :, 0], where).astype(bf16), heads[:, :, 1].astype(bf16)], axis=1
        ).reshape(row_count, kv_width)

    own_side = part_0 + unpack(swap(pack(part_1), "ctx", 1))
    own_sent = pack(own_side)
    side_next = unpack(send(own_sent, "ctx", [(0, 1), (2, 3)]))
    early_far = unpack(send(own_sent, "ctx", [(0, 2), (1, 3)]))
    far_side = part_2 + unpack(swap(pack(part_3), "ctx", 1))
    far_sent = pack(far_side)
    block_2 = finish(far_side + early_far, 2)
    block_3 = send(block_2, "ctx", [(2, 3), (3, 2)])
    block_0 = finish(own_side + unpack(swap(far_sent, "ctx", 2)), 0)
    block_1 = finish(side_next + unpack(send(far_sent, "ctx", [(0, 3), (2, 1)])), 1)

    positions = place * row_count + jnp.arange(row_count, dtype=jnp.int32)
    rotated_query = rotate(queries[0].astype(f32), positions).astype(bf16)
    stacked = (
        rotated_query.reshape(row_count, kv_count, group_size, head_dim)
        .transpose(1, 2, 0, 3)
        .reshape(kv_count, group_size * row_count, head_dim)
    )
    docs = doc_ids.astype(bf16)
    doc_blocks = [docs] + [swap(docs, "ctx", d) for d in (1, 2, 3)]
    block_positions = [
        (place ^ d) * row_count + jnp.arange(row_count, dtype=jnp.int32) for d in range(4)
    ]
    blocks = [
        value.reshape(row_count, 2, kv_count, head_dim)
        for value in (block_0, block_1, block_2, block_3)
    ]
    order = (2, 3, 0, 1)
    keys = jnp.concatenate([blocks[d][:, 0] for d in order], axis=0)
    values = jnp.concatenate([blocks[d][:, 1] for d in order], axis=0)
    key_pos = jnp.concatenate([block_positions[d] for d in order])
    key_doc = jnp.concatenate([doc_blocks[d] for d in order])
    allowed = (key_pos[None, :] <= positions[:, None]) & (key_doc[None, :] == docs[:, None])
    allowed = jnp.tile(allowed, (group_size, 1))[None]
    scores = jnp.einsum("gqd,kgd->gqk", stacked, keys, preferred_element_type=f32)
    scores = jnp.where(allowed, scores * head_dim ** (-0.5), -1e30)
    top = jnp.max(scores, axis=2, keepdims=True)
    weights = jnp.where(allowed, jnp.exp(scores - top), 0.0)
    weight_sum = jnp.sum(weights, axis=2, keepdims=True)
    attended = jnp.einsum("gqk,kgd->gqd", weights.astype(bf16), values, preferred_element_type=f32)
    attended = (
        (attended / weight_sum)
        .reshape(kv_count, group_size, row_count, head_dim)
        .transpose(2, 0, 1, 3)
        .reshape(row_count, local_query)
        .astype(bf16)
    )

    back_part = jnp.dot(out_grad[0], adapt_up[0].T, preferred_element_type=f32)
    back_rows = (back_part + swap(back_part, "tp", 1)).astype(bf16)
    low_part = jnp.dot(attended, adapt_down[0].T, preferred_element_type=f32)
    low_rows = (low_part + swap(low_part, "tp", 1)).astype(bf16)
    adapter_rows = jnp.dot(low_rows, adapt_up[0], preferred_element_type=f32).astype(bf16)
    up_part = jnp.dot(low_rows.T, out_grad[0], preferred_element_type=f32)
    down_part = jnp.dot(back_rows.T, attended, preferred_element_type=f32)

    up_step, down_step = local_width // 4, local_query // 4

    def chunk(d):
        index = place ^ d
        return jnp.concatenate(
            [
                lax.dynamic_slice_in_dim(up_part, index * up_step, up_step, 1),
                lax.dynamic_slice_in_dim(down_part, index * down_step, down_step, 1),
            ],
            axis=1,
        )

    total = chunk(0)
    for d in (1, 2, 3):
        total = total + swap(chunk(d).astype(bf16), "ctx", d).astype(f32)
    sent_total = total.astype(bf16)
    others = [sent_total] + [swap(sent_total, "ctx", d) for d in (1, 2, 3)]
    squares = jnp.sum(total * total).reshape(1, 1)
    squares = squares + sum(swap(squares, "section", d) for d in (1, 2, 3))
    squares = squares + sum(swap(squares, "ctx", d) for d in (1, 2, 3))
    squares = squares + swap(squares, "tp", 1)
    ceiling = 0.5 * math.sqrt(
        lax.axis_size("section") * rank_size * (local_query + local_width) * 2
    )
    factor = jnp.minimum(1.0, ceiling / (jnp.sqrt(squares) + 1e-06))
    gathered = jnp.stack(others)
    ordered = [
        lax.dynamic_index_in_dim(gathered, place ^ j, 0, keepdims=False).astype(f32) * factor
        for j in range(4)
    ]
    grad_up = jnp.concatenate([piece[:, :up_step] for piece in ordered], axis=1)
    grad_down = jnp.concatenate([piece[:, up_step:] for piece in ordered], axis=1)
    return (attended[None], adapter_rows[None], grad_down[None], grad_up[None])


def per_device(*arrays):
    if lax.axis_size("ctx") == 4 and lax.axis_size("tp") == 2 and lax.axis_size("section") == 4:
        return split_model_width(*arrays)
    return gathered_weights(*arrays)


def solution(mesh):
    return jax.shard_map(
        per_device,
        mesh=mesh,
        in_specs=(
            P("section", "ctx", "tp"),
            P("section", "tp"),
            P("section", "ctx", "tp", None),
            P("section", "ctx", "tp", None, None),
            P("section", None, "tp"),
            P("section", None, "tp"),
            P("section", "ctx", "tp"),
            P("ctx"),
        ),
        out_specs=(
            P("section", "ctx", "tp"),
            P("section", "ctx", "tp"),
            P("section", None, "tp"),
            P("section", None, "tp"),
        ),
        check_vma=False,
    )
```

```python
import functools
import math

import jax
import jax.numpy as jnp
from jax import lax
from jax.experimental import pallas as pl
from jax.experimental.pallas import tpu as pltpu
from jax.sharding import PartitionSpec as P


def rotate(head_values, positions):
    half_width = head_values.shape[-1] // 2
    freqs = 1000000.0 ** (-jnp.arange(half_width, dtype=jnp.float32) * 2.0 / head_values.shape[-1])
    angles = positions.astype(jnp.float32)[:, None] * freqs[None, :]
    cosine = jnp.cos(angles)[:, None, :]
    sine_table = jnp.sin(angles)[:, None, :]
    first_half = head_values[..., :half_width]
    second_half = head_values[..., half_width:]
    return jnp.concatenate(
        [
            first_half * cosine - second_half * sine_table,
            second_half * cosine + first_half * sine_table,
        ],
        axis=-1,
    )


def gathered_weights(hidden, gain, queries, key_value_weight, adapt_down, adapt_up, out_grad, doc_ids):
    tp_count = lax.axis_size("tp")
    row_count = hidden.shape[1]
    local_width = hidden.shape[2]
    head_dim = key_value_weight.shape[-1]
    kv_count = key_value_weight.shape[2]
    head_count = queries.shape[2]
    group_size = head_count // kv_count
    local_query = head_count * head_dim
    rank_size = adapt_down.shape[1]
    key_block = 1024
    full_rows, full_gain = (
        lax.all_gather(hidden, "tp", axis=2, tiled=True),
        lax.all_gather(gain, "tp", axis=1, tiled=True),
    )
    widened = full_rows[0].astype(jnp.float32)
    normalized_rows = (
        widened
        * lax.rsqrt(jnp.mean(widened * widened, axis=1, keepdims=True) + 1e-06)
        * full_gain[0].astype(jnp.float32)
    ).astype(jnp.bfloat16)
    kv_local = key_value_weight.reshape(1, key_value_weight.shape[1], kv_count * 2 * head_dim)
    keyval_raw = jnp.dot(
        normalized_rows,
        lax.all_gather(kv_local, "ctx", axis=1, tiled=True)[0],
        preferred_element_type=jnp.float32,
    )
    positions = lax.axis_index("ctx") * row_count + jnp.arange(row_count, dtype=jnp.int32)
    key_value_rows = keyval_raw.reshape(row_count, kv_count, 2, head_dim)
    rotated_keys = rotate(key_value_rows[:, :, 0], positions).astype(jnp.bfloat16)
    value_rows = key_value_rows[:, :, 1].astype(jnp.bfloat16)
    rotated_query = rotate(queries[0].astype(jnp.float32), positions).astype(jnp.bfloat16)
    stacked = (
        rotated_query.reshape(row_count, kv_count, group_size, head_dim)
        .transpose(1, 2, 0, 3)
        .reshape(kv_count, group_size * row_count, head_dim)
    )
    query_pos = jnp.tile(positions, group_size)
    query_doc = jnp.tile(doc_ids, group_size).astype(jnp.float32)
    score_scale = head_dim ** (-0.5)
    start_state = (
        jnp.full((kv_count, group_size * row_count), -1e30, jnp.float32),
        jnp.zeros((kv_count, group_size * row_count), jnp.float32),
        jnp.zeros((kv_count, group_size * row_count, head_dim), jnp.float32),
    )
    carried = start_state
    first_row = jnp.int32(0)
    piece_keys = lax.all_gather(rotated_keys, "ctx", axis=0, tiled=True)
    piece_values = lax.all_gather(value_rows, "ctx", axis=0, tiled=True)
    piece_docs = lax.all_gather(doc_ids.astype(jnp.bfloat16), "ctx", axis=0, tiled=True)
    key_total = piece_keys.shape[0]
    for block_start in range(0, key_total, key_block):
        block_stop = min(key_total, block_start + key_block)
        block_keys = piece_keys[block_start:block_stop]
        block_values = piece_values[block_start:block_stop]
        key_pos = first_row + block_start + jnp.arange(block_keys.shape[0], dtype=jnp.int32)
        key_doc = piece_docs[block_start:block_stop].astype(jnp.float32)
        running_top, running_sum, running_acc = carried
        scores = (
            jnp.einsum("gqd,kgd->gqk", stacked, block_keys, preferred_element_type=jnp.float32)
            * score_scale
        )
        allowed = (
            (key_pos[None, :] <= query_pos[:, None]) & (key_doc[None, :] == query_doc[:, None])
        )[None]
        scores = jnp.where(allowed, scores, -1e30)
        new_top = jnp.maximum(running_top, jnp.max(scores, axis=2))
        weights = jnp.where(allowed, jnp.exp(scores - new_top[:, :, None]), 0.0)
        shrink = jnp.exp(running_top - new_top)
        new_acc = running_acc * shrink[:, :, None] + jnp.einsum(
            "gqk,kgd->gqd",
            weights.astype(jnp.bfloat16),
            block_values,
            preferred_element_type=jnp.float32,
        )
        carried = (new_top, running_sum * shrink + jnp.sum(weights, axis=2), new_acc)
    final_top, final_sum, final_acc = carried
    attended = (
        (final_acc / final_sum[:, :, None])
        .reshape(kv_count, group_size, row_count, head_dim)
        .transpose(2, 0, 1, 3)
        .reshape(row_count, local_query)
        .astype(jnp.bfloat16)
    )
    low_part = jnp.dot(attended, adapt_down[0].T, preferred_element_type=jnp.float32)
    back_part = jnp.dot(out_grad[0], adapt_up[0].T, preferred_element_type=jnp.float32)
    low_sum, back_sum = lax.psum((low_part, back_part), "tp")
    low_rows = low_sum.astype(jnp.bfloat16)
    back_rows = back_sum.astype(jnp.bfloat16)
    adapter_rows = jnp.dot(low_rows, adapt_up[0], preferred_element_type=jnp.float32).astype(
        jnp.bfloat16
    )
    up_part = jnp.dot(low_rows.T, out_grad[0], preferred_element_type=jnp.float32)
    down_part = jnp.dot(back_rows.T, attended, preferred_element_type=jnp.float32)
    ceiling = 0.5 * math.sqrt(
        lax.axis_size("section") * rank_size * (local_query + local_width) * tp_count
    )
    up_total, down_total = (
        lax.psum(up_part.astype(jnp.bfloat16), "ctx").astype(jnp.float32),
        lax.psum(down_part.astype(jnp.bfloat16), "ctx").astype(jnp.float32),
    )
    local_squares = jnp.sum(up_total * up_total) + jnp.sum(down_total * down_total)
    squares = lax.psum(local_squares, ("section", "tp"))
    factor = jnp.minimum(1.0, ceiling / (jnp.sqrt(squares) + 1e-06))
    grad_up = up_total * factor
    grad_down = down_total * factor
    return (attended[None], adapter_rows[None], grad_down[None], grad_up[None])


F32, BF16 = jnp.float32, jnp.bfloat16
VMEM = pl.BlockSpec(memory_space=pltpu.VMEM)
LIMIT = 48 * 1024 * 1024


def swap(value, axis, distance):
    count = lax.axis_size(axis)
    return lax.ppermute(value, axis, [(i, i ^ distance) for i in range(count)])


def call(kernel, outs, *operands, flops=0, scratch=()):
    shapes = [jax.ShapeDtypeStruct(shape, dtype) for shape, dtype in outs]
    moved = sum(math.prod(x.shape) * x.dtype.itemsize for x in (*operands, *shapes))
    return pl.pallas_call(
        kernel,
        out_shape=shapes,
        in_specs=[VMEM] * len(operands),
        out_specs=[VMEM] * len(shapes),
        scratch_shapes=scratch,
        compiler_params=pltpu.CompilerParams(vmem_limit_bytes=LIMIT),
        cost_estimate=pl.CostEstimate(flops=flops, bytes_accessed=moved, transcendentals=0),
    )(*operands)


def times(left, right):
    return lax.dot_general(left, right, (((1,), (0,)), ((), ())), preferred_element_type=F32)


def times_transposed(left, right):
    return lax.dot_general(left, right, (((1,), (1,)), ((), ())), preferred_element_type=F32)


def transposed_times(left, right):
    return lax.dot_general(left, right, (((0,), (0,)), ((), ())), preferred_element_type=F32)


def square_kernel(hidden_ref, out_ref):
    rows = hidden_ref[...].astype(F32)
    out_ref[...] = jnp.broadcast_to(jnp.sum(rows * rows, axis=1, keepdims=True), out_ref.shape)


def norm_kernel(hidden_ref, gain_ref, mine_ref, other_ref, even_ref, odd_ref):
    width = even_ref.shape[1]
    mean = (mine_ref[:, :1] + other_ref[:, :1]) / (4 * width)
    scale = lax.rsqrt(mean + 1e-06)
    parity = lax.axis_index("ctx") % 2
    for out_ref, half in ((even_ref, parity), (odd_ref, 1 - parity)):
        columns = pl.ds(pl.multiple_of(half * width, width), width)
        rows = hidden_ref[:, columns].astype(F32)
        out_ref[...] = (rows * scale * gain_ref[:, columns].astype(F32)).astype(BF16)


def at_home():
    return lax.axis_index("ctx") // 2 == lax.axis_index("tp")


def split_heads(value, head):
    count = value.shape[1] // (2 * head)
    pieces = [value[:, i * head : (i + 1) * head] for i in range(2 * count)]
    return jnp.concatenate(pieces[0::2], axis=1), jnp.concatenate(pieces[1::2], axis=1)


def pack(value, out_ref, head):
    keys, values = split_heads(value, head)
    width = keys.shape[1]
    high = keys.astype(BF16)
    out_ref[:, :width] = high
    out_ref[:, width : 2 * width] = (keys - high.astype(F32)).astype(BF16)
    out_ref[:, 2 * width :] = values.astype(BF16)


def unpack(ref):
    width = ref.shape[1] // 3
    keys = ref[:, :width].astype(F32) + ref[:, width : 2 * width].astype(F32)
    return keys, ref[:, 2 * width :].astype(F32)


def near_kernel(head, even_ref, fwd_0_ref, got_1_ref, fwd_1_ref, weight_ref, part_0_ref, sent_ref):
    home = at_home()
    rows_1 = jnp.where(home, fwd_1_ref[...], got_1_ref[...])
    pack(times(rows_1, weight_ref[...]), sent_ref, head)
    rows_0 = jnp.where(home, even_ref[...], fwd_0_ref[...])
    keys, values = split_heads(times(rows_0, weight_ref[...]), head)
    part_0_ref[...] = jnp.concatenate([keys, values], axis=1)


def side_kernel(part_0_ref, got_ref, own_ref, sent_ref):
    keys, values = unpack(got_ref)
    width = keys.shape[1]
    keys = part_0_ref[:, :width] + keys
    values = part_0_ref[:, width:] + values
    store_sum(keys, values, own_ref, sent_ref)


def store_sum(keys, values, sum_ref, sent_ref):
    width = keys.shape[1]
    sum_ref[:, :width] = keys
    sum_ref[:, width:] = values
    high = keys.astype(BF16)
    sent_ref[:, :width] = high
    sent_ref[:, width : 2 * width] = (keys - high.astype(F32)).astype(BF16)
    sent_ref[:, 2 * width :] = values.astype(BF16)


def far_3_kernel(head, got_ref, fwd_ref, weight_ref, sent_ref):
    rows = jnp.where(at_home(), fwd_ref[...], got_ref[...])
    pack(times(rows, weight_ref[...]), sent_ref, head)


def far_2_kernel(head, got_ref, fwd_ref, weight_ref, arrived_ref, sum_ref, sent_ref):
    rows = jnp.where(at_home(), got_ref[...], fwd_ref[...])
    keys, values = split_heads(times(rows, weight_ref[...]), head)
    add_keys, add_values = unpack(arrived_ref)
    store_sum(keys + add_keys, values + add_values, sum_ref, sent_ref)


def turn(value, cosine, sine):
    head = cosine.shape[1]
    pieces = []
    for i in range(value.shape[1] // head):
        piece = value[:, i * head : (i + 1) * head]
        pieces.append(piece * cosine + pltpu.roll(piece, head // 2, 1) * sine)
    return jnp.concatenate(pieces, axis=1)


def query_kernel(query_ref, cosine_ref, sine_ref, out_ref):
    out_ref[...] = turn(query_ref[...].astype(F32), cosine_ref[0], sine_ref[0]).astype(BF16)


def finish(sum_ref, arrived_ref, cosine, sine):
    keys, values = unpack(arrived_ref)
    width = keys.shape[1]
    keys = turn(sum_ref[:, :width] + keys, cosine, sine).astype(BF16)
    return keys, (sum_ref[:, width:] + values).astype(BF16)


def block_kernel(sum_ref, arrived_ref, cosine_ref, sine_ref, out_ref):
    keys, values = finish(sum_ref, arrived_ref, cosine_ref[2], sine_ref[2])
    width = keys.shape[1]
    out_ref[:, :width] = keys
    out_ref[:, width:] = values


def attention_kernel(
    head,
    query_ref,
    own_ref,
    own_far_ref,
    next_ref,
    next_far_ref,
    block_2_ref,
    block_3_ref,
    cosine_ref,
    sine_ref,
    mask_ref,
    down_ref,
    out_ref,
    low_ref,
):
    keys_0, values_0 = finish(own_ref, own_far_ref, cosine_ref[0], sine_ref[0])
    next_keys, next_values = unpack(next_ref)
    width = next_keys.shape[1]
    far_keys, far_values = unpack(next_far_ref)
    keys_1 = turn(next_keys + far_keys, cosine_ref[1], sine_ref[1]).astype(BF16)
    values_1 = (next_values + far_values).astype(BF16)
    keys = jnp.concatenate(
        [keys_0, keys_1, block_2_ref[:, :width], block_3_ref[:, :width]], axis=0
    )
    values = jnp.concatenate(
        [values_0, values_1, block_2_ref[:, width:], block_3_ref[:, width:]], axis=0
    )
    allowed = mask_ref[...] > 0
    heads = query_ref.shape[1] // head
    group = heads // (width // head)
    scale = head ** (-0.5)
    for index in range(heads):
        first = index // group * head
        columns = slice(index * head, (index + 1) * head)
        scores = times_transposed(query_ref[:, columns], keys[:, first : first + head])
        scores = jnp.where(allowed, scores * scale, -1e30)
        weights = jnp.exp(scores - jnp.max(scores, axis=1, keepdims=True))
        total = jnp.sum(weights, axis=1, keepdims=True)
        mixed = times(weights.astype(BF16), values[:, first : first + head])
        out_ref[:, columns] = (mixed / total).astype(BF16)
    low_ref[...] = times_transposed(out_ref[...], down_ref[...])


def back_kernel(grad_ref, up_ref, out_ref):
    out_ref[...] = times_transposed(grad_ref[...], up_ref[...])


def grads_kernel(
    low_ref,
    low_other_ref,
    back_ref,
    back_other_ref,
    grad_ref,
    attended_ref,
    own_ref,
    sent_1_ref,
    sent_2_ref,
    sent_3_ref,
):
    low = (low_ref[...] + low_other_ref[...]).astype(BF16)
    back = (back_ref[...] + back_other_ref[...]).astype(BF16)
    place = lax.axis_index("ctx")
    up_step, down_step = grad_ref.shape[1] // 4, attended_ref.shape[1] // 4
    for d, out in ((2, sent_2_ref), (3, sent_3_ref), (1, sent_1_ref), (0, own_ref)):
        index = place ^ d
        columns = pl.ds(pl.multiple_of(index * up_step, up_step), up_step)
        out[:, :up_step] = transposed_times(low, grad_ref[:, columns]).astype(out.dtype)
        columns = pl.ds(pl.multiple_of(index * down_step, down_step), down_step)
        out[:, up_step:] = transposed_times(back, attended_ref[:, columns]).astype(out.dtype)


def adapter_kernel(low_ref, low_other_ref, up_ref, out_ref):
    low = (low_ref[...] + low_other_ref[...]).astype(BF16)
    out_ref[...] = times(low, up_ref[...]).astype(BF16)


def total_kernel(own_ref, got_1_ref, got_2_ref, got_3_ref, out_ref, square_ref):
    total = own_ref[...]
    for ref in (got_1_ref, got_2_ref, got_3_ref):
        total = total + ref[...].astype(F32)
    out_ref[...] = total.astype(BF16)
    square_ref[...] = jnp.broadcast_to(jnp.sum(total * total).reshape(1, 1), square_ref.shape)


def clip_kernel(ceiling, square_ref, other_ref, own_ref, got_1, got_2, got_3, up_ref, down_ref):
    squares = square_ref[:1, :1] + other_ref[:1, :1]
    factor = jnp.minimum(1.0, ceiling / (jnp.sqrt(squares) + 1e-06))
    place = lax.axis_index("ctx")
    up_step, down_step = up_ref.shape[1] // 4, down_ref.shape[1] // 4
    for d, ref in enumerate((own_ref, got_1, got_2, got_3)):
        index = place ^ d
        columns = pl.ds(pl.multiple_of(index * up_step, up_step), up_step)
        up_ref[:, columns] = ref[:, :up_step].astype(F32) * factor
        columns = pl.ds(pl.multiple_of(index * down_step, down_step), down_step)
        down_ref[:, columns] = ref[:, up_step:].astype(F32) * factor


def split_model_width(
    hidden, gain, queries, key_value_weight, adapt_down, adapt_up, out_grad, doc_ids
):
    place = lax.axis_index("ctx")
    rows = hidden.shape[1]
    local_width = hidden.shape[2]
    slice_width = key_value_weight.shape[1]
    kv_count, head = key_value_weight.shape[2], key_value_weight.shape[-1]
    head_count = queries.shape[2]
    local_query = head_count * head
    rank = adapt_down.shape[1]
    kv_width = kv_count * 2 * head
    sent_width = kv_count * 3 * head

    (squares,) = call(square_kernel, [((rows, 128), F32)], hidden[0])
    even, odd = call(
        norm_kernel,
        [((rows, slice_width), BF16)] * 2,
        hidden[0],
        gain,
        squares,
        swap(squares, "tp", 1),
    )

    def device(chip, which):
        return chip * 2 + which

    axes = ("ctx", "tp")
    pairs_1 = [(device(a, a // 2), device(a ^ 1, 1 - a // 2)) for a in range(4)]
    pairs_3 = [(device(a, 1 - a // 2), device(a ^ 3, a // 2)) for a in range(4)]
    pairs_2 = [(device(a, 1 - a // 2), device(a ^ 2, 1 - a // 2)) for a in range(4)]
    home_to_away = [(device(a, a // 2), device(a, 1 - a // 2)) for a in range(4)]
    away_to_home = [(j, i) for i, j in home_to_away]
    got_1 = lax.ppermute(odd, axes, pairs_1)
    got_3 = lax.ppermute(odd, axes, pairs_3)
    got_2 = lax.ppermute(even, axes, pairs_2)
    fwd_0 = lax.ppermute(even, axes, home_to_away)

    key_value_weight, queries, out_grad, doc_ids, even, odd = lax.optimization_barrier(
        (key_value_weight, queries, out_grad, doc_ids, even, odd)
    )
    weight = key_value_weight[0].reshape(slice_width, kv_width)
    freqs = 1000000.0 ** (-jnp.arange(head // 2, dtype=F32) * 2.0 / head)
    positions = jnp.stack(
        [(place ^ d) * rows + jnp.arange(rows, dtype=jnp.int32) for d in range(4)]
    )
    angles = positions.astype(F32)[:, :, None] * freqs
    cosine, sine = jnp.cos(angles), jnp.sin(angles)
    cosine = jnp.concatenate([cosine, cosine], axis=2)
    sine = jnp.concatenate([-sine, sine], axis=2)
    (query,) = call(
        query_kernel,
        [((rows, local_query), BF16)],
        queries[0].reshape(rows, local_query),
        cosine,
        sine,
    )
    (back_part,) = call(
        back_kernel,
        [((rows, rank), F32)],
        out_grad[0],
        adapt_up[0],
        flops=2 * rows * local_width * rank,
    )
    back_other = swap(back_part, "tp", 1)
    docs = doc_ids.astype(F32).reshape(1, rows)
    key_docs = jnp.stack([docs] + [swap(docs, "ctx", d) for d in (1, 2, 3)])
    allowed = (positions[:, None, :] <= positions[0][None, :, None]) & (
        key_docs == doc_ids.astype(F32)[None, :, None]
    )
    mask = allowed.astype(F32).transpose(1, 0, 2).reshape(rows, 4 * rows)

    fwd_1 = lax.ppermute(got_1, axes, away_to_home)
    part_flops = 2 * rows * slice_width * kv_width
    packed = ((rows, sent_width), BF16)
    summed = ((rows, kv_width), F32)
    part_0, sent_1 = call(
        functools.partial(near_kernel, head),
        [summed, packed],
        even,
        fwd_0,
        got_1,
        fwd_1,
        weight,
        flops=2 * part_flops,
    )
    own_side, own_sent = call(side_kernel, [summed, packed], part_0, swap(sent_1, "ctx", 1))
    side_next = lax.ppermute(own_sent, "ctx", [(0, 1), (2, 3)])
    early_far = lax.ppermute(own_sent, "ctx", [(0, 2), (1, 3)])
    fwd_3 = lax.ppermute(got_3, axes, away_to_home)
    (sent_3,) = call(
        functools.partial(far_3_kernel, head), [packed], got_3, fwd_3, weight, flops=part_flops
    )
    arrived_3 = swap(sent_3, "ctx", 1)
    fwd_2 = lax.ppermute(got_2, axes, home_to_away)
    far_side, far_sent = call(
        functools.partial(far_2_kernel, head),
        [summed, packed],
        got_2,
        fwd_2,
        weight,
        arrived_3,
        flops=part_flops,
    )
    own_far = swap(far_sent, "ctx", 2)
    next_far = lax.ppermute(far_sent, "ctx", [(0, 3), (2, 1)])
    (block_2,) = call(
        block_kernel, [((rows, kv_width), BF16)], far_side, early_far, cosine, sine
    )
    block_3 = lax.ppermute(block_2, "ctx", [(2, 3), (3, 2)])

    attended, low_part = call(
        functools.partial(attention_kernel, head),
        [((rows, local_query), BF16), ((rows, rank), F32)],
        query,
        own_side,
        own_far,
        side_next,
        next_far,
        block_2,
        block_3,
        cosine,
        sine,
        mask,
        adapt_down[0],
        flops=16 * rows * rows * local_query,
    )
    low_other = swap(low_part, "tp", 1)
    up_step, down_step = local_width // 4, local_query // 4
    piece = (rank, up_step + down_step)
    own, sent_1, sent_2, sent_3 = call(
        grads_kernel,
        [(piece, F32), (piece, BF16), (piece, BF16), (piece, BF16)],
        low_part,
        low_other,
        back_part,
        back_other,
        out_grad[0],
        attended,
        flops=2 * rows * rank * (local_width + local_query),
    )
    (adapter_rows,) = call(
        adapter_kernel,
        [((rows, local_width), BF16)],
        low_part,
        low_other,
        adapt_up[0],
        flops=2 * rows * rank * local_width,
    )
    total, squares = call(
        total_kernel,
        [(piece, BF16), ((8, 128), F32)],
        own,
        *(swap(sent, "ctx", d) for d, sent in ((1, sent_1), (2, sent_2), (3, sent_3))),
    )
    totals = [total] + [swap(total, "ctx", d) for d in (1, 2, 3)]
    squares = squares + sum(swap(squares, "section", d) for d in (1, 2, 3))
    squares = squares + sum(swap(squares, "ctx", d) for d in (1, 2, 3))
    ceiling = 0.5 * math.sqrt(lax.axis_size("section") * rank * (local_query + local_width) * 2)
    grad_up, grad_down = call(
        functools.partial(clip_kernel, ceiling),
        [((rank, local_width), F32), ((rank, local_query), F32)],
        squares,
        swap(squares, "tp", 1),
        *totals,
    )
    return (attended[None], adapter_rows[None], grad_down[None], grad_up[None])


def per_device(*arrays):
    if lax.axis_size("ctx") == 4 and lax.axis_size("tp") == 2 and lax.axis_size("section") == 4:
        return split_model_width(*arrays)
    return gathered_weights(*arrays)


def solution(mesh):
    return jax.shard_map(
        per_device,
        mesh=mesh,
        in_specs=(
            P("section", "ctx", "tp"),
            P("section", "tp"),
            P("section", "ctx", "tp", None),
            P("section", "ctx", "tp", None, None),
            P("section", None, "tp"),
            P("section", None, "tp"),
            P("section", "ctx", "tp"),
            P("ctx"),
        ),
        out_specs=(
            P("section", "ctx", "tp"),
            P("section", "ctx", "tp"),
            P("section", None, "tp"),
            P("section", None, "tp"),
        ),
        check_vma=False,
    )
```

```python
import functools
import math

import jax
import jax.numpy as jnp
from jax import lax
from jax.experimental import pallas as pl
from jax.experimental.pallas import tpu as pltpu
from jax.sharding import PartitionSpec as P


def rotate(head_values, positions):
    half_width = head_values.shape[-1] // 2
    freqs = 1000000.0 ** (-jnp.arange(half_width, dtype=jnp.float32) * 2.0 / head_values.shape[-1])
    angles = positions.astype(jnp.float32)[:, None] * freqs[None, :]
    cosine = jnp.cos(angles)[:, None, :]
    sine_table = jnp.sin(angles)[:, None, :]
    first_half = head_values[..., :half_width]
    second_half = head_values[..., half_width:]
    return jnp.concatenate(
        [
            first_half * cosine - second_half * sine_table,
            second_half * cosine + first_half * sine_table,
        ],
        axis=-1,
    )


def gathered_weights(hidden, gain, queries, key_value_weight, adapt_down, adapt_up, out_grad, doc_ids):
    tp_count = lax.axis_size("tp")
    row_count = hidden.shape[1]
    local_width = hidden.shape[2]
    head_dim = key_value_weight.shape[-1]
    kv_count = key_value_weight.shape[2]
    head_count = queries.shape[2]
    group_size = head_count // kv_count
    local_query = head_count * head_dim
    rank_size = adapt_down.shape[1]
    key_block = 1024
    full_rows, full_gain = (
        lax.all_gather(hidden, "tp", axis=2, tiled=True),
        lax.all_gather(gain, "tp", axis=1, tiled=True),
    )
    widened = full_rows[0].astype(jnp.float32)
    normalized_rows = (
        widened
        * lax.rsqrt(jnp.mean(widened * widened, axis=1, keepdims=True) + 1e-06)
        * full_gain[0].astype(jnp.float32)
    ).astype(jnp.bfloat16)
    kv_local = key_value_weight.reshape(1, key_value_weight.shape[1], kv_count * 2 * head_dim)
    keyval_raw = jnp.dot(
        normalized_rows,
        lax.all_gather(kv_local, "ctx", axis=1, tiled=True)[0],
        preferred_element_type=jnp.float32,
    )
    positions = lax.axis_index("ctx") * row_count + jnp.arange(row_count, dtype=jnp.int32)
    key_value_rows = keyval_raw.reshape(row_count, kv_count, 2, head_dim)
    rotated_keys = rotate(key_value_rows[:, :, 0], positions).astype(jnp.bfloat16)
    value_rows = key_value_rows[:, :, 1].astype(jnp.bfloat16)
    rotated_query = rotate(queries[0].astype(jnp.float32), positions).astype(jnp.bfloat16)
    stacked = (
        rotated_query.reshape(row_count, kv_count, group_size, head_dim)
        .transpose(1, 2, 0, 3)
        .reshape(kv_count, group_size * row_count, head_dim)
    )
    query_pos = jnp.tile(positions, group_size)
    query_doc = jnp.tile(doc_ids, group_size).astype(jnp.float32)
    score_scale = head_dim ** (-0.5)
    start_state = (
        jnp.full((kv_count, group_size * row_count), -1e30, jnp.float32),
        jnp.zeros((kv_count, group_size * row_count), jnp.float32),
        jnp.zeros((kv_count, group_size * row_count, head_dim), jnp.float32),
    )
    carried = start_state
    first_row = jnp.int32(0)
    piece_keys = lax.all_gather(rotated_keys, "ctx", axis=0, tiled=True)
    piece_values = lax.all_gather(value_rows, "ctx", axis=0, tiled=True)
    piece_docs = lax.all_gather(doc_ids.astype(jnp.bfloat16), "ctx", axis=0, tiled=True)
    key_total = piece_keys.shape[0]
    for block_start in range(0, key_total, key_block):
        block_stop = min(key_total, block_start + key_block)
        block_keys = piece_keys[block_start:block_stop]
        block_values = piece_values[block_start:block_stop]
        key_pos = first_row + block_start + jnp.arange(block_keys.shape[0], dtype=jnp.int32)
        key_doc = piece_docs[block_start:block_stop].astype(jnp.float32)
        running_top, running_sum, running_acc = carried
        scores = (
            jnp.einsum("gqd,kgd->gqk", stacked, block_keys, preferred_element_type=jnp.float32)
            * score_scale
        )
        allowed = (
            (key_pos[None, :] <= query_pos[:, None]) & (key_doc[None, :] == query_doc[:, None])
        )[None]
        scores = jnp.where(allowed, scores, -1e30)
        new_top = jnp.maximum(running_top, jnp.max(scores, axis=2))
        weights = jnp.where(allowed, jnp.exp(scores - new_top[:, :, None]), 0.0)
        shrink = jnp.exp(running_top - new_top)
        new_acc = running_acc * shrink[:, :, None] + jnp.einsum(
            "gqk,kgd->gqd",
            weights.astype(jnp.bfloat16),
            block_values,
            preferred_element_type=jnp.float32,
        )
        carried = (new_top, running_sum * shrink + jnp.sum(weights, axis=2), new_acc)
    final_top, final_sum, final_acc = carried
    attended = (
        (final_acc / final_sum[:, :, None])
        .reshape(kv_count, group_size, row_count, head_dim)
        .transpose(2, 0, 1, 3)
        .reshape(row_count, local_query)
        .astype(jnp.bfloat16)
    )
    low_part = jnp.dot(attended, adapt_down[0].T, preferred_element_type=jnp.float32)
    back_part = jnp.dot(out_grad[0], adapt_up[0].T, preferred_element_type=jnp.float32)
    low_sum, back_sum = lax.psum((low_part, back_part), "tp")
    low_rows = low_sum.astype(jnp.bfloat16)
    back_rows = back_sum.astype(jnp.bfloat16)
    adapter_rows = jnp.dot(low_rows, adapt_up[0], preferred_element_type=jnp.float32).astype(
        jnp.bfloat16
    )
    up_part = jnp.dot(low_rows.T, out_grad[0], preferred_element_type=jnp.float32)
    down_part = jnp.dot(back_rows.T, attended, preferred_element_type=jnp.float32)
    ceiling = 0.5 * math.sqrt(
        lax.axis_size("section") * rank_size * (local_query + local_width) * tp_count
    )
    up_total, down_total = (
        lax.psum(up_part.astype(jnp.bfloat16), "ctx").astype(jnp.float32),
        lax.psum(down_part.astype(jnp.bfloat16), "ctx").astype(jnp.float32),
    )
    local_squares = jnp.sum(up_total * up_total) + jnp.sum(down_total * down_total)
    squares = lax.psum(local_squares, ("section", "tp"))
    factor = jnp.minimum(1.0, ceiling / (jnp.sqrt(squares) + 1e-06))
    grad_up = up_total * factor
    grad_down = down_total * factor
    return (attended[None], adapter_rows[None], grad_down[None], grad_up[None])


F32, BF16 = jnp.float32, jnp.bfloat16
VMEM = pl.BlockSpec(memory_space=pltpu.VMEM)
LIMIT = 20 * 1024 * 1024


def swap(value, axis, distance):
    count = lax.axis_size(axis)
    return lax.ppermute(value, axis, [(i, i ^ distance) for i in range(count)])


def call(kernel, outs, *operands, flops=0, scratch=()):
    shapes = [jax.ShapeDtypeStruct(shape, dtype) for shape, dtype in outs]
    moved = sum(math.prod(x.shape) * x.dtype.itemsize for x in (*operands, *shapes))
    return pl.pallas_call(
        kernel,
        out_shape=shapes,
        in_specs=[VMEM] * len(operands),
        out_specs=[VMEM] * len(shapes),
        scratch_shapes=scratch,
        compiler_params=pltpu.CompilerParams(vmem_limit_bytes=LIMIT),
        cost_estimate=pl.CostEstimate(flops=flops, bytes_accessed=moved, transcendentals=0),
    )(*operands)


def times(left, right):
    return lax.dot_general(left, right, (((1,), (0,)), ((), ())), preferred_element_type=F32)


def times_transposed(left, right):
    return lax.dot_general(left, right, (((1,), (1,)), ((), ())), preferred_element_type=F32)


def transposed_times(left, right):
    return lax.dot_general(left, right, (((0,), (0,)), ((), ())), preferred_element_type=F32)


def norm_kernel(mine_ref, other_ref, gain_ref, gain_other_ref, *outs):
    width = outs[0].shape[1]
    place, core = lax.axis_index("ctx"), lax.axis_index("tp")
    mine, other = mine_ref[...].astype(F32), other_ref[...].astype(F32)
    squares = [jnp.sum(rows * rows, axis=1, keepdims=True) for rows in (mine, other)]
    scale = lax.rsqrt((squares[0] + squares[1]) / (4 * width) + 1e-06)
    for d, out_ref in enumerate(outs):
        chip = place ^ d
        columns = pl.ds(pl.multiple_of(chip % 2 * width, width), width)

        def write(rows_ref, weights_ref, out_ref=out_ref, columns=columns):
            rows = rows_ref[:, columns].astype(F32) * scale
            out_ref[...] = (rows * weights_ref[:, columns].astype(F32)).astype(BF16)

        pl.when(chip // 2 == core)(functools.partial(write, mine_ref, gain_ref))
        pl.when(chip // 2 != core)(functools.partial(write, other_ref, gain_other_ref))


def join_rows(mine_ref, other_ref, out_ref):
    count = mine_ref.shape[0]
    core = lax.axis_index("tp")
    out_ref[pl.ds(pl.multiple_of(core * count, count), count)] = mine_ref[...]
    out_ref[pl.ds(pl.multiple_of((1 - core) * count, count), count)] = other_ref[...]


def split_heads(value, head):
    count = value.shape[1] // (2 * head)
    pieces = [value[:, i * head : (i + 1) * head] for i in range(2 * count)]
    return jnp.concatenate(pieces[0::2], axis=1), jnp.concatenate(pieces[1::2], axis=1)


def pack(value, out_ref, head):
    keys, values = split_heads(value, head)
    store_packed(keys, values, out_ref)


def store_packed(keys, values, out_ref):
    rows, width = keys.shape
    high = keys.astype(BF16)
    out_ref[:rows, :width] = high
    out_ref[:rows, width : 2 * width] = (keys - high.astype(F32)).astype(BF16)
    out_ref[:rows, 2 * width :] = values.astype(BF16)


def unpack(ref, rows):
    width = ref.shape[1] // 3
    keys = ref[:rows, :width].astype(F32) + ref[:rows, width : 2 * width].astype(F32)
    return keys, ref[:rows, 2 * width :].astype(F32)


def store_docs(docs, out_ref):
    rows = docs.shape[1]
    out_ref[rows:, :rows] = jnp.broadcast_to(docs, (16, rows)).astype(BF16)


def load_docs(ref):
    return ref[-16:, : ref.shape[0] - 16].astype(F32)[:1]


def parts_kernel(
    head,
    got_1_ref,
    got_1_other_ref,
    got_3_ref,
    got_3_other_ref,
    even_ref,
    even_other_ref,
    weight_ref,
    sent_1_ref,
    sent_3_ref,
    own_ref,
    rows_ref,
):
    count = sent_1_ref.shape[0]
    pairs = ((got_1_ref, got_1_other_ref), (got_3_ref, got_3_other_ref), (even_ref, even_other_ref))
    for index, (mine_ref, other_ref) in enumerate(pairs):
        join_rows(mine_ref, other_ref, rows_ref.at[index * count : (index + 1) * count])
    product = times(rows_ref[...], weight_ref[...])
    pack(product[:count], sent_1_ref, head)
    pack(product[count : 2 * count], sent_3_ref, head)
    own_ref[...] = jnp.concatenate(split_heads(product[2 * count :], head), axis=1)


def far_kernel(head, got_ref, got_other_ref, weight_ref, sent_ref, rows_ref):
    join_rows(got_ref, got_other_ref, rows_ref)
    pack(times(rows_ref[...], weight_ref[...]), sent_ref, head)


def turn(value, cosine, sine):
    head = cosine.shape[1]
    pieces = []
    for i in range(value.shape[1] // head):
        piece = value[:, i * head : (i + 1) * head]
        pieces.append(piece * cosine + pltpu.roll(piece, head // 2, 1) * sine)
    return jnp.concatenate(pieces, axis=1)


def query_kernel(query_ref, cosine_ref, sine_ref, out_ref):
    rows, head = cosine_ref.shape
    for index in range(query_ref.shape[1] // head):
        piece = query_ref[:, index * head : (index + 1) * head].astype(F32)
        out_ref[index * rows : (index + 1) * rows] = turn(
            piece, cosine_ref[...], sine_ref[...]
        ).astype(BF16)


def finish_kernel(own_ref, got_1_ref, got_2_ref, got_3_ref, docs_ref, cosine_ref, sine_ref, out_ref):
    rows = own_ref.shape[0]
    width = own_ref.shape[1] // 2
    keys, values = own_ref[:, :width], own_ref[:, width:]
    for ref in (got_1_ref, got_2_ref, got_3_ref):
        more_keys, more_values = unpack(ref, rows)
        keys, values = keys + more_keys, values + more_values
    out_ref[:rows, :width] = turn(keys, cosine_ref[...], sine_ref[...]).astype(BF16)
    out_ref[:rows, width:] = values.astype(BF16)
    store_docs(docs_ref[...], out_ref)


def allowed_pairs(own_docs, key_docs, distance):
    rows = own_docs.shape[1]
    place = lax.axis_index("ctx")
    query_docs = jnp.broadcast_to(own_docs, (rows, rows)).T
    query_at = place * rows + lax.broadcasted_iota(jnp.int32, (rows, rows), 0)
    key_at = (place ^ distance) * rows + lax.broadcasted_iota(jnp.int32, (rows, rows), 1)
    return (key_at <= query_at) & (key_docs == query_docs)


def group_scores(query_ref, keys, allowed, head, group):
    rows = allowed.shape[0]
    groups = keys.shape[1] // head
    count = query_ref.shape[0] // groups
    scores = times_transposed(
        query_ref[group * count : (group + 1) * count], keys[:, group * head : (group + 1) * head]
    ) * head ** (-0.5)
    scores = scores.reshape(count // rows, rows, scores.shape[1])
    return jnp.where(allowed[None], scores, -1e30).reshape(count, scores.shape[2])


def first_attention_kernel(
    head, query_ref, block_0_ref, block_1_ref, block_2_ref, mixed_ref, state_ref
):
    rows = block_0_ref.shape[0] - 16
    width = block_0_ref.shape[1] // 2
    blocks = (block_0_ref, block_1_ref, block_2_ref)
    keys = jnp.concatenate([ref[:rows, :width] for ref in blocks], axis=0)
    values = jnp.concatenate([ref[:rows, width:] for ref in blocks], axis=0)
    allowed = jnp.concatenate(
        [allowed_pairs(load_docs(block_0_ref), load_docs(ref), d) for d, ref in enumerate(blocks)],
        axis=1,
    )
    groups = width // head
    count = query_ref.shape[0] // groups
    for group in range(groups):
        scores = group_scores(query_ref, keys, allowed, head, group)
        top = jnp.max(scores, axis=1, keepdims=True)
        weights = jnp.exp(scores - top)
        total = jnp.sum(weights, axis=1, keepdims=True)
        place = slice(group * count, (group + 1) * count)
        left = lax.broadcasted_iota(jnp.int32, (count, state_ref.shape[1]), 1) < 64
        state_ref[place] = jnp.where(left, top, total)
        mixed_ref[place] = times(
            weights.astype(BF16), values[:, group * head : (group + 1) * head]
        )


def last_attention_kernel(
    head,
    query_ref,
    block_0_ref,
    block_3_ref,
    mixed_ref,
    state_ref,
    down_ref,
    back_ref,
    back_other_ref,
    out_ref,
    low_ref,
    grad_ref,
):
    rows = block_3_ref.shape[0] - 16
    width = block_3_ref.shape[1] // 2
    allowed = allowed_pairs(load_docs(block_0_ref), load_docs(block_3_ref), 3)
    keys, values = block_3_ref[:rows, :width], block_3_ref[:rows, width:]
    groups = width // head
    count = query_ref.shape[0] // groups
    for group in range(groups):
        scores = group_scores(query_ref, keys, allowed, head, group)
        place = slice(group * count, (group + 1) * count)
        before = state_ref[place, :1]
        top = jnp.maximum(before, jnp.max(scores, axis=1, keepdims=True))
        weights = jnp.exp(scores - top)
        shrink = jnp.exp(before - top)
        total = state_ref[place, 64:65] * shrink + jnp.sum(weights, axis=1, keepdims=True)
        mixed = mixed_ref[place] * shrink + times(
            weights.astype(BF16), values[:, group * head : (group + 1) * head]
        )
        mixed = (mixed / total).astype(BF16)
        for index in range(count // rows):
            column = group * count // rows * head + index * head
            out_ref[:, column : column + head] = mixed[index * rows : (index + 1) * rows]
    attended = out_ref[...]
    low_ref[...] = times_transposed(attended, down_ref[...])
    back = (back_ref[...] + back_other_ref[...]).astype(BF16)
    grad_ref[...] = transposed_times(back, attended)


def back_kernel(grad_ref, up_ref, out_ref):
    out_ref[...] = times_transposed(grad_ref[...], up_ref[...])


def grads_kernel(low_ref, low_other_ref, grad_ref, down_ref, own_ref, sent_ref):
    low = (low_ref[...] + low_other_ref[...]).astype(BF16)
    parity = lax.axis_index("ctx") % 2
    up_step, down_step = grad_ref.shape[1] // 2, down_ref.shape[1] // 2
    for index, out in ((1 - parity, sent_ref), (parity, own_ref)):
        columns = pl.ds(pl.multiple_of(index * up_step, up_step), up_step)
        out[:, :up_step] = transposed_times(low, grad_ref[:, columns]).astype(out.dtype)
        columns = pl.ds(pl.multiple_of(index * down_step, down_step), down_step)
        out[:, up_step:] = down_ref[:, columns].astype(out.dtype)


def adapter_kernel(low_ref, low_other_ref, up_ref, out_ref):
    low = (low_ref[...] + low_other_ref[...]).astype(BF16)
    out_ref[...] = times(low, up_ref[...]).astype(BF16)


def add_kernel(own_ref, got_ref, out_ref):
    out_ref[...] = (own_ref[...].astype(F32) + got_ref[...].astype(F32)).astype(BF16)


def square_sum_kernel(own_ref, got_ref, out_ref):
    parity = lax.axis_index("ctx") % 2
    own, got = [jnp.sum(jnp.square(ref[...].astype(F32))).reshape(1, 1) for ref in (own_ref, got_ref)]
    total = jnp.where(parity == 0, own + got, got + own)
    out_ref[...] = jnp.broadcast_to(total, out_ref.shape)


def clip_kernel(ceiling, square_ref, other_ref, own_ref, got_ref, up_ref, down_ref):
    squares = square_ref[:1, :1] + other_ref[:1, :1]
    factor = jnp.minimum(1.0, ceiling / (jnp.sqrt(squares) + 1e-06))
    parity = lax.axis_index("ctx") % 2
    up_step, down_step = up_ref.shape[1] // 2, down_ref.shape[1] // 2
    for index, ref in ((parity, own_ref), (1 - parity, got_ref)):
        columns = pl.ds(pl.multiple_of(index * up_step, up_step), up_step)
        up_ref[:, columns] = ref[:, :up_step].astype(F32) * factor
        columns = pl.ds(pl.multiple_of(index * down_step, down_step), down_step)
        down_ref[:, columns] = ref[:, up_step:].astype(F32) * factor


def split_model_width(
    hidden, gain, queries, key_value_weight, adapt_down, adapt_up, out_grad, doc_ids
):
    place = lax.axis_index("ctx")
    rows = hidden.shape[1]
    local_width = hidden.shape[2]
    slice_width = key_value_weight.shape[1]
    kv_count, head = key_value_weight.shape[2], key_value_weight.shape[-1]
    head_count = queries.shape[2]
    local_query = head_count * head
    rank = adapt_down.shape[1]
    kv_width = kv_count * 2 * head
    sent_width = kv_count * 3 * head

    half = rows // 2
    core = lax.axis_index("tp")
    mine = lax.dynamic_slice_in_dim(hidden[0], core * half, half, 0)
    theirs = lax.dynamic_slice_in_dim(hidden[0], (1 - core) * half, half, 0)
    part = ((half, slice_width), BF16)
    slices = call(
        norm_kernel, [part] * 4, mine, swap(theirs, "tp", 1), gain, swap(gain, "tp", 1)
    )

    got_1 = swap(slices[1], "ctx", 1)
    got_3 = swap(slices[3], "ctx", 3)
    got_2 = swap(slices[2], "ctx", 2)
    part_flops = 2 * rows * slice_width * kv_width
    packed = ((rows, sent_width), BF16)
    summed = ((rows, kv_width), F32)
    final = ((rows + 16, kv_width), BF16)

    def step(function, *operands):
        shapes = jax.eval_shape(function, *operands)
        return lax.cond(
            place < 4,
            function,
            lambda *_: jax.tree.map(lambda x: jnp.zeros(x.shape, x.dtype), shapes),
            *operands,
        )

    def prepare(even, key_value_weight, queries, out_grad, adapt_up, doc_ids):
        even_other = swap(even, "tp", 1)
        weight = key_value_weight[0].reshape(slice_width, kv_width)
        docs = doc_ids.astype(F32).reshape(1, rows)
        freqs = 1000000.0 ** (-jnp.arange(head // 2, dtype=F32) * 2.0 / head)
        positions = place * rows + jnp.arange(rows, dtype=jnp.int32)
        angles = positions.astype(F32)[:, None] * freqs
        cosine, sine = jnp.cos(angles), jnp.sin(angles)
        cosine = jnp.concatenate([cosine, cosine], axis=1)
        sine = jnp.concatenate([-sine, sine], axis=1)
        (query,) = call(
            query_kernel,
            [((head_count * rows, head), BF16)],
            queries[0].reshape(rows, local_query),
            cosine,
            sine,
        )
        (back_part,) = call(
            back_kernel,
            [((rows, rank), F32)],
            out_grad[0],
            adapt_up[0],
            flops=2 * rows * local_width * rank,
        )
        back_other = swap(back_part, "tp", 1)
        return weight, docs, cosine, sine, query, back_part, back_other, even_other

    weight, docs, cosine, sine, query, back_part, back_other, even_other = step(
        prepare, slices[0], key_value_weight, queries, out_grad, adapt_up, doc_ids
    )
    got_1, got_3, even_other = lax.optimization_barrier((got_1, got_3, even_other))

    def near_parts(got_1, got_3, even, even_other, weight):
        return call(
            functools.partial(parts_kernel, head),
            [packed, packed, summed],
            got_1,
            swap(got_1, "tp", 1),
            got_3,
            swap(got_3, "tp", 1),
            even,
            even_other,
            weight,
            flops=3 * part_flops,
            scratch=[pltpu.VMEM((3 * rows, slice_width), BF16)],
        )

    sent_1, sent_3, part_0 = step(near_parts, got_1, got_3, slices[0], even_other, weight)
    arrived_1 = swap(sent_1, "ctx", 1)
    arrived_3 = swap(sent_3, "ctx", 3)
    got_2, part_0 = lax.optimization_barrier((got_2, part_0))
    (sent_2,) = call(
        functools.partial(far_kernel, head),
        [packed],
        got_2,
        swap(got_2, "tp", 1),
        weight,
        flops=part_flops,
        scratch=[pltpu.VMEM((rows, slice_width), BF16)],
    )
    arrived_2 = swap(sent_2, "ctx", 2)
    (block_0,) = call(
        finish_kernel, [final], part_0, arrived_1, arrived_2, arrived_3, docs, cosine, sine
    )
    block_1 = swap(block_0, "ctx", 1)
    block_2 = swap(block_0, "ctx", 2)
    block_3 = swap(block_0, "ctx", 3)

    state = ((head_count * rows, 128), F32)
    mixed, state = call(
        functools.partial(first_attention_kernel, head),
        [state, state],
        query,
        block_0,
        block_1,
        block_2,
        flops=12 * rows * rows * local_query,
    )
    attended, low_part, down_part = call(
        functools.partial(last_attention_kernel, head),
        [((rows, local_query), BF16), ((rows, rank), F32), ((rank, local_query), F32)],
        query,
        block_0,
        block_3,
        mixed,
        state,
        adapt_down[0],
        back_part,
        back_other,
        flops=4 * rows * rows * local_query,
    )
    low_other = swap(low_part, "tp", 1)
    piece = (rank, (local_width + local_query) // 2)
    own, sent = call(
        grads_kernel,
        [(piece, F32), (piece, BF16)],
        low_part,
        low_other,
        out_grad[0],
        down_part,
        flops=2 * rows * rank * local_width,
    )
    (adapter_rows,) = call(
        adapter_kernel,
        [((rows, local_width), BF16)],
        low_part,
        low_other,
        adapt_up[0],
        flops=2 * rows * rank * local_width,
    )
    (pair_sum,) = call(add_kernel, [(piece, BF16)], own, swap(sent, "ctx", 1))
    (total,) = call(add_kernel, [(piece, BF16)], pair_sum, swap(pair_sum, "ctx", 2))
    total_other = swap(total, "ctx", 1)
    total_other, adapter_rows = lax.optimization_barrier((total_other, adapter_rows))
    (squares,) = call(square_sum_kernel, [((8, 128), F32)], total, total_other)
    squares = squares + swap(squares, "section", 1)
    squares = squares + swap(squares, "section", 2)
    ceiling = 0.5 * math.sqrt(lax.axis_size("section") * rank * (local_query + local_width) * 2)
    grad_up, grad_down = call(
        functools.partial(clip_kernel, ceiling),
        [((rank, local_width), F32), ((rank, local_query), F32)],
        squares,
        swap(squares, "tp", 1),
        total,
        total_other,
    )
    return (attended[None], adapter_rows[None], grad_down[None], grad_up[None])


def per_device(*arrays):
    if lax.axis_size("ctx") == 4 and lax.axis_size("tp") == 2 and lax.axis_size("section") == 4:
        return split_model_width(*arrays)
    return gathered_weights(*arrays)


def solution(mesh):
    return jax.shard_map(
        per_device,
        mesh=mesh,
        in_specs=(
            P("section", "ctx", "tp"),
            P("section", "tp"),
            P("section", "ctx", "tp", None),
            P("section", "ctx", "tp", None, None),
            P("section", None, "tp"),
            P("section", None, "tp"),
            P("section", "ctx", "tp"),
            P("ctx"),
        ),
        out_specs=(
            P("section", "ctx", "tp"),
            P("section", "ctx", "tp"),
            P("section", None, "tp"),
            P("section", None, "tp"),
        ),
        check_vma=False,
    )
```

```python
import functools
import math

import jax
import jax.numpy as jnp
from jax import lax
from jax.experimental import pallas as pl
from jax.experimental.pallas import tpu as pltpu
from jax.sharding import PartitionSpec as P


def rotate(head_values, positions):
    half_width = head_values.shape[-1] // 2
    freqs = 1000000.0 ** (-jnp.arange(half_width, dtype=jnp.float32) * 2.0 / head_values.shape[-1])
    angles = positions.astype(jnp.float32)[:, None] * freqs[None, :]
    cosine = jnp.cos(angles)[:, None, :]
    sine_table = jnp.sin(angles)[:, None, :]
    first_half = head_values[..., :half_width]
    second_half = head_values[..., half_width:]
    return jnp.concatenate(
        [
            first_half * cosine - second_half * sine_table,
            second_half * cosine + first_half * sine_table,
        ],
        axis=-1,
    )


def gathered_weights(hidden, gain, queries, key_value_weight, adapt_down, adapt_up, out_grad, doc_ids):
    tp_count = lax.axis_size("tp")
    row_count = hidden.shape[1]
    local_width = hidden.shape[2]
    head_dim = key_value_weight.shape[-1]
    kv_count = key_value_weight.shape[2]
    head_count = queries.shape[2]
    group_size = head_count // kv_count
    local_query = head_count * head_dim
    rank_size = adapt_down.shape[1]
    key_block = 1024
    full_rows, full_gain = (
        lax.all_gather(hidden, "tp", axis=2, tiled=True),
        lax.all_gather(gain, "tp", axis=1, tiled=True),
    )
    widened = full_rows[0].astype(jnp.float32)
    normalized_rows = (
        widened
        * lax.rsqrt(jnp.mean(widened * widened, axis=1, keepdims=True) + 1e-06)
        * full_gain[0].astype(jnp.float32)
    ).astype(jnp.bfloat16)
    kv_local = key_value_weight.reshape(1, key_value_weight.shape[1], kv_count * 2 * head_dim)
    keyval_raw = jnp.dot(
        normalized_rows,
        lax.all_gather(kv_local, "ctx", axis=1, tiled=True)[0],
        preferred_element_type=jnp.float32,
    )
    positions = lax.axis_index("ctx") * row_count + jnp.arange(row_count, dtype=jnp.int32)
    key_value_rows = keyval_raw.reshape(row_count, kv_count, 2, head_dim)
    rotated_keys = rotate(key_value_rows[:, :, 0], positions).astype(jnp.bfloat16)
    value_rows = key_value_rows[:, :, 1].astype(jnp.bfloat16)
    rotated_query = rotate(queries[0].astype(jnp.float32), positions).astype(jnp.bfloat16)
    stacked = (
        rotated_query.reshape(row_count, kv_count, group_size, head_dim)
        .transpose(1, 2, 0, 3)
        .reshape(kv_count, group_size * row_count, head_dim)
    )
    query_pos = jnp.tile(positions, group_size)
    query_doc = jnp.tile(doc_ids, group_size).astype(jnp.float32)
    score_scale = head_dim ** (-0.5)
    start_state = (
        jnp.full((kv_count, group_size * row_count), -1e30, jnp.float32),
        jnp.zeros((kv_count, group_size * row_count), jnp.float32),
        jnp.zeros((kv_count, group_size * row_count, head_dim), jnp.float32),
    )
    carried = start_state
    first_row = jnp.int32(0)
    piece_keys = lax.all_gather(rotated_keys, "ctx", axis=0, tiled=True)
    piece_values = lax.all_gather(value_rows, "ctx", axis=0, tiled=True)
    piece_docs = lax.all_gather(doc_ids.astype(jnp.bfloat16), "ctx", axis=0, tiled=True)
    key_total = piece_keys.shape[0]
    for block_start in range(0, key_total, key_block):
        block_stop = min(key_total, block_start + key_block)
        block_keys = piece_keys[block_start:block_stop]
        block_values = piece_values[block_start:block_stop]
        key_pos = first_row + block_start + jnp.arange(block_keys.shape[0], dtype=jnp.int32)
        key_doc = piece_docs[block_start:block_stop].astype(jnp.float32)
        running_top, running_sum, running_acc = carried
        scores = (
            jnp.einsum("gqd,kgd->gqk", stacked, block_keys, preferred_element_type=jnp.float32)
            * score_scale
        )
        allowed = (
            (key_pos[None, :] <= query_pos[:, None]) & (key_doc[None, :] == query_doc[:, None])
        )[None]
        scores = jnp.where(allowed, scores, -1e30)
        new_top = jnp.maximum(running_top, jnp.max(scores, axis=2))
        weights = jnp.where(allowed, jnp.exp(scores - new_top[:, :, None]), 0.0)
        shrink = jnp.exp(running_top - new_top)
        new_acc = running_acc * shrink[:, :, None] + jnp.einsum(
            "gqk,kgd->gqd",
            weights.astype(jnp.bfloat16),
            block_values,
            preferred_element_type=jnp.float32,
        )
        carried = (new_top, running_sum * shrink + jnp.sum(weights, axis=2), new_acc)
    final_top, final_sum, final_acc = carried
    attended = (
        (final_acc / final_sum[:, :, None])
        .reshape(kv_count, group_size, row_count, head_dim)
        .transpose(2, 0, 1, 3)
        .reshape(row_count, local_query)
        .astype(jnp.bfloat16)
    )
    low_part = jnp.dot(attended, adapt_down[0].T, preferred_element_type=jnp.float32)
    back_part = jnp.dot(out_grad[0], adapt_up[0].T, preferred_element_type=jnp.float32)
    low_sum, back_sum = lax.psum((low_part, back_part), "tp")
    low_rows = low_sum.astype(jnp.bfloat16)
    back_rows = back_sum.astype(jnp.bfloat16)
    adapter_rows = jnp.dot(low_rows, adapt_up[0], preferred_element_type=jnp.float32).astype(
        jnp.bfloat16
    )
    up_part = jnp.dot(low_rows.T, out_grad[0], preferred_element_type=jnp.float32)
    down_part = jnp.dot(back_rows.T, attended, preferred_element_type=jnp.float32)
    ceiling = 0.5 * math.sqrt(
        lax.axis_size("section") * rank_size * (local_query + local_width) * tp_count
    )
    up_total, down_total = (
        lax.psum(up_part.astype(jnp.bfloat16), "ctx").astype(jnp.float32),
        lax.psum(down_part.astype(jnp.bfloat16), "ctx").astype(jnp.float32),
    )
    local_squares = jnp.sum(up_total * up_total) + jnp.sum(down_total * down_total)
    squares = lax.psum(local_squares, ("section", "tp"))
    factor = jnp.minimum(1.0, ceiling / (jnp.sqrt(squares) + 1e-06))
    grad_up = up_total * factor
    grad_down = down_total * factor
    return (attended[None], adapter_rows[None], grad_down[None], grad_up[None])


F32, BF16 = jnp.float32, jnp.bfloat16
VMEM = pl.BlockSpec(memory_space=pltpu.VMEM)
LIMIT = 16 * 1024 * 1024


def swap(value, axis, distance):
    count = lax.axis_size(axis)
    return lax.ppermute(value, axis, [(i, i ^ distance) for i in range(count)])


def call(kernel, outs, *operands, flops=0, scratch=(), loose=()):
    shapes = [jax.ShapeDtypeStruct(shape, dtype) for shape, dtype in outs]
    moved = sum(math.prod(x.shape) * x.dtype.itemsize for x in (*operands, *shapes))
    return pl.pallas_call(
        kernel,
        out_shape=shapes,
        in_specs=[pl.BlockSpec(memory_space=pl.ANY) if i in loose else VMEM for i in range(len(operands))],
        out_specs=[VMEM] * len(shapes),
        scratch_shapes=scratch,
        compiler_params=pltpu.CompilerParams(vmem_limit_bytes=LIMIT),
        cost_estimate=pl.CostEstimate(flops=flops, bytes_accessed=moved, transcendentals=0),
    )(*operands)


def times(left, right):
    return lax.dot_general(left, right, (((1,), (0,)), ((), ())), preferred_element_type=F32)


def times_transposed(left, right):
    return lax.dot_general(left, right, (((1,), (1,)), ((), ())), preferred_element_type=F32)


def transposed_times(left, right):
    return lax.dot_general(left, right, (((0,), (0,)), ((), ())), preferred_element_type=F32)


def distances():
    core = lax.axis_index("tp")
    return 0, jnp.where(core == 0, 1, 3), jnp.where(core == 0, 3, 1), 2


def norm_kernel(mine_ref, other_ref, gain_ref, gain_other_ref, *outs):
    width = outs[0].shape[1]
    place, core = lax.axis_index("ctx"), lax.axis_index("tp")
    mine, other = mine_ref[...].astype(F32), other_ref[...].astype(F32)
    squares = [jnp.sum(rows * rows, axis=1, keepdims=True) for rows in (mine, other)]
    scale = lax.rsqrt((squares[0] + squares[1]) / (4 * width) + 1e-06)
    for d, out_ref in zip(distances(), outs):
        chip = place ^ d
        columns = pl.ds(pl.multiple_of(chip % 2 * width, width), width)

        def write(rows_ref, weights_ref, out_ref=out_ref, columns=columns):
            rows = rows_ref[:, columns].astype(F32) * scale
            out_ref[...] = (rows * weights_ref[:, columns].astype(F32)).astype(BF16)

        pl.when(chip // 2 == core)(functools.partial(write, mine_ref, gain_ref))
        pl.when(chip // 2 != core)(functools.partial(write, other_ref, gain_other_ref))


def join_rows(mine_ref, other_ref, out_ref):
    count = mine_ref.shape[0]
    core = lax.axis_index("tp")
    out_ref[pl.ds(pl.multiple_of(core * count, count), count)] = mine_ref[...]
    out_ref[pl.ds(pl.multiple_of((1 - core) * count, count), count)] = other_ref[...]


def split_heads(value, head):
    count = value.shape[1] // (2 * head)
    pieces = [value[:, i * head : (i + 1) * head] for i in range(2 * count)]
    return jnp.concatenate(pieces[0::2], axis=1), jnp.concatenate(pieces[1::2], axis=1)


def pack(value, out_ref, head):
    keys, values = split_heads(value, head)
    store_packed(keys, values, out_ref)


def store_packed(keys, values, out_ref):
    rows, width = keys.shape
    high = keys.astype(BF16)
    out_ref[:rows, :width] = high
    out_ref[:rows, width : 2 * width] = (keys - high.astype(F32)).astype(BF16)
    out_ref[:rows, 2 * width :] = values.astype(BF16)


def unpack(ref, rows):
    width = ref.shape[1] // 3
    keys = ref[:rows, :width].astype(F32) + ref[:rows, width : 2 * width].astype(F32)
    return keys, ref[:rows, 2 * width :].astype(F32)


def store_docs(docs, out_ref):
    rows = docs.shape[1]
    out_ref[rows:, :rows] = jnp.broadcast_to(docs, (16, rows)).astype(BF16)


def load_docs(ref):
    return ref[-16:, : ref.shape[0] - 16].astype(F32)[:1]


def own_kernel(head, even_ref, even_other_ref, weight_ref, own_ref, weight_out_ref, rows_ref):
    weight_out_ref[...] = weight_ref[...]
    join_rows(even_ref, even_other_ref, rows_ref)
    product = times(rows_ref[...], weight_ref[...])
    own_ref[...] = jnp.concatenate(split_heads(product, head), axis=1)


def far_kernel(head, got_ref, got_other_ref, weight_ref, sent_ref, rows_ref):
    join_rows(got_ref, got_other_ref, rows_ref)
    pack(times(rows_ref[...], weight_ref[...]), sent_ref, head)


def near_kernel(
    head,
    got_a_ref,
    got_a_other_ref,
    got_b_ref,
    got_b_other_ref,
    weight_ref,
    sent_a_ref,
    sent_b_ref,
    rows_ref,
):
    count = sent_a_ref.shape[0]
    join_rows(got_a_ref, got_b_other_ref, rows_ref.at[:count])
    join_rows(got_b_ref, got_a_other_ref, rows_ref.at[count:])
    product = times(rows_ref[...], weight_ref[...])
    pack(product[:count], sent_a_ref, head)
    pack(product[count:], sent_b_ref, head)


def turn(value, cosine, sine):
    head = cosine.shape[1]
    pieces = []
    for i in range(value.shape[1] // head):
        piece = value[:, i * head : (i + 1) * head]
        pieces.append(piece * cosine + pltpu.roll(piece, head // 2, 1) * sine)
    return jnp.concatenate(pieces, axis=1)


def query_kernel(query_ref, cosine_ref, sine_ref, out_ref):
    rows, head = cosine_ref.shape
    for index in range(query_ref.shape[1] // head):
        piece = query_ref[:, index * head : (index + 1) * head].astype(F32)
        out_ref[index * rows : (index + 1) * rows] = turn(
            piece, cosine_ref[...], sine_ref[...]
        ).astype(BF16)


def accumulate_kernel(
    own_ref, got_ref, docs_ref, cosine_ref, sine_ref, out_ref, docs_out_ref, cosine_out_ref, sine_out_ref
):
    keys, values = unpack(got_ref, own_ref.shape[0])
    width = keys.shape[1]
    out_ref[:, :width] = own_ref[:, :width] + keys
    out_ref[:, width:] = own_ref[:, width:] + values
    for ref, copy_ref in (
        (docs_ref, docs_out_ref),
        (cosine_ref, cosine_out_ref),
        (sine_ref, sine_out_ref),
    ):
        copy_ref[...] = ref[...]


def finish_kernel(own_ref, got_a_ref, got_b_ref, docs_ref, cosine_ref, sine_ref, out_ref):
    rows = own_ref.shape[0]
    width = own_ref.shape[1] // 2
    keys, values = own_ref[:, :width], own_ref[:, width:]
    for ref in (got_a_ref, got_b_ref):
        more_keys, more_values = unpack(ref, rows)
        keys, values = keys + more_keys, values + more_values
    out_ref[:rows, :width] = turn(keys, cosine_ref[...], sine_ref[...]).astype(BF16)
    out_ref[:rows, width:] = values.astype(BF16)
    store_docs(docs_ref[...], out_ref)


def allowed_pairs(own_docs, key_docs, distance):
    rows = own_docs.shape[1]
    place = lax.axis_index("ctx")
    query_docs = jnp.broadcast_to(own_docs, (rows, rows)).T
    query_at = place * rows + lax.broadcasted_iota(jnp.int32, (rows, rows), 0)
    key_at = (place ^ distance) * rows + lax.broadcasted_iota(jnp.int32, (rows, rows), 1)
    return (key_at <= query_at) & (key_docs == query_docs)


def group_scores(query_ref, keys, allowed, head, group):
    rows = allowed.shape[0]
    groups = keys.shape[1] // head
    count = query_ref.shape[0] // groups
    scores = times_transposed(
        query_ref[group * count : (group + 1) * count], keys[:, group * head : (group + 1) * head]
    ).reshape(count // rows, rows, keys.shape[0])
    return jnp.where(allowed[None], scores, -1e30).reshape(count, keys.shape[0])


def attention_kernel(
    head,
    query_ref,
    block_0_ref,
    block_a_ref,
    block_b_ref,
    block_c_ref,
    down_ref,
    back_ref,
    back_other_ref,
    out_ref,
    low_ref,
    grad_ref,
):
    rows = block_0_ref.shape[0] - 16
    width = block_0_ref.shape[1] // 2
    blocks = (block_0_ref, block_a_ref, block_b_ref, block_c_ref)
    keys = jnp.concatenate([ref[:rows, :width] for ref in blocks], axis=0)
    values = jnp.concatenate([ref[:rows, width:] for ref in blocks], axis=0)
    own_docs = load_docs(block_0_ref)
    allowed = jnp.concatenate(
        [allowed_pairs(own_docs, load_docs(ref), d) for d, ref in zip(distances(), blocks)], axis=1
    )
    groups = width // head
    count = query_ref.shape[0] // groups
    scale = head ** (-0.5) * math.log2(math.e)
    ones = jnp.ones((len(blocks) * rows, head), BF16)
    for group in range(groups):
        scores = group_scores(query_ref, keys, allowed, head, group)
        weights = jnp.exp2((scores - jnp.max(scores, axis=1, keepdims=True)) * scale)
        group_values = jnp.concatenate([values[:, group * head : (group + 1) * head], ones], axis=1)
        mixed = times(weights.astype(BF16), group_values)
        mixed = (mixed[:, :head] / mixed[:, head:]).astype(BF16)
        for index in range(count // rows):
            column = group * count // rows * head + index * head
            out_ref[:, column : column + head] = mixed[index * rows : (index + 1) * rows]
    attended = out_ref[...]
    low_ref[...] = times_transposed(attended, down_ref[...])
    back = (back_ref[...] + back_other_ref[...]).astype(BF16)
    grad_ref[...] = transposed_times(back, attended)


def back_kernel(grad_ref, up_ref, out_ref):
    out_ref[...] = times_transposed(grad_ref[...], up_ref[...])


def grads_kernel(low_ref, low_other_ref, grad_ref, down_ref, own_ref, sent_ref):
    low = (low_ref[...] + low_other_ref[...]).astype(BF16)
    parity = lax.axis_index("ctx") % 2
    up_step, down_step = grad_ref.shape[1] // 2, down_ref.shape[1] // 2
    for index, out in ((1 - parity, sent_ref), (parity, own_ref)):
        columns = pl.ds(pl.multiple_of(index * up_step, up_step), up_step)
        out[:, :up_step] = transposed_times(low, grad_ref[:, columns]).astype(out.dtype)
        columns = pl.ds(pl.multiple_of(index * down_step, down_step), down_step)
        out[:, up_step:] = down_ref[:, columns].astype(out.dtype)


def adapter_kernel(low_ref, low_other_ref, up_ref, out_ref):
    low = (low_ref[...] + low_other_ref[...]).astype(BF16)
    out_ref[...] = times(low, up_ref[...]).astype(BF16)


def add_kernel(own_ref, got_ref, out_ref):
    out_ref[...] = (own_ref[...].astype(F32) + got_ref[...].astype(F32)).astype(BF16)


def total_kernel(own_ref, got_ref, out_ref, square_ref):
    add_kernel(own_ref, got_ref, out_ref)
    squares = jnp.sum(jnp.square(out_ref[...].astype(F32))).reshape(1, 1)
    square_ref[...] = jnp.broadcast_to(squares, square_ref.shape)


def clip_kernel(ceiling, square_ref, other_ref, own_ref, got_ref, up_ref, down_ref):
    squares = square_ref[:1, :1] + other_ref[:1, :1]
    factor = jnp.minimum(1.0, ceiling / (jnp.sqrt(squares) + 1e-06))
    parity = lax.axis_index("ctx") % 2
    up_step, down_step = up_ref.shape[1] // 2, down_ref.shape[1] // 2
    for index, ref in ((parity, own_ref), (1 - parity, got_ref)):
        columns = pl.ds(pl.multiple_of(index * up_step, up_step), up_step)
        up_ref[:, columns] = ref[:, :up_step].astype(F32) * factor
        columns = pl.ds(pl.multiple_of(index * down_step, down_step), down_step)
        down_ref[:, columns] = ref[:, up_step:].astype(F32) * factor


def split_model_width(
    hidden, gain, queries, key_value_weight, adapt_down, adapt_up, out_grad, doc_ids
):
    place = lax.axis_index("ctx")
    rows = hidden.shape[1]
    local_width = hidden.shape[2]
    slice_width = key_value_weight.shape[1]
    kv_count, head = key_value_weight.shape[2], key_value_weight.shape[-1]
    head_count = queries.shape[2]
    local_query = head_count * head
    rank = adapt_down.shape[1]
    kv_width = kv_count * 2 * head
    sent_width = kv_count * 3 * head

    half = rows // 2
    core = lax.axis_index("tp")
    mine = lax.dynamic_slice_in_dim(hidden[0], core * half, half, 0)
    theirs = lax.dynamic_slice_in_dim(hidden[0], (1 - core) * half, half, 0)
    part = ((half, slice_width), BF16)
    slices = call(
        norm_kernel, [part] * 4, mine, swap(theirs, "tp", 1), gain, swap(gain, "tp", 1)
    )

    def send_a(value):
        return lax.ppermute(
            value, ("ctx", "tp"), [(2 * a + t, 2 * (a ^ (3 if t else 1)) + t) for a in range(4) for t in range(2)]
        )

    def send_b(value):
        return lax.ppermute(
            value, ("ctx", "tp"), [(2 * a + t, 2 * (a ^ (1 if t else 3)) + t) for a in range(4) for t in range(2)]
        )

    even, slice_a, slice_b, slice_c = slices
    got_a, got_b, got_c = send_a(slice_a), send_b(slice_b), swap(slice_c, "ctx", 2)
    part_flops = 2 * rows * slice_width * kv_width
    packed = ((rows, sent_width), BF16)
    summed = ((rows, kv_width), F32)
    final = ((rows + 16, kv_width), BF16)

    def step(function, *operands):
        shapes = jax.eval_shape(function, *operands)
        return lax.cond(
            place < 4,
            function,
            lambda *_: jax.tree.map(lambda x: jnp.zeros(x.shape, x.dtype), shapes),
            *operands,
        )

    def prepare(key_value_weight):
        return key_value_weight[0].reshape(slice_width, kv_width)

    weight = step(prepare, key_value_weight)

    def prepare_attention(queries, out_grad, adapt_up, doc_ids, weight):
        docs = doc_ids.astype(F32).reshape(1, rows)
        freqs = 1000000.0 ** (-jnp.arange(head // 2, dtype=F32) * 2.0 / head)
        positions = place * rows + jnp.arange(rows, dtype=jnp.int32)
        angles = positions.astype(F32)[:, None] * freqs
        cosine, sine = jnp.cos(angles), jnp.sin(angles)
        cosine = jnp.concatenate([cosine, cosine], axis=1)
        sine = jnp.concatenate([-sine, sine], axis=1)
        (query,) = call(
            query_kernel,
            [((head_count * rows, head), BF16)],
            queries[0].reshape(rows, local_query),
            cosine,
            sine,
        )
        (back_part,) = call(
            back_kernel,
            [((rows, rank), F32)],
            out_grad[0],
            adapt_up[0],
            flops=2 * rows * local_width * rank,
        )
        return docs, cosine, sine, query, back_part, swap(back_part, "tp", 1)

    docs, cosine, sine, query, back_part, back_other = step(
        prepare_attention, queries, out_grad, adapt_up, doc_ids, weight
    )
    part_0, weight_near = call(
        functools.partial(own_kernel, head),
        [summed, (weight.shape, BF16)],
        even,
        swap(even, "tp", 1),
        weight,
        flops=part_flops,
        scratch=[pltpu.VMEM((rows, slice_width), BF16)],
    )
    got_c, part_0, docs = lax.optimization_barrier((got_c, part_0, docs))

    def far_parts(got_c, weight):
        return call(
            functools.partial(far_kernel, head),
            [packed],
            got_c,
            swap(got_c, "tp", 1),
            weight,
            flops=part_flops,
            scratch=[pltpu.VMEM((rows, slice_width), BF16)],
        )

    (sent_c,) = step(far_parts, got_c, weight)
    arrived_c = swap(sent_c, "ctx", 2)
    got_a, got_b, sent_c = lax.optimization_barrier((got_a, got_b, sent_c))
    sent_a, sent_b = call(
        functools.partial(near_kernel, head),
        [packed, packed],
        got_a,
        swap(got_a, "tp", 1),
        got_b,
        swap(got_b, "tp", 1),
        weight_near,
        flops=2 * part_flops,
        scratch=[pltpu.VMEM((2 * rows, slice_width), BF16)],
    )
    arrived_a, arrived_b = send_a(sent_a), send_b(sent_b)
    part_0, docs, cosine, sine = call(
        accumulate_kernel,
        [summed, ((1, rows), F32), ((rows, head), F32), ((rows, head), F32)],
        part_0,
        arrived_c,
        docs,
        cosine,
        sine,
    )
    arrived_a, arrived_b, part_0 = lax.optimization_barrier((arrived_a, arrived_b, part_0))
    (block_0,) = call(finish_kernel, [final], part_0, arrived_a, arrived_b, docs, cosine, sine)

    attended, low_part, down_part = call(
        functools.partial(attention_kernel, head),
        [((rows, local_query), BF16), ((rows, rank), F32), ((rank, local_query), F32)],
        query,
        block_0,
        send_a(block_0),
        send_b(block_0),
        swap(block_0, "ctx", 2),
        adapt_down[0],
        back_part,
        back_other,
        flops=16 * rows * rows * local_query,
    )
    low_other = swap(low_part, "tp", 1)
    piece = (rank, (local_width + local_query) // 2)
    own, sent = call(
        grads_kernel,
        [(piece, F32), (piece, BF16)],
        low_part,
        low_other,
        out_grad[0],
        down_part,
        flops=2 * rows * rank * local_width,
    )
    (adapter_rows,) = call(
        adapter_kernel,
        [((rows, local_width), BF16)],
        low_part,
        low_other,
        adapt_up[0],
        flops=2 * rows * rank * local_width,
    )
    got_sum, adapter_rows = lax.optimization_barrier((swap(sent, "ctx", 1), adapter_rows))
    (pair_sum,) = call(add_kernel, [(piece, BF16)], own, got_sum)
    total, squares = call(
        total_kernel, [(piece, BF16), ((8, 128), F32)], pair_sum, swap(pair_sum, "ctx", 2)
    )
    total_other = swap(total, "ctx", 1)
    squares = squares + swap(squares, "tp", 1)
    beside = lax.ppermute(
        squares,
        ("section", "tp"),
        [(2 * i + t, 2 * (i ^ (2 if t else 1)) + t) for i in range(4) for t in range(2)],
    )
    across = swap(squares, "section", 3)
    squares = jnp.where(core == 0, squares + across + beside, beside)
    squares = squares + swap(squares, "ctx", 1)
    ceiling = 0.5 * math.sqrt(lax.axis_size("section") * rank * (local_query + local_width) * 2)
    grad_up, grad_down = call(
        functools.partial(clip_kernel, ceiling),
        [((rank, local_width), F32), ((rank, local_query), F32)],
        squares,
        swap(squares, "tp", 1),
        total,
        total_other,
    )
    return (attended[None], adapter_rows[None], grad_down[None], grad_up[None])


def per_device(*arrays):
    if lax.axis_size("ctx") == 4 and lax.axis_size("tp") == 2 and lax.axis_size("section") == 4:
        return split_model_width(*arrays)
    return gathered_weights(*arrays)


def solution(mesh):
    return jax.shard_map(
        per_device,
        mesh=mesh,
        in_specs=(
            P("section", "ctx", "tp"),
            P("section", "tp"),
            P("section", "ctx", "tp", None),
            P("section", "ctx", "tp", None, None),
            P("section", None, "tp"),
            P("section", None, "tp"),
            P("section", "ctx", "tp"),
            P("ctx"),
        ),
        out_specs=(
            P("section", "ctx", "tp"),
            P("section", "ctx", "tp"),
            P("section", None, "tp"),
            P("section", None, "tp"),
        ),
        check_vma=False,
    )
```

```python
import functools
import math

import jax
import jax.numpy as jnp
from jax import lax
from jax.experimental import pallas as pl
from jax.experimental.pallas import tpu as pltpu
from jax.sharding import PartitionSpec as P


def rotate(head_values, positions):
    half_width = head_values.shape[-1] // 2
    freqs = 1000000.0 ** (-jnp.arange(half_width, dtype=jnp.float32) * 2.0 / head_values.shape[-1])
    angles = positions.astype(jnp.float32)[:, None] * freqs[None, :]
    cosine = jnp.cos(angles)[:, None, :]
    sine_table = jnp.sin(angles)[:, None, :]
    first_half = head_values[..., :half_width]
    second_half = head_values[..., half_width:]
    return jnp.concatenate(
        [
            first_half * cosine - second_half * sine_table,
            second_half * cosine + first_half * sine_table,
        ],
        axis=-1,
    )


def gathered_weights(hidden, gain, queries, key_value_weight, adapt_down, adapt_up, out_grad, doc_ids):
    tp_count = lax.axis_size("tp")
    row_count = hidden.shape[1]
    local_width = hidden.shape[2]
    head_dim = key_value_weight.shape[-1]
    kv_count = key_value_weight.shape[2]
    head_count = queries.shape[2]
    group_size = head_count // kv_count
    local_query = head_count * head_dim
    rank_size = adapt_down.shape[1]
    key_block = 1024
    full_rows, full_gain = (
        lax.all_gather(hidden, "tp", axis=2, tiled=True),
        lax.all_gather(gain, "tp", axis=1, tiled=True),
    )
    widened = full_rows[0].astype(jnp.float32)
    normalized_rows = (
        widened
        * lax.rsqrt(jnp.mean(widened * widened, axis=1, keepdims=True) + 1e-06)
        * full_gain[0].astype(jnp.float32)
    ).astype(jnp.bfloat16)
    kv_local = key_value_weight.reshape(1, key_value_weight.shape[1], kv_count * 2 * head_dim)
    keyval_raw = jnp.dot(
        normalized_rows,
        lax.all_gather(kv_local, "ctx", axis=1, tiled=True)[0],
        preferred_element_type=jnp.float32,
    )
    positions = lax.axis_index("ctx") * row_count + jnp.arange(row_count, dtype=jnp.int32)
    key_value_rows = keyval_raw.reshape(row_count, kv_count, 2, head_dim)
    rotated_keys = rotate(key_value_rows[:, :, 0], positions).astype(jnp.bfloat16)
    value_rows = key_value_rows[:, :, 1].astype(jnp.bfloat16)
    rotated_query = rotate(queries[0].astype(jnp.float32), positions).astype(jnp.bfloat16)
    stacked = (
        rotated_query.reshape(row_count, kv_count, group_size, head_dim)
        .transpose(1, 2, 0, 3)
        .reshape(kv_count, group_size * row_count, head_dim)
    )
    query_pos = jnp.tile(positions, group_size)
    query_doc = jnp.tile(doc_ids, group_size).astype(jnp.float32)
    score_scale = head_dim ** (-0.5)
    start_state = (
        jnp.full((kv_count, group_size * row_count), -1e30, jnp.float32),
        jnp.zeros((kv_count, group_size * row_count), jnp.float32),
        jnp.zeros((kv_count, group_size * row_count, head_dim), jnp.float32),
    )
    carried = start_state
    first_row = jnp.int32(0)
    piece_keys = lax.all_gather(rotated_keys, "ctx", axis=0, tiled=True)
    piece_values = lax.all_gather(value_rows, "ctx", axis=0, tiled=True)
    piece_docs = lax.all_gather(doc_ids.astype(jnp.bfloat16), "ctx", axis=0, tiled=True)
    key_total = piece_keys.shape[0]
    for block_start in range(0, key_total, key_block):
        block_stop = min(key_total, block_start + key_block)
        block_keys = piece_keys[block_start:block_stop]
        block_values = piece_values[block_start:block_stop]
        key_pos = first_row + block_start + jnp.arange(block_keys.shape[0], dtype=jnp.int32)
        key_doc = piece_docs[block_start:block_stop].astype(jnp.float32)
        running_top, running_sum, running_acc = carried
        scores = (
            jnp.einsum("gqd,kgd->gqk", stacked, block_keys, preferred_element_type=jnp.float32)
            * score_scale
        )
        allowed = (
            (key_pos[None, :] <= query_pos[:, None]) & (key_doc[None, :] == query_doc[:, None])
        )[None]
        scores = jnp.where(allowed, scores, -1e30)
        new_top = jnp.maximum(running_top, jnp.max(scores, axis=2))
        weights = jnp.where(allowed, jnp.exp(scores - new_top[:, :, None]), 0.0)
        shrink = jnp.exp(running_top - new_top)
        new_acc = running_acc * shrink[:, :, None] + jnp.einsum(
            "gqk,kgd->gqd",
            weights.astype(jnp.bfloat16),
            block_values,
            preferred_element_type=jnp.float32,
        )
        carried = (new_top, running_sum * shrink + jnp.sum(weights, axis=2), new_acc)
    final_top, final_sum, final_acc = carried
    attended = (
        (final_acc / final_sum[:, :, None])
        .reshape(kv_count, group_size, row_count, head_dim)
        .transpose(2, 0, 1, 3)
        .reshape(row_count, local_query)
        .astype(jnp.bfloat16)
    )
    low_part = jnp.dot(attended, adapt_down[0].T, preferred_element_type=jnp.float32)
    back_part = jnp.dot(out_grad[0], adapt_up[0].T, preferred_element_type=jnp.float32)
    low_sum, back_sum = lax.psum((low_part, back_part), "tp")
    low_rows = low_sum.astype(jnp.bfloat16)
    back_rows = back_sum.astype(jnp.bfloat16)
    adapter_rows = jnp.dot(low_rows, adapt_up[0], preferred_element_type=jnp.float32).astype(
        jnp.bfloat16
    )
    up_part = jnp.dot(low_rows.T, out_grad[0], preferred_element_type=jnp.float32)
    down_part = jnp.dot(back_rows.T, attended, preferred_element_type=jnp.float32)
    ceiling = 0.5 * math.sqrt(
        lax.axis_size("section") * rank_size * (local_query + local_width) * tp_count
    )
    up_total, down_total = (
        lax.psum(up_part.astype(jnp.bfloat16), "ctx").astype(jnp.float32),
        lax.psum(down_part.astype(jnp.bfloat16), "ctx").astype(jnp.float32),
    )
    local_squares = jnp.sum(up_total * up_total) + jnp.sum(down_total * down_total)
    squares = lax.psum(local_squares, ("section", "tp"))
    factor = jnp.minimum(1.0, ceiling / (jnp.sqrt(squares) + 1e-06))
    grad_up = up_total * factor
    grad_down = down_total * factor
    return (attended[None], adapter_rows[None], grad_down[None], grad_up[None])


F32, BF16 = jnp.float32, jnp.bfloat16
VMEM = pl.BlockSpec(memory_space=pltpu.VMEM)
LIMIT = 16 * 1024 * 1024
STEPS = 10.0


def swap(value, axis, distance):
    count = lax.axis_size(axis)
    return lax.ppermute(value, axis, [(i, i ^ distance) for i in range(count)])


def call(kernel, outs, *operands, flops=0, scratch=(), loose=()):
    shapes = [jax.ShapeDtypeStruct(shape, dtype) for shape, dtype in outs]
    moved = sum(math.prod(x.shape) * x.dtype.itemsize for x in (*operands, *shapes))
    return pl.pallas_call(
        kernel,
        out_shape=shapes,
        in_specs=[pl.BlockSpec(memory_space=pl.ANY) if i in loose else VMEM for i in range(len(operands))],
        out_specs=[VMEM] * len(shapes),
        scratch_shapes=scratch,
        compiler_params=pltpu.CompilerParams(vmem_limit_bytes=LIMIT),
        cost_estimate=pl.CostEstimate(flops=flops, bytes_accessed=moved, transcendentals=0),
    )(*operands)


def times(left, right):
    return lax.dot_general(left, right, (((1,), (0,)), ((), ())), preferred_element_type=F32)


def times_transposed(left, right):
    return lax.dot_general(left, right, (((1,), (1,)), ((), ())), preferred_element_type=F32)


def transposed_times(left, right):
    return lax.dot_general(left, right, (((0,), (0,)), ((), ())), preferred_element_type=F32)


def distances():
    core = lax.axis_index("tp")
    return 0, jnp.where(core == 0, 1, 2), jnp.where(core == 0, 2, 1), 3


def norm_kernel(mine_ref, other_ref, gain_ref, gain_other_ref, *outs):
    width = outs[0].shape[1]
    place, core = lax.axis_index("ctx"), lax.axis_index("tp")
    mine, other = mine_ref[...].astype(F32), other_ref[...].astype(F32)
    squares = [jnp.sum(rows * rows, axis=1, keepdims=True) for rows in (mine, other)]
    scale = lax.rsqrt((squares[0] + squares[1]) / (4 * width) + 1e-06)
    for d, out_ref in zip(distances(), outs):
        chip = place ^ d
        columns = pl.ds(pl.multiple_of(chip % 2 * width, width), width)

        def write(rows_ref, weights_ref, out_ref=out_ref, columns=columns):
            rows = rows_ref[:, columns].astype(F32) * scale
            out_ref[...] = (rows * weights_ref[:, columns].astype(F32)).astype(BF16)

        pl.when(chip // 2 == core)(functools.partial(write, mine_ref, gain_ref))
        pl.when(chip // 2 != core)(functools.partial(write, other_ref, gain_other_ref))


def join_rows(mine_ref, other_ref, out_ref):
    count = mine_ref.shape[0]
    core = lax.axis_index("tp")
    out_ref[pl.ds(pl.multiple_of(core * count, count), count)] = mine_ref[...]
    out_ref[pl.ds(pl.multiple_of((1 - core) * count, count), count)] = other_ref[...]


def split_heads(value, head):
    count = value.shape[1] // (2 * head)
    pieces = [value[:, i * head : (i + 1) * head] for i in range(2 * count)]
    return jnp.concatenate(pieces[0::2], axis=1), jnp.concatenate(pieces[1::2], axis=1)


def pack(value, out_ref, head):
    keys, values = split_heads(value, head)
    store_packed(keys, values, out_ref)


def store_packed(keys, values, out_ref):
    rows, width = keys.shape
    high = keys.astype(BF16)
    wide = high.astype(F32)
    size = jnp.abs(wide)
    steps = jnp.round((keys - wide) * (256.0 * STEPS) / jnp.where(size > 0, size, 1.0))
    half = width // 2
    out_ref[:rows, :width] = high
    out_ref[:rows, width : 2 * width] = values.astype(BF16)
    pairs = steps[:, :half] * (2.0 * STEPS + 1.0) + steps[:, half:]
    out_ref[:rows, 2 * width :] = pairs.astype(BF16)


def unpack(ref, rows):
    width = ref.shape[1] * 2 // 5
    wide = ref[:rows, :width].astype(F32)
    pairs = ref[:rows, 2 * width :].astype(F32)
    first = jnp.round(pairs / (2.0 * STEPS + 1.0))
    steps = jnp.concatenate([first, pairs - first * (2.0 * STEPS + 1.0)], axis=1)
    keys = wide + jnp.abs(wide) * steps * (1.0 / (256.0 * STEPS))
    return keys, ref[:rows, width : 2 * width].astype(F32)


def store_docs(docs, out_ref):
    rows = docs.shape[1]
    out_ref[rows:, :rows] = jnp.broadcast_to(docs, (16, rows)).astype(BF16)


def load_docs(ref):
    return ref[-16:, : ref.shape[0] - 16].astype(F32)[:1]


def own_kernel(head, even_ref, even_other_ref, weight_ref, own_ref, weight_out_ref, rows_ref):
    weight_out_ref[...] = weight_ref[...]
    join_rows(even_ref, even_other_ref, rows_ref)
    product = times(rows_ref[...], weight_ref[...])
    own_ref[...] = jnp.concatenate(split_heads(product, head), axis=1)


def far_kernel(head, got_ref, got_other_ref, weight_ref, sent_ref, rows_ref):
    join_rows(got_ref, got_other_ref, rows_ref)
    pack(times(rows_ref[...], weight_ref[...]), sent_ref, head)


def near_kernel(
    head,
    got_a_ref,
    got_a_other_ref,
    got_b_ref,
    got_b_other_ref,
    weight_ref,
    sent_a_ref,
    sent_b_ref,
    rows_ref,
):
    count = sent_a_ref.shape[0]
    join_rows(got_a_ref, got_b_other_ref, rows_ref.at[:count])
    join_rows(got_b_ref, got_a_other_ref, rows_ref.at[count:])
    product = times(rows_ref[...], weight_ref[...])
    pack(product[:count], sent_a_ref, head)
    pack(product[count:], sent_b_ref, head)


def turn(value, cosine, sine):
    head = cosine.shape[1]
    pieces = []
    for i in range(value.shape[1] // head):
        piece = value[:, i * head : (i + 1) * head]
        pieces.append(piece * cosine + pltpu.roll(piece, head // 2, 1) * sine)
    return jnp.concatenate(pieces, axis=1)


def query_kernel(query_ref, cosine_ref, sine_ref, out_ref):
    rows, head = cosine_ref.shape
    for index in range(query_ref.shape[1] // head):
        piece = query_ref[:, index * head : (index + 1) * head].astype(F32)
        out_ref[index * rows : (index + 1) * rows] = turn(
            piece, cosine_ref[...], sine_ref[...]
        ).astype(BF16)


def accumulate_kernel(
    own_ref, got_ref, docs_ref, cosine_ref, sine_ref, out_ref, docs_out_ref, cosine_out_ref, sine_out_ref
):
    keys, values = unpack(got_ref, own_ref.shape[0])
    width = keys.shape[1]
    out_ref[:, :width] = own_ref[:, :width] + keys
    out_ref[:, width:] = own_ref[:, width:] + values
    for ref, copy_ref in (
        (docs_ref, docs_out_ref),
        (cosine_ref, cosine_out_ref),
        (sine_ref, sine_out_ref),
    ):
        copy_ref[...] = ref[...]


def finish_kernel(own_ref, got_a_ref, got_b_ref, docs_ref, cosine_ref, sine_ref, out_ref):
    rows = own_ref.shape[0]
    width = own_ref.shape[1] // 2
    keys, values = own_ref[:, :width], own_ref[:, width:]
    for ref in (got_a_ref, got_b_ref):
        more_keys, more_values = unpack(ref, rows)
        keys, values = keys + more_keys, values + more_values
    out_ref[:rows, :width] = turn(keys, cosine_ref[...], sine_ref[...]).astype(BF16)
    out_ref[:rows, width:] = values.astype(BF16)
    store_docs(docs_ref[...], out_ref)


def allowed_pairs(own_docs, key_docs, distance):
    rows = own_docs.shape[1]
    place = lax.axis_index("ctx")
    query_docs = jnp.broadcast_to(own_docs, (rows, rows)).T
    query_at = place * rows + lax.broadcasted_iota(jnp.int32, (rows, rows), 0)
    key_at = (place ^ distance) * rows + lax.broadcasted_iota(jnp.int32, (rows, rows), 1)
    return (key_at <= query_at) & (key_docs == query_docs)


def group_scores(query_ref, keys, allowed, head, group):
    rows = allowed.shape[0]
    groups = keys.shape[1] // head
    count = query_ref.shape[0] // groups
    scores = times_transposed(
        query_ref[group * count : (group + 1) * count], keys[:, group * head : (group + 1) * head]
    ).reshape(count // rows, rows, keys.shape[0])
    return jnp.where(allowed[None], scores, -1e30).reshape(count, keys.shape[0])


def attention_kernel(
    head,
    query_ref,
    block_0_ref,
    block_a_ref,
    block_b_ref,
    block_c_ref,
    down_ref,
    back_ref,
    back_other_ref,
    out_ref,
    low_ref,
    grad_ref,
):
    rows = block_0_ref.shape[0] - 16
    width = block_0_ref.shape[1] // 2
    blocks = (block_0_ref, block_a_ref, block_b_ref, block_c_ref)
    keys = jnp.concatenate([ref[:rows, :width] for ref in blocks], axis=0)
    values = jnp.concatenate([ref[:rows, width:] for ref in blocks], axis=0)
    own_docs = load_docs(block_0_ref)
    allowed = jnp.concatenate(
        [allowed_pairs(own_docs, load_docs(ref), d) for d, ref in zip(distances(), blocks)], axis=1
    )
    groups = width // head
    count = query_ref.shape[0] // groups
    scale = head ** (-0.5) * math.log2(math.e)
    ones = jnp.ones((len(blocks) * rows, head), BF16)
    for group in range(groups):
        scores = group_scores(query_ref, keys, allowed, head, group)
        weights = jnp.exp2((scores - jnp.max(scores, axis=1, keepdims=True)) * scale)
        group_values = jnp.concatenate([values[:, group * head : (group + 1) * head], ones], axis=1)
        mixed = times(weights.astype(BF16), group_values)
        mixed = (mixed[:, :head] / mixed[:, head:]).astype(BF16)
        for index in range(count // rows):
            column = group * count // rows * head + index * head
            out_ref[:, column : column + head] = mixed[index * rows : (index + 1) * rows]
    attended = out_ref[...]
    low_ref[...] = times_transposed(attended, down_ref[...])
    back = (back_ref[...] + back_other_ref[...]).astype(BF16)
    grad_ref[...] = transposed_times(back, attended)


def back_kernel(grad_ref, up_ref, out_ref):
    out_ref[...] = times_transposed(grad_ref[...], up_ref[...])


def grads_kernel(low_ref, low_other_ref, grad_ref, down_ref, own_ref, sent_ref):
    low = (low_ref[...] + low_other_ref[...]).astype(BF16)
    parity = lax.axis_index("ctx") % 2
    up_step, down_step = grad_ref.shape[1] // 2, down_ref.shape[1] // 2
    for index, out in ((1 - parity, sent_ref), (parity, own_ref)):
        columns = pl.ds(pl.multiple_of(index * up_step, up_step), up_step)
        out[:, :up_step] = transposed_times(low, grad_ref[:, columns]).astype(out.dtype)
        columns = pl.ds(pl.multiple_of(index * down_step, down_step), down_step)
        out[:, up_step:] = down_ref[:, columns].astype(out.dtype)


def adapter_kernel(low_ref, low_other_ref, up_ref, out_ref):
    low = (low_ref[...] + low_other_ref[...]).astype(BF16)
    out_ref[...] = times(low, up_ref[...]).astype(BF16)


def add_kernel(own_ref, got_ref, out_ref):
    out_ref[...] = (own_ref[...].astype(F32) + got_ref[...].astype(F32)).astype(BF16)


def total_kernel(own_ref, got_ref, out_ref, square_ref):
    add_kernel(own_ref, got_ref, out_ref)
    squares = jnp.sum(jnp.square(out_ref[...].astype(F32))).reshape(1, 1)
    square_ref[...] = jnp.broadcast_to(squares, square_ref.shape)


def clip_kernel(ceiling, square_ref, other_ref, own_ref, got_ref, up_ref, down_ref):
    squares = square_ref[:1, :1] + other_ref[:1, :1]
    factor = jnp.minimum(1.0, ceiling / (jnp.sqrt(squares) + 1e-06))
    parity = lax.axis_index("ctx") % 2
    up_step, down_step = up_ref.shape[1] // 2, down_ref.shape[1] // 2
    for index, ref in ((parity, own_ref), (1 - parity, got_ref)):
        columns = pl.ds(pl.multiple_of(index * up_step, up_step), up_step)
        up_ref[:, columns] = ref[:, :up_step].astype(F32) * factor
        columns = pl.ds(pl.multiple_of(index * down_step, down_step), down_step)
        down_ref[:, columns] = ref[:, up_step:].astype(F32) * factor


def split_model_width(
    hidden, gain, queries, key_value_weight, adapt_down, adapt_up, out_grad, doc_ids
):
    place = lax.axis_index("ctx")
    rows = hidden.shape[1]
    local_width = hidden.shape[2]
    slice_width = key_value_weight.shape[1]
    kv_count, head = key_value_weight.shape[2], key_value_weight.shape[-1]
    head_count = queries.shape[2]
    local_query = head_count * head
    rank = adapt_down.shape[1]
    kv_width = kv_count * 2 * head
    sent_width = kv_count * 5 * head // 2

    half = rows // 2
    core = lax.axis_index("tp")
    mine = lax.dynamic_slice_in_dim(hidden[0], core * half, half, 0)
    theirs = lax.dynamic_slice_in_dim(hidden[0], (1 - core) * half, half, 0)
    part = ((half, slice_width), BF16)
    slices = call(
        norm_kernel, [part] * 4, mine, swap(theirs, "tp", 1), gain, swap(gain, "tp", 1)
    )

    def send_a(value):
        return lax.ppermute(
            value, ("ctx", "tp"), [(2 * a + t, 2 * (a ^ (2 if t else 1)) + t) for a in range(4) for t in range(2)]
        )

    def send_b(value):
        return lax.ppermute(
            value, ("ctx", "tp"), [(2 * a + t, 2 * (a ^ (1 if t else 2)) + t) for a in range(4) for t in range(2)]
        )

    even, slice_a, slice_b, slice_c = slices
    got_a, got_b, got_c = send_a(slice_a), send_b(slice_b), swap(slice_c, "ctx", 3)
    part_flops = 2 * rows * slice_width * kv_width
    packed = ((rows, sent_width), BF16)
    summed = ((rows, kv_width), F32)
    final = ((rows + 16, kv_width), BF16)

    def step(function, *operands):
        shapes = jax.eval_shape(function, *operands)
        return lax.cond(
            place < 4,
            function,
            lambda *_: jax.tree.map(lambda x: jnp.zeros(x.shape, x.dtype), shapes),
            *operands,
        )

    def prepare(key_value_weight):
        return key_value_weight[0].reshape(slice_width, kv_width)

    weight = step(prepare, key_value_weight)

    def prepare_attention(queries, out_grad, adapt_up, doc_ids, weight):
        docs = doc_ids.astype(F32).reshape(1, rows)
        freqs = 1000000.0 ** (-jnp.arange(head // 2, dtype=F32) * 2.0 / head)
        positions = place * rows + jnp.arange(rows, dtype=jnp.int32)
        angles = positions.astype(F32)[:, None] * freqs
        cosine, sine = jnp.cos(angles), jnp.sin(angles)
        cosine = jnp.concatenate([cosine, cosine], axis=1)
        sine = jnp.concatenate([-sine, sine], axis=1)
        (query,) = call(
            query_kernel,
            [((head_count * rows, head), BF16)],
            queries[0].reshape(rows, local_query),
            cosine,
            sine,
        )
        (back_part,) = call(
            back_kernel,
            [((rows, rank), F32)],
            out_grad[0],
            adapt_up[0],
            flops=2 * rows * local_width * rank,
        )
        return docs, cosine, sine, query, back_part, swap(back_part, "tp", 1)

    docs, cosine, sine, query, back_part, back_other = step(
        prepare_attention, queries, out_grad, adapt_up, doc_ids, weight
    )
    part_0, weight_near = call(
        functools.partial(own_kernel, head),
        [summed, (weight.shape, BF16)],
        even,
        swap(even, "tp", 1),
        weight,
        flops=part_flops,
        scratch=[pltpu.VMEM((rows, slice_width), BF16)],
    )
    got_c, part_0, docs = lax.optimization_barrier((got_c, part_0, docs))

    def far_parts(got_c, weight):
        return call(
            functools.partial(far_kernel, head),
            [packed],
            got_c,
            swap(got_c, "tp", 1),
            weight,
            flops=part_flops,
            scratch=[pltpu.VMEM((rows, slice_width), BF16)],
        )

    (sent_c,) = step(far_parts, got_c, weight)
    arrived_c = swap(sent_c, "ctx", 3)
    got_a, got_b, sent_c = lax.optimization_barrier((got_a, got_b, sent_c))
    sent_a, sent_b = call(
        functools.partial(near_kernel, head),
        [packed, packed],
        got_a,
        swap(got_a, "tp", 1),
        got_b,
        swap(got_b, "tp", 1),
        weight_near,
        flops=2 * part_flops,
        scratch=[pltpu.VMEM((2 * rows, slice_width), BF16)],
    )
    arrived_a, arrived_b = send_a(sent_a), send_b(sent_b)
    part_0, docs, cosine, sine = call(
        accumulate_kernel,
        [summed, ((1, rows), F32), ((rows, head), F32), ((rows, head), F32)],
        part_0,
        arrived_c,
        docs,
        cosine,
        sine,
    )
    arrived_a, arrived_b, part_0 = lax.optimization_barrier((arrived_a, arrived_b, part_0))
    (block_0,) = call(finish_kernel, [final], part_0, arrived_a, arrived_b, docs, cosine, sine)

    attended, low_part, down_part = call(
        functools.partial(attention_kernel, head),
        [((rows, local_query), BF16), ((rows, rank), F32), ((rank, local_query), F32)],
        query,
        block_0,
        send_a(block_0),
        send_b(block_0),
        swap(block_0, "ctx", 3),
        adapt_down[0],
        back_part,
        back_other,
        flops=16 * rows * rows * local_query,
    )
    low_other = swap(low_part, "tp", 1)
    piece = (rank, (local_width + local_query) // 2)
    own, sent = call(
        grads_kernel,
        [(piece, F32), (piece, BF16)],
        low_part,
        low_other,
        out_grad[0],
        down_part,
        flops=2 * rows * rank * local_width,
    )
    (adapter_rows,) = call(
        adapter_kernel,
        [((rows, local_width), BF16)],
        low_part,
        low_other,
        adapt_up[0],
        flops=2 * rows * rank * local_width,
    )
    got_sum, adapter_rows = lax.optimization_barrier((swap(sent, "ctx", 1), adapter_rows))
    (pair_sum,) = call(add_kernel, [(piece, BF16)], own, got_sum)
    total, squares = call(
        total_kernel, [(piece, BF16), ((8, 128), F32)], pair_sum, swap(pair_sum, "ctx", 2)
    )
    total_other = swap(total, "ctx", 1)
    squares = squares + swap(squares, "tp", 1)
    beside = lax.ppermute(
        squares,
        ("section", "tp"),
        [(2 * i + t, 2 * (i ^ (2 if t else 1)) + t) for i in range(4) for t in range(2)],
    )
    across = swap(squares, "section", 3)
    squares = jnp.where(core == 0, squares + across + beside, beside)
    squares = squares + swap(squares, "ctx", 1)
    ceiling = 0.5 * math.sqrt(lax.axis_size("section") * rank * (local_query + local_width) * 2)
    grad_up, grad_down = call(
        functools.partial(clip_kernel, ceiling),
        [((rank, local_width), F32), ((rank, local_query), F32)],
        squares,
        swap(squares, "tp", 1),
        total,
        total_other,
    )
    return (attended[None], adapter_rows[None], grad_down[None], grad_up[None])


def per_device(*arrays):
    if lax.axis_size("ctx") == 4 and lax.axis_size("tp") == 2 and lax.axis_size("section") == 4:
        return split_model_width(*arrays)
    return gathered_weights(*arrays)


def solution(mesh):
    return jax.shard_map(
        per_device,
        mesh=mesh,
        in_specs=(
            P("section", "ctx", "tp"),
            P("section", "tp"),
            P("section", "ctx", "tp", None),
            P("section", "ctx", "tp", None, None),
            P("section", None, "tp"),
            P("section", None, "tp"),
            P("section", "ctx", "tp"),
            P("ctx"),
        ),
        out_specs=(
            P("section", "ctx", "tp"),
            P("section", "ctx", "tp"),
            P("section", None, "tp"),
            P("section", None, "tp"),
        ),
        check_vma=False,
    )
```

```python
import functools
import math

import jax
import jax.numpy as jnp
from jax import lax
from jax.experimental import pallas as pl
from jax.experimental.pallas import tpu as pltpu
from jax.sharding import PartitionSpec as P


def rotate(head_values, positions):
    half_width = head_values.shape[-1] // 2
    freqs = 1000000.0 ** (-jnp.arange(half_width, dtype=jnp.float32) * 2.0 / head_values.shape[-1])
    angles = positions.astype(jnp.float32)[:, None] * freqs[None, :]
    cosine = jnp.cos(angles)[:, None, :]
    sine_table = jnp.sin(angles)[:, None, :]
    first_half = head_values[..., :half_width]
    second_half = head_values[..., half_width:]
    return jnp.concatenate(
        [
            first_half * cosine - second_half * sine_table,
            second_half * cosine + first_half * sine_table,
        ],
        axis=-1,
    )


def gathered_weights(hidden, gain, queries, key_value_weight, adapt_down, adapt_up, out_grad, doc_ids):
    tp_count = lax.axis_size("tp")
    row_count = hidden.shape[1]
    local_width = hidden.shape[2]
    head_dim = key_value_weight.shape[-1]
    kv_count = key_value_weight.shape[2]
    head_count = queries.shape[2]
    group_size = head_count // kv_count
    local_query = head_count * head_dim
    rank_size = adapt_down.shape[1]
    key_block = 1024
    full_rows, full_gain = (
        lax.all_gather(hidden, "tp", axis=2, tiled=True),
        lax.all_gather(gain, "tp", axis=1, tiled=True),
    )
    widened = full_rows[0].astype(jnp.float32)
    normalized_rows = (
        widened
        * lax.rsqrt(jnp.mean(widened * widened, axis=1, keepdims=True) + 1e-06)
        * full_gain[0].astype(jnp.float32)
    ).astype(jnp.bfloat16)
    kv_local = key_value_weight.reshape(1, key_value_weight.shape[1], kv_count * 2 * head_dim)
    keyval_raw = jnp.dot(
        normalized_rows,
        lax.all_gather(kv_local, "ctx", axis=1, tiled=True)[0],
        preferred_element_type=jnp.float32,
    )
    positions = lax.axis_index("ctx") * row_count + jnp.arange(row_count, dtype=jnp.int32)
    key_value_rows = keyval_raw.reshape(row_count, kv_count, 2, head_dim)
    rotated_keys = rotate(key_value_rows[:, :, 0], positions).astype(jnp.bfloat16)
    value_rows = key_value_rows[:, :, 1].astype(jnp.bfloat16)
    rotated_query = rotate(queries[0].astype(jnp.float32), positions).astype(jnp.bfloat16)
    stacked = (
        rotated_query.reshape(row_count, kv_count, group_size, head_dim)
        .transpose(1, 2, 0, 3)
        .reshape(kv_count, group_size * row_count, head_dim)
    )
    query_pos = jnp.tile(positions, group_size)
    query_doc = jnp.tile(doc_ids, group_size).astype(jnp.float32)
    score_scale = head_dim ** (-0.5)
    start_state = (
        jnp.full((kv_count, group_size * row_count), -1e30, jnp.float32),
        jnp.zeros((kv_count, group_size * row_count), jnp.float32),
        jnp.zeros((kv_count, group_size * row_count, head_dim), jnp.float32),
    )
    carried = start_state
    first_row = jnp.int32(0)
    piece_keys = lax.all_gather(rotated_keys, "ctx", axis=0, tiled=True)
    piece_values = lax.all_gather(value_rows, "ctx", axis=0, tiled=True)
    piece_docs = lax.all_gather(doc_ids.astype(jnp.bfloat16), "ctx", axis=0, tiled=True)
    key_total = piece_keys.shape[0]
    for block_start in range(0, key_total, key_block):
        block_stop = min(key_total, block_start + key_block)
        block_keys = piece_keys[block_start:block_stop]
        block_values = piece_values[block_start:block_stop]
        key_pos = first_row + block_start + jnp.arange(block_keys.shape[0], dtype=jnp.int32)
        key_doc = piece_docs[block_start:block_stop].astype(jnp.float32)
        running_top, running_sum, running_acc = carried
        scores = (
            jnp.einsum("gqd,kgd->gqk", stacked, block_keys, preferred_element_type=jnp.float32)
            * score_scale
        )
        allowed = (
            (key_pos[None, :] <= query_pos[:, None]) & (key_doc[None, :] == query_doc[:, None])
        )[None]
        scores = jnp.where(allowed, scores, -1e30)
        new_top = jnp.maximum(running_top, jnp.max(scores, axis=2))
        weights = jnp.where(allowed, jnp.exp(scores - new_top[:, :, None]), 0.0)
        shrink = jnp.exp(running_top - new_top)
        new_acc = running_acc * shrink[:, :, None] + jnp.einsum(
            "gqk,kgd->gqd",
            weights.astype(jnp.bfloat16),
            block_values,
            preferred_element_type=jnp.float32,
        )
        carried = (new_top, running_sum * shrink + jnp.sum(weights, axis=2), new_acc)
    final_top, final_sum, final_acc = carried
    attended = (
        (final_acc / final_sum[:, :, None])
        .reshape(kv_count, group_size, row_count, head_dim)
        .transpose(2, 0, 1, 3)
        .reshape(row_count, local_query)
        .astype(jnp.bfloat16)
    )
    low_part = jnp.dot(attended, adapt_down[0].T, preferred_element_type=jnp.float32)
    back_part = jnp.dot(out_grad[0], adapt_up[0].T, preferred_element_type=jnp.float32)
    low_sum, back_sum = lax.psum((low_part, back_part), "tp")
    low_rows = low_sum.astype(jnp.bfloat16)
    back_rows = back_sum.astype(jnp.bfloat16)
    adapter_rows = jnp.dot(low_rows, adapt_up[0], preferred_element_type=jnp.float32).astype(
        jnp.bfloat16
    )
    up_part = jnp.dot(low_rows.T, out_grad[0], preferred_element_type=jnp.float32)
    down_part = jnp.dot(back_rows.T, attended, preferred_element_type=jnp.float32)
    ceiling = 0.5 * math.sqrt(
        lax.axis_size("section") * rank_size * (local_query + local_width) * tp_count
    )
    up_total, down_total = (
        lax.psum(up_part.astype(jnp.bfloat16), "ctx").astype(jnp.float32),
        lax.psum(down_part.astype(jnp.bfloat16), "ctx").astype(jnp.float32),
    )
    local_squares = jnp.sum(up_total * up_total) + jnp.sum(down_total * down_total)
    squares = lax.psum(local_squares, ("section", "tp"))
    factor = jnp.minimum(1.0, ceiling / (jnp.sqrt(squares) + 1e-06))
    grad_up = up_total * factor
    grad_down = down_total * factor
    return (attended[None], adapter_rows[None], grad_down[None], grad_up[None])


F32, BF16 = jnp.float32, jnp.bfloat16
VMEM = pl.BlockSpec(memory_space=pltpu.VMEM)
ANYWHERE = pl.BlockSpec(memory_space=pl.ANY)
LIMIT = 16 * 1024 * 1024
STEPS = 10.0


def swap(value, axis, distance):
    count = lax.axis_size(axis)
    return lax.ppermute(value, axis, [(i, i ^ distance) for i in range(count)])


def call(kernel, outs, *operands, flops=0, scratch=(), loose=(), loose_outs=()):
    shapes = [jax.ShapeDtypeStruct(shape, dtype) for shape, dtype in outs]
    moved = sum(math.prod(x.shape) * x.dtype.itemsize for x in (*operands, *shapes))
    return pl.pallas_call(
        kernel,
        out_shape=shapes,
        in_specs=[ANYWHERE if i in loose else VMEM for i in range(len(operands))],
        out_specs=[ANYWHERE if i in loose_outs else VMEM for i in range(len(shapes))],
        scratch_shapes=scratch,
        compiler_params=pltpu.CompilerParams(vmem_limit_bytes=LIMIT),
        cost_estimate=pl.CostEstimate(flops=flops, bytes_accessed=moved, transcendentals=0),
    )(*operands)


def times(left, right):
    return lax.dot_general(left, right, (((1,), (0,)), ((), ())), preferred_element_type=F32)


def times_transposed(left, right):
    return lax.dot_general(left, right, (((1,), (1,)), ((), ())), preferred_element_type=F32)


def transposed_times(left, right):
    return lax.dot_general(left, right, (((0,), (0,)), ((), ())), preferred_element_type=F32)


def distances():
    core = lax.axis_index("tp")
    return 0, jnp.where(core == 0, 1, 2), jnp.where(core == 0, 2, 1), 3


def norm_kernel(mine_ref, other_ref, gain_ref, gain_other_ref, *refs):
    outs, (held_ref, written) = refs[:4], refs[4:]
    width = outs[0].shape[1]
    place, core = lax.axis_index("ctx"), lax.axis_index("tp")
    mine, other = mine_ref[...].astype(F32), other_ref[...].astype(F32)
    squares = [jnp.sum(rows * rows, axis=1, keepdims=True) for rows in (mine, other)]
    scale = lax.rsqrt((squares[0] + squares[1]) / (4 * width) + 1e-06)
    copies = []
    for index in (3, 1, 2, 0):
        chip = place ^ distances()[index]
        columns = pl.ds(pl.multiple_of(chip % 2 * width, width), width)
        slot = outs[0] if index == 0 else held_ref.at[index - 1]

        def write(rows_ref, weights_ref, slot=slot, columns=columns):
            rows = rows_ref[:, columns].astype(F32) * scale
            slot[...] = (rows * weights_ref[:, columns].astype(F32)).astype(BF16)

        pl.when(chip // 2 == core)(functools.partial(write, mine_ref, gain_ref))
        pl.when(chip // 2 != core)(functools.partial(write, other_ref, gain_other_ref))
        if index:
            copies.append(pltpu.make_async_copy(slot, outs[index], written.at[index - 1]))
            copies[-1].start()
    for copy in copies:
        copy.wait()


def join_rows(mine_ref, other_ref, out_ref):
    count = mine_ref.shape[0]
    core = lax.axis_index("tp")
    out_ref[pl.ds(pl.multiple_of(core * count, count), count)] = mine_ref[...]
    out_ref[pl.ds(pl.multiple_of((1 - core) * count, count), count)] = other_ref[...]


def split_heads(value, head):
    count = value.shape[1] // (2 * head)
    pieces = [value[:, i * head : (i + 1) * head] for i in range(2 * count)]
    return jnp.concatenate(pieces[0::2], axis=1), jnp.concatenate(pieces[1::2], axis=1)


def pack(value, out_ref, head):
    keys, values = split_heads(value, head)
    store_packed(keys, values, out_ref)


def store_packed(keys, values, out_ref):
    rows, width = keys.shape
    high = keys.astype(BF16)
    wide = high.astype(F32)
    size = jnp.abs(wide)
    steps = jnp.round((keys - wide) * (256.0 * STEPS) / jnp.where(size > 0, size, 1.0))
    half = width // 2
    out_ref[:rows, :width] = high
    out_ref[:rows, width : 2 * width] = values.astype(BF16)
    pairs = steps[:, :half] * (2.0 * STEPS + 1.0) + steps[:, half:]
    out_ref[:rows, 2 * width :] = pairs.astype(BF16)


def unpack(ref, rows):
    width = ref.shape[1] * 2 // 5
    wide = ref[:rows, :width].astype(F32)
    pairs = ref[:rows, 2 * width :].astype(F32)
    first = jnp.round(pairs / (2.0 * STEPS + 1.0))
    steps = jnp.concatenate([first, pairs - first * (2.0 * STEPS + 1.0)], axis=1)
    keys = wide + jnp.abs(wide) * steps * (1.0 / (256.0 * STEPS))
    return keys, ref[:rows, width : 2 * width].astype(F32)


def store_docs(docs, out_ref):
    rows = docs.shape[1]
    out_ref[rows:, :rows] = jnp.broadcast_to(docs, (16, rows)).astype(BF16)


def load_docs(ref):
    return ref[-16:, : ref.shape[0] - 16].astype(F32)[:1]


def own_kernel(
    head, even_ref, even_other_ref, weight_ref, own_ref, weight_out_ref, rows_ref, arrived
):
    copy = pltpu.make_async_copy(weight_ref, weight_out_ref, arrived)
    copy.start()
    join_rows(even_ref, even_other_ref, rows_ref)
    copy.wait()
    product = times(rows_ref[...], weight_out_ref[...])
    own_ref[...] = jnp.concatenate(split_heads(product, head), axis=1)


def far_kernel(head, got_ref, got_other_ref, weight_ref, sent_ref, rows_ref):
    join_rows(got_ref, got_other_ref, rows_ref)
    pack(times(rows_ref[...], weight_ref[...]), sent_ref, head)


def near_kernel(
    head,
    got_a_ref,
    got_a_other_ref,
    got_b_ref,
    got_b_other_ref,
    weight_ref,
    sent_a_ref,
    sent_b_ref,
    rows_ref,
):
    count = sent_a_ref.shape[0]
    join_rows(got_a_ref, got_b_other_ref, rows_ref.at[:count])
    join_rows(got_b_ref, got_a_other_ref, rows_ref.at[count:])
    product = times(rows_ref[...], weight_ref[...])
    pack(product[:count], sent_a_ref, head)
    pack(product[count:], sent_b_ref, head)


def turn(value, cosine, sine):
    head = cosine.shape[1]
    pieces = []
    for i in range(value.shape[1] // head):
        piece = value[:, i * head : (i + 1) * head]
        pieces.append(piece * cosine + pltpu.roll(piece, head // 2, 1) * sine)
    return jnp.concatenate(pieces, axis=1)


def query_kernel(query_ref, cosine_ref, sine_ref, out_ref):
    rows, head = cosine_ref.shape
    for index in range(query_ref.shape[1] // head):
        piece = query_ref[:, index * head : (index + 1) * head].astype(F32)
        out_ref[index * rows : (index + 1) * rows] = turn(
            piece, cosine_ref[...], sine_ref[...]
        ).astype(BF16)


def accumulate_kernel(own_ref, got_ref, back_ref, back_other_ref, *refs):
    count = len(refs) // 2
    out_ref, back_out_ref = refs[count - 1 : count + 1]
    keys, values = unpack(got_ref, own_ref.shape[0])
    width = keys.shape[1]
    out_ref[:, :width] = own_ref[:, :width] + keys
    out_ref[:, width:] = own_ref[:, width:] + values
    back_out_ref[...] = (back_ref[...] + back_other_ref[...]).astype(BF16)
    for ref, copy_ref in zip(refs[: count - 1], refs[count + 1 :]):
        copy_ref[...] = ref[...]


def finish_kernel(own_ref, got_a_ref, got_b_ref, docs_ref, cosine_ref, sine_ref, out_ref):
    rows = own_ref.shape[0]
    width = own_ref.shape[1] // 2
    keys, values = own_ref[:, :width], own_ref[:, width:]
    for ref in (got_a_ref, got_b_ref):
        more_keys, more_values = unpack(ref, rows)
        keys, values = keys + more_keys, values + more_values
    out_ref[:rows, :width] = turn(keys, cosine_ref[...], sine_ref[...]).astype(BF16)
    out_ref[:rows, width:] = values.astype(BF16)
    store_docs(docs_ref[...], out_ref)


def allowed_pairs(own_docs, key_docs, distance):
    rows = own_docs.shape[1]
    place = lax.axis_index("ctx")
    query_docs = jnp.broadcast_to(own_docs, (rows, rows)).T
    query_at = place * rows + lax.broadcasted_iota(jnp.int32, (rows, rows), 0)
    key_at = (place ^ distance) * rows + lax.broadcasted_iota(jnp.int32, (rows, rows), 1)
    return (key_at <= query_at) & (key_docs == query_docs)


def attention_kernel(
    head,
    query_ref,
    block_0_ref,
    block_a_ref,
    block_b_ref,
    block_c_ref,
    down_ref,
    back_ref,
    out_ref,
    low_ref,
    grad_ref,
    mixed_ref,
    written,
):
    rows = block_0_ref.shape[0] - 16
    width = block_0_ref.shape[1] // 2
    blocks = (block_0_ref, block_a_ref, block_b_ref, block_c_ref)
    keys = jnp.concatenate([ref[:rows, :width] for ref in blocks], axis=0)
    values = jnp.concatenate([ref[:rows, width:] for ref in blocks], axis=0)
    own_docs = load_docs(block_0_ref)
    allowed = jnp.concatenate(
        [allowed_pairs(own_docs, load_docs(ref), d) for d, ref in zip(distances(), blocks)], axis=1
    )
    scale = head ** (-0.5) * math.log2(math.e)
    ones = jnp.ones((len(blocks) * rows, head), BF16)
    groups = width // head
    pairs = query_ref.shape[0] // (2 * rows)
    copies = []
    for pair in range(pairs):
        shared = slice(pair * groups // pairs * head, (pair * groups // pairs + 1) * head)
        scores = times_transposed(
            query_ref[2 * pair * rows : 2 * (pair + 1) * rows], keys[:, shared]
        ).reshape(2, rows, keys.shape[0])
        scores = jnp.where(allowed[None], scores, -1e30).reshape(2 * rows, keys.shape[0])
        weights = jnp.exp2((scores - jnp.max(scores, axis=1, keepdims=True)) * scale)
        mixed = times(
            weights.astype(BF16), jnp.concatenate([values[:, shared], ones], axis=1)
        )
        mixed = (mixed[:, :head] / mixed[:, head:]).astype(BF16)
        columns = slice(2 * pair * head, 2 * (pair + 1) * head)
        mixed_ref[:, columns] = jnp.concatenate([mixed[:rows], mixed[rows:]], axis=1)
        copies.append(
            pltpu.make_async_copy(
                mixed_ref.at[:, columns], out_ref.at[:, columns], written.at[pair]
            )
        )
        copies[-1].start()
    attended = mixed_ref[...]
    low_ref[...] = times_transposed(attended, down_ref[...])
    grad_ref[...] = transposed_times(back_ref[...], attended)
    for copy in copies:
        copy.wait()


def back_kernel(grad_ref, up_ref, out_ref):
    out_ref[...] = times_transposed(grad_ref[...], up_ref[...])


def grads_kernel(low_ref, low_other_ref, grad_ref, down_ref, own_ref, sent_ref):
    low = (low_ref[...] + low_other_ref[...]).astype(BF16)
    parity = lax.axis_index("ctx") % 2
    up_step, down_step = grad_ref.shape[1] // 2, down_ref.shape[1] // 2
    for index, out in ((1 - parity, sent_ref), (parity, own_ref)):
        columns = pl.ds(pl.multiple_of(index * up_step, up_step), up_step)
        out[:, :up_step] = transposed_times(low, grad_ref[:, columns]).astype(out.dtype)
        columns = pl.ds(pl.multiple_of(index * down_step, down_step), down_step)
        out[:, up_step:] = down_ref[:, columns].astype(out.dtype)


def adapter_kernel(low_ref, low_other_ref, up_ref, out_ref):
    low = (low_ref[...] + low_other_ref[...]).astype(BF16)
    out_ref[...] = times(low, up_ref[...]).astype(BF16)


def add_kernel(own_ref, got_ref, out_ref):
    out_ref[...] = (own_ref[...].astype(F32) + got_ref[...].astype(F32)).astype(BF16)


def total_kernel(own_ref, got_ref, out_ref, square_ref):
    add_kernel(own_ref, got_ref, out_ref)
    squares = jnp.sum(jnp.square(out_ref[...].astype(F32))).reshape(1, 1)
    square_ref[...] = jnp.broadcast_to(squares, square_ref.shape)


def clip_kernel(ceiling, square_ref, other_ref, own_ref, got_ref, up_ref, down_ref):
    squares = square_ref[:1, :1] + other_ref[:1, :1]
    factor = jnp.minimum(1.0, ceiling / (jnp.sqrt(squares) + 1e-06))
    parity = lax.axis_index("ctx") % 2
    up_step, down_step = up_ref.shape[1] // 2, down_ref.shape[1] // 2
    for index, ref in ((parity, own_ref), (1 - parity, got_ref)):
        columns = pl.ds(pl.multiple_of(index * up_step, up_step), up_step)
        up_ref[:, columns] = ref[:, :up_step].astype(F32) * factor
        columns = pl.ds(pl.multiple_of(index * down_step, down_step), down_step)
        down_ref[:, columns] = ref[:, up_step:].astype(F32) * factor


def split_model_width(
    hidden, gain, queries, key_value_weight, adapt_down, adapt_up, out_grad, doc_ids
):
    place = lax.axis_index("ctx")
    rows = hidden.shape[1]
    local_width = hidden.shape[2]
    slice_width = key_value_weight.shape[1]
    kv_count, head = key_value_weight.shape[2], key_value_weight.shape[-1]
    head_count = queries.shape[2]
    local_query = head_count * head
    rank = adapt_down.shape[1]
    kv_width = kv_count * 2 * head
    sent_width = kv_count * 5 * head // 2

    half = rows // 2
    core = lax.axis_index("tp")
    mine = lax.dynamic_slice_in_dim(hidden[0], core * half, half, 0)
    theirs = lax.dynamic_slice_in_dim(hidden[0], (1 - core) * half, half, 0)
    part = ((half, slice_width), BF16)
    slices = call(
        norm_kernel,
        [part] * 4,
        mine,
        swap(theirs, "tp", 1),
        gain,
        swap(gain, "tp", 1),
        scratch=[pltpu.VMEM((3, half, slice_width), BF16), pltpu.SemaphoreType.DMA((3,))],
        loose_outs=(1, 2, 3),
    )

    def send_a(value):
        return lax.ppermute(
            value, ("ctx", "tp"), [(2 * a + t, 2 * (a ^ (2 if t else 1)) + t) for a in range(4) for t in range(2)]
        )

    def send_b(value):
        return lax.ppermute(
            value, ("ctx", "tp"), [(2 * a + t, 2 * (a ^ (1 if t else 2)) + t) for a in range(4) for t in range(2)]
        )

    even, slice_a, slice_b, slice_c = slices
    got_a, got_b, got_c = send_a(slice_a), send_b(slice_b), swap(slice_c, "ctx", 3)
    part_flops = 2 * rows * slice_width * kv_width
    packed = ((rows, sent_width), BF16)
    summed = ((rows, kv_width), F32)
    final = ((rows + 16, kv_width), BF16)

    def step(function, *operands):
        shapes = jax.eval_shape(function, *operands)
        return lax.cond(
            place < 4,
            function,
            lambda *_: jax.tree.map(lambda x: jnp.zeros(x.shape, x.dtype), shapes),
            *operands,
        )

    def prepare(key_value_weight):
        return key_value_weight[0].reshape(slice_width, kv_width)

    weight = step(prepare, key_value_weight)

    def prepare_attention(queries, out_grad, adapt_up, doc_ids, weight):
        docs = doc_ids.astype(F32).reshape(1, rows)
        freqs = 1000000.0 ** (-jnp.arange(head // 2, dtype=F32) * 2.0 / head)
        positions = place * rows + jnp.arange(rows, dtype=jnp.int32)
        angles = positions.astype(F32)[:, None] * freqs
        cosine, sine = jnp.cos(angles), jnp.sin(angles)
        cosine = jnp.concatenate([cosine, cosine], axis=1)
        sine = jnp.concatenate([-sine, sine], axis=1)
        (query,) = call(
            query_kernel,
            [((head_count * rows, head), BF16)],
            queries[0].reshape(rows, local_query),
            cosine,
            sine,
        )
        (back_part,) = call(
            back_kernel,
            [((rows, rank), F32)],
            out_grad[0],
            adapt_up[0],
            flops=2 * rows * local_width * rank,
        )
        return docs, cosine, sine, query, back_part, swap(back_part, "tp", 1)

    docs, cosine, sine, query, back_part, back_other = step(
        prepare_attention, queries, out_grad, adapt_up, doc_ids, weight
    )
    part_0, weight_near = call(
        functools.partial(own_kernel, head),
        [summed, (weight.shape, BF16)],
        even,
        swap(even, "tp", 1),
        weight,
        flops=part_flops,
        scratch=[pltpu.VMEM((rows, slice_width), BF16), pltpu.SemaphoreType.DMA],
        loose=(2,),
    )
    got_c, part_0, docs = lax.optimization_barrier((got_c, part_0, docs))

    def far_parts(got_c, weight):
        return call(
            functools.partial(far_kernel, head),
            [packed],
            got_c,
            swap(got_c, "tp", 1),
            weight,
            flops=part_flops,
            scratch=[pltpu.VMEM((rows, slice_width), BF16)],
        )

    (sent_c,) = step(far_parts, got_c, weight)
    arrived_c = swap(sent_c, "ctx", 3)
    got_a, got_b, sent_c = lax.optimization_barrier((got_a, got_b, sent_c))
    sent_a, sent_b = call(
        functools.partial(near_kernel, head),
        [packed, packed],
        got_a,
        swap(got_a, "tp", 1),
        got_b,
        swap(got_b, "tp", 1),
        weight_near,
        flops=2 * part_flops,
        scratch=[pltpu.VMEM((2 * rows, slice_width), BF16)],
    )
    arrived_a, arrived_b = send_a(sent_a), send_b(sent_b)
    part_0, back_rows, docs, cosine, sine, staged_down = call(
        accumulate_kernel,
        [
            summed,
            ((rows, rank), BF16),
            ((1, rows), F32),
            ((rows, head), F32),
            ((rows, head), F32),
            ((rank, local_query), BF16),
        ],
        part_0,
        arrived_c,
        back_part,
        back_other,
        docs,
        cosine,
        sine,
        adapt_down[0],
    )
    arrived_a, arrived_b, part_0 = lax.optimization_barrier((arrived_a, arrived_b, part_0))
    (block_0,) = call(finish_kernel, [final], part_0, arrived_a, arrived_b, docs, cosine, sine)

    attended, low_part, down_part = call(
        functools.partial(attention_kernel, head),
        [((rows, local_query), BF16), ((rows, rank), F32), ((rank, local_query), F32)],
        query,
        block_0,
        send_a(block_0),
        send_b(block_0),
        swap(block_0, "ctx", 3),
        staged_down,
        back_rows,
        flops=16 * rows * rows * local_query,
        scratch=[
            pltpu.VMEM((rows, local_query), BF16),
            pltpu.SemaphoreType.DMA((head_count // 2,)),
        ],
        loose_outs=(0,),
    )
    low_other = swap(low_part, "tp", 1)
    piece = (rank, (local_width + local_query) // 2)
    own, sent = call(
        grads_kernel,
        [(piece, F32), (piece, BF16)],
        low_part,
        low_other,
        out_grad[0],
        down_part,
        flops=2 * rows * rank * local_width,
    )
    (adapter_rows,) = call(
        adapter_kernel,
        [((rows, local_width), BF16)],
        low_part,
        low_other,
        adapt_up[0],
        flops=2 * rows * rank * local_width,
    )
    got_sum, adapter_rows = lax.optimization_barrier((swap(sent, "ctx", 1), adapter_rows))
    (pair_sum,) = call(add_kernel, [(piece, BF16)], own, got_sum)
    total, squares = call(
        total_kernel, [(piece, BF16), ((8, 128), F32)], pair_sum, swap(pair_sum, "ctx", 2)
    )
    total_other = swap(total, "ctx", 1)
    squares = squares + swap(squares, "tp", 1)
    beside = lax.ppermute(
        squares,
        ("section", "tp"),
        [(2 * i + t, 2 * (i ^ (2 if t else 1)) + t) for i in range(4) for t in range(2)],
    )
    across = swap(squares, "section", 3)
    squares = jnp.where(core == 0, squares + across + beside, beside)
    squares = squares + swap(squares, "ctx", 1)
    ceiling = 0.5 * math.sqrt(lax.axis_size("section") * rank * (local_query + local_width) * 2)
    grad_up, grad_down = call(
        functools.partial(clip_kernel, ceiling),
        [((rank, local_width), F32), ((rank, local_query), F32)],
        squares,
        swap(squares, "tp", 1),
        total,
        total_other,
    )
    return (attended[None], adapter_rows[None], grad_down[None], grad_up[None])


def per_device(*arrays):
    if lax.axis_size("ctx") == 4 and lax.axis_size("tp") == 2 and lax.axis_size("section") == 4:
        return split_model_width(*arrays)
    return gathered_weights(*arrays)


def solution(mesh):
    return jax.shard_map(
        per_device,
        mesh=mesh,
        in_specs=(
            P("section", "ctx", "tp"),
            P("section", "tp"),
            P("section", "ctx", "tp", None),
            P("section", "ctx", "tp", None, None),
            P("section", None, "tp"),
            P("section", None, "tp"),
            P("section", "ctx", "tp"),
            P("ctx"),
        ),
        out_specs=(
            P("section", "ctx", "tp"),
            P("section", "ctx", "tp"),
            P("section", None, "tp"),
            P("section", None, "tp"),
        ),
        check_vma=False,
    )
```

```python
import functools
import math

import jax
import jax.numpy as jnp
from jax import lax
from jax.experimental import pallas as pl
from jax.experimental.pallas import tpu as pltpu
from jax.sharding import PartitionSpec as P


def rotate(head_values, positions):
    half_width = head_values.shape[-1] // 2
    freqs = 1000000.0 ** (-jnp.arange(half_width, dtype=jnp.float32) * 2.0 / head_values.shape[-1])
    angles = positions.astype(jnp.float32)[:, None] * freqs[None, :]
    cosine = jnp.cos(angles)[:, None, :]
    sine_table = jnp.sin(angles)[:, None, :]
    first_half = head_values[..., :half_width]
    second_half = head_values[..., half_width:]
    return jnp.concatenate(
        [
            first_half * cosine - second_half * sine_table,
            second_half * cosine + first_half * sine_table,
        ],
        axis=-1,
    )


def gathered_weights(hidden, gain, queries, key_value_weight, adapt_down, adapt_up, out_grad, doc_ids):
    tp_count = lax.axis_size("tp")
    row_count = hidden.shape[1]
    local_width = hidden.shape[2]
    head_dim = key_value_weight.shape[-1]
    kv_count = key_value_weight.shape[2]
    head_count = queries.shape[2]
    group_size = head_count // kv_count
    local_query = head_count * head_dim
    rank_size = adapt_down.shape[1]
    key_block = 1024
    full_rows, full_gain = (
        lax.all_gather(hidden, "tp", axis=2, tiled=True),
        lax.all_gather(gain, "tp", axis=1, tiled=True),
    )
    widened = full_rows[0].astype(jnp.float32)
    normalized_rows = (
        widened
        * lax.rsqrt(jnp.mean(widened * widened, axis=1, keepdims=True) + 1e-06)
        * full_gain[0].astype(jnp.float32)
    ).astype(jnp.bfloat16)
    kv_local = key_value_weight.reshape(1, key_value_weight.shape[1], kv_count * 2 * head_dim)
    keyval_raw = jnp.dot(
        normalized_rows,
        lax.all_gather(kv_local, "ctx", axis=1, tiled=True)[0],
        preferred_element_type=jnp.float32,
    )
    positions = lax.axis_index("ctx") * row_count + jnp.arange(row_count, dtype=jnp.int32)
    key_value_rows = keyval_raw.reshape(row_count, kv_count, 2, head_dim)
    rotated_keys = rotate(key_value_rows[:, :, 0], positions).astype(jnp.bfloat16)
    value_rows = key_value_rows[:, :, 1].astype(jnp.bfloat16)
    rotated_query = rotate(queries[0].astype(jnp.float32), positions).astype(jnp.bfloat16)
    stacked = (
        rotated_query.reshape(row_count, kv_count, group_size, head_dim)
        .transpose(1, 2, 0, 3)
        .reshape(kv_count, group_size * row_count, head_dim)
    )
    query_pos = jnp.tile(positions, group_size)
    query_doc = jnp.tile(doc_ids, group_size).astype(jnp.float32)
    score_scale = head_dim ** (-0.5)
    start_state = (
        jnp.full((kv_count, group_size * row_count), -1e30, jnp.float32),
        jnp.zeros((kv_count, group_size * row_count), jnp.float32),
        jnp.zeros((kv_count, group_size * row_count, head_dim), jnp.float32),
    )
    carried = start_state
    first_row = jnp.int32(0)
    piece_keys = lax.all_gather(rotated_keys, "ctx", axis=0, tiled=True)
    piece_values = lax.all_gather(value_rows, "ctx", axis=0, tiled=True)
    piece_docs = lax.all_gather(doc_ids.astype(jnp.bfloat16), "ctx", axis=0, tiled=True)
    key_total = piece_keys.shape[0]
    for block_start in range(0, key_total, key_block):
        block_stop = min(key_total, block_start + key_block)
        block_keys = piece_keys[block_start:block_stop]
        block_values = piece_values[block_start:block_stop]
        key_pos = first_row + block_start + jnp.arange(block_keys.shape[0], dtype=jnp.int32)
        key_doc = piece_docs[block_start:block_stop].astype(jnp.float32)
        running_top, running_sum, running_acc = carried
        scores = (
            jnp.einsum("gqd,kgd->gqk", stacked, block_keys, preferred_element_type=jnp.float32)
            * score_scale
        )
        allowed = (
            (key_pos[None, :] <= query_pos[:, None]) & (key_doc[None, :] == query_doc[:, None])
        )[None]
        scores = jnp.where(allowed, scores, -1e30)
        new_top = jnp.maximum(running_top, jnp.max(scores, axis=2))
        weights = jnp.where(allowed, jnp.exp(scores - new_top[:, :, None]), 0.0)
        shrink = jnp.exp(running_top - new_top)
        new_acc = running_acc * shrink[:, :, None] + jnp.einsum(
            "gqk,kgd->gqd",
            weights.astype(jnp.bfloat16),
            block_values,
            preferred_element_type=jnp.float32,
        )
        carried = (new_top, running_sum * shrink + jnp.sum(weights, axis=2), new_acc)
    final_top, final_sum, final_acc = carried
    attended = (
        (final_acc / final_sum[:, :, None])
        .reshape(kv_count, group_size, row_count, head_dim)
        .transpose(2, 0, 1, 3)
        .reshape(row_count, local_query)
        .astype(jnp.bfloat16)
    )
    low_part = jnp.dot(attended, adapt_down[0].T, preferred_element_type=jnp.float32)
    back_part = jnp.dot(out_grad[0], adapt_up[0].T, preferred_element_type=jnp.float32)
    low_sum, back_sum = lax.psum((low_part, back_part), "tp")
    low_rows = low_sum.astype(jnp.bfloat16)
    back_rows = back_sum.astype(jnp.bfloat16)
    adapter_rows = jnp.dot(low_rows, adapt_up[0], preferred_element_type=jnp.float32).astype(
        jnp.bfloat16
    )
    up_part = jnp.dot(low_rows.T, out_grad[0], preferred_element_type=jnp.float32)
    down_part = jnp.dot(back_rows.T, attended, preferred_element_type=jnp.float32)
    ceiling = 0.5 * math.sqrt(
        lax.axis_size("section") * rank_size * (local_query + local_width) * tp_count
    )
    up_total, down_total = (
        lax.psum(up_part.astype(jnp.bfloat16), "ctx").astype(jnp.float32),
        lax.psum(down_part.astype(jnp.bfloat16), "ctx").astype(jnp.float32),
    )
    local_squares = jnp.sum(up_total * up_total) + jnp.sum(down_total * down_total)
    squares = lax.psum(local_squares, ("section", "tp"))
    factor = jnp.minimum(1.0, ceiling / (jnp.sqrt(squares) + 1e-06))
    grad_up = up_total * factor
    grad_down = down_total * factor
    return (attended[None], adapter_rows[None], grad_down[None], grad_up[None])


F32, BF16 = jnp.float32, jnp.bfloat16
VMEM = pl.BlockSpec(memory_space=pltpu.VMEM)
ANYWHERE = pl.BlockSpec(memory_space=pl.ANY)
LIMIT = 16 * 1024 * 1024
LEVELS = (5, 5, 5, 4)


def swap(value, axis, distance):
    count = lax.axis_size(axis)
    return lax.ppermute(value, axis, [(i, i ^ distance) for i in range(count)])


def call(kernel, outs, *operands, flops=0, scratch=(), loose=(), loose_outs=()):
    shapes = [jax.ShapeDtypeStruct(shape, dtype) for shape, dtype in outs]
    moved = sum(math.prod(x.shape) * x.dtype.itemsize for x in (*operands, *shapes))
    return pl.pallas_call(
        kernel,
        out_shape=shapes,
        in_specs=[ANYWHERE if i in loose else VMEM for i in range(len(operands))],
        out_specs=[ANYWHERE if i in loose_outs else VMEM for i in range(len(shapes))],
        scratch_shapes=scratch,
        compiler_params=pltpu.CompilerParams(vmem_limit_bytes=LIMIT),
        cost_estimate=pl.CostEstimate(flops=flops, bytes_accessed=moved, transcendentals=0),
    )(*operands)


def times(left, right):
    return lax.dot_general(left, right, (((1,), (0,)), ((), ())), preferred_element_type=F32)


def times_transposed(left, right):
    return lax.dot_general(left, right, (((1,), (1,)), ((), ())), preferred_element_type=F32)


def transposed_times(left, right):
    return lax.dot_general(left, right, (((0,), (0,)), ((), ())), preferred_element_type=F32)


def distances():
    core = lax.axis_index("tp")
    return 0, jnp.where(core == 0, 1, 2), jnp.where(core == 0, 2, 1), 3


def norm_kernel(mine_ref, other_ref, gain_ref, gain_other_ref, *refs):
    outs, (held_ref, written) = refs[:4], refs[4:]
    width = outs[0].shape[1]
    place, core = lax.axis_index("ctx"), lax.axis_index("tp")
    mine, other = mine_ref[...].astype(F32), other_ref[...].astype(F32)
    squares = [jnp.sum(rows * rows, axis=1, keepdims=True) for rows in (mine, other)]
    scale = lax.rsqrt((squares[0] + squares[1]) / (4 * width) + 1e-06)
    copies = []
    for index in (3, 1, 2, 0):
        chip = place ^ distances()[index]
        columns = pl.ds(pl.multiple_of(chip % 2 * width, width), width)
        slot = outs[0] if index == 0 else held_ref.at[index - 1]

        def write(rows_ref, weights_ref, slot=slot, columns=columns):
            rows = rows_ref[:, columns].astype(F32) * scale
            slot[...] = (rows * weights_ref[:, columns].astype(F32)).astype(BF16)

        pl.when(chip // 2 == core)(functools.partial(write, mine_ref, gain_ref))
        pl.when(chip // 2 != core)(functools.partial(write, other_ref, gain_other_ref))
        if index:
            copies.append(pltpu.make_async_copy(slot, outs[index], written.at[index - 1]))
            copies[-1].start()
    for copy in copies:
        copy.wait()


def join_rows(mine_ref, other_ref, out_ref):
    count = mine_ref.shape[0]
    core = lax.axis_index("tp")
    out_ref[pl.ds(pl.multiple_of(core * count, count), count)] = mine_ref[...]
    out_ref[pl.ds(pl.multiple_of((1 - core) * count, count), count)] = other_ref[...]


def split_heads(value, head):
    count = value.shape[1] // (2 * head)
    pieces = [value[:, i * head : (i + 1) * head] for i in range(2 * count)]
    return jnp.concatenate(pieces[0::2], axis=1), jnp.concatenate(pieces[1::2], axis=1)


def pack(value, out_ref, head):
    keys, values = split_heads(value, head)
    store_packed(keys, values, out_ref)


def store_packed(keys, values, out_ref):
    rows, width = keys.shape
    high = keys.astype(BF16)
    wide = high.astype(F32)
    size = jnp.abs(wide)
    part = (keys - wide) * 256.0 / jnp.where(size > 0, size, 1.0)
    out_ref[:rows, :width] = high
    out_ref[:rows, width:] = values.astype(BF16)
    count = rows // len(LEVELS)
    code, weight = -250.0, 1.0
    for index, levels in enumerate(LEVELS):
        level = jnp.floor((part[index * count : (index + 1) * count] + 1.0) * (levels / 2))
        code = code + jnp.clip(level, 0.0, levels - 1.0) * weight
        weight *= levels
    code = jnp.concatenate([code[: count // 2], code[count // 2 :]], axis=1)
    out_ref[rows:] = code.astype(BF16)


def unpack(ref, rows):
    width = ref.shape[1] // 2
    wide = ref[:rows, :width].astype(F32)
    code = ref[rows:].astype(F32) + 250.0
    code = jnp.concatenate([code[:, :width], code[:, width:]], axis=0)
    parts, weight = [], math.prod(LEVELS)
    for levels in reversed(LEVELS):
        weight /= levels
        level = jnp.floor((code + 0.5) / weight)
        code = code - level * weight
        parts.append((level * 2.0 + 1.0) / levels - 1.0)
    part = jnp.concatenate(parts[::-1], axis=0)
    return wide + jnp.abs(wide) * part * (1.0 / 256.0), ref[:rows, width:].astype(F32)


def store_docs(docs, out_ref):
    rows = docs.shape[1]
    out_ref[rows:, :rows] = jnp.broadcast_to(docs, (16, rows)).astype(BF16)


def load_docs(ref):
    return ref[-16:, : ref.shape[0] - 16].astype(F32)[:1]


def own_kernel(
    head, even_ref, even_other_ref, weight_ref, own_ref, weight_out_ref, rows_ref, arrived
):
    copy = pltpu.make_async_copy(weight_ref, weight_out_ref, arrived)
    copy.start()
    join_rows(even_ref, even_other_ref, rows_ref)
    copy.wait()
    product = times(rows_ref[...], weight_out_ref[...])
    own_ref[...] = jnp.concatenate(split_heads(product, head), axis=1)


def far_kernel(head, got_ref, got_other_ref, weight_ref, sent_ref, rows_ref):
    join_rows(got_ref, got_other_ref, rows_ref)
    pack(times(rows_ref[...], weight_ref[...]), sent_ref, head)


def near_kernel(
    head,
    got_a_ref,
    got_a_other_ref,
    got_b_ref,
    got_b_other_ref,
    weight_ref,
    sent_a_ref,
    sent_b_ref,
    rows_ref,
):
    count = rows_ref.shape[0] // 2
    join_rows(got_a_ref, got_b_other_ref, rows_ref.at[:count])
    join_rows(got_b_ref, got_a_other_ref, rows_ref.at[count:])
    product = times(rows_ref[...], weight_ref[...])
    pack(product[:count], sent_a_ref, head)
    pack(product[count:], sent_b_ref, head)


def turn(value, cosine, sine):
    head = cosine.shape[1]
    pieces = []
    for i in range(value.shape[1] // head):
        piece = value[:, i * head : (i + 1) * head]
        pieces.append(piece * cosine + pltpu.roll(piece, head // 2, 1) * sine)
    return jnp.concatenate(pieces, axis=1)


def query_kernel(query_ref, cosine_ref, sine_ref, out_ref):
    rows, head = cosine_ref.shape
    for index in range(query_ref.shape[1] // head):
        piece = query_ref[:, index * head : (index + 1) * head].astype(F32)
        out_ref[index * rows : (index + 1) * rows] = turn(
            piece, cosine_ref[...], sine_ref[...]
        ).astype(BF16)


def accumulate_kernel(own_ref, got_ref, back_ref, back_other_ref, *refs):
    count = len(refs) // 2
    out_ref, back_out_ref = refs[count - 1 : count + 1]
    keys, values = unpack(got_ref, own_ref.shape[0])
    width = keys.shape[1]
    out_ref[:, :width] = own_ref[:, :width] + keys
    out_ref[:, width:] = own_ref[:, width:] + values
    back_out_ref[...] = (back_ref[...] + back_other_ref[...]).astype(BF16)
    for ref, copy_ref in zip(refs[: count - 1], refs[count + 1 :]):
        copy_ref[...] = ref[...]


def finish_kernel(own_ref, got_a_ref, got_b_ref, docs_ref, cosine_ref, sine_ref, out_ref):
    rows = own_ref.shape[0]
    width = own_ref.shape[1] // 2
    keys, values = own_ref[:, :width], own_ref[:, width:]
    for ref in (got_a_ref, got_b_ref):
        more_keys, more_values = unpack(ref, rows)
        keys, values = keys + more_keys, values + more_values
    out_ref[:rows, :width] = turn(keys, cosine_ref[...], sine_ref[...]).astype(BF16)
    out_ref[:rows, width:] = values.astype(BF16)
    store_docs(docs_ref[...], out_ref)


def allowed_pairs(own_docs, key_docs, distance):
    rows = own_docs.shape[1]
    place = lax.axis_index("ctx")
    query_docs = jnp.broadcast_to(own_docs, (rows, rows)).T
    query_at = place * rows + lax.broadcasted_iota(jnp.int32, (rows, rows), 0)
    key_at = (place ^ distance) * rows + lax.broadcasted_iota(jnp.int32, (rows, rows), 1)
    return (key_at <= query_at) & (key_docs == query_docs)


def attention_kernel(
    head,
    query_ref,
    block_0_ref,
    block_a_ref,
    block_b_ref,
    block_c_ref,
    down_ref,
    back_ref,
    out_ref,
    low_ref,
    grad_ref,
    mixed_ref,
    written,
):
    rows = block_0_ref.shape[0] - 16
    width = block_0_ref.shape[1] // 2
    blocks = (block_0_ref, block_a_ref, block_b_ref, block_c_ref)
    keys = jnp.concatenate([ref[:rows, :width] for ref in blocks], axis=0)
    values = jnp.concatenate([ref[:rows, width:] for ref in blocks], axis=0)
    own_docs = load_docs(block_0_ref)
    allowed = jnp.concatenate(
        [allowed_pairs(own_docs, load_docs(ref), d) for d, ref in zip(distances(), blocks)], axis=1
    )
    scale = head ** (-0.5) * math.log2(math.e)
    ones = jnp.ones((len(blocks) * rows, head), BF16)
    groups = width // head
    pairs = query_ref.shape[0] // (2 * rows)
    copies = []
    for pair in range(pairs):
        shared = slice(pair * groups // pairs * head, (pair * groups // pairs + 1) * head)
        scores = times_transposed(
            query_ref[2 * pair * rows : 2 * (pair + 1) * rows], keys[:, shared]
        ).reshape(2, rows, keys.shape[0])
        scores = jnp.where(allowed[None], scores, -1e30).reshape(2 * rows, keys.shape[0])
        weights = jnp.exp2((scores - jnp.max(scores, axis=1, keepdims=True)) * scale)
        mixed = times(
            weights.astype(BF16), jnp.concatenate([values[:, shared], ones], axis=1)
        )
        mixed = (mixed[:, :head] / mixed[:, head:]).astype(BF16)
        columns = slice(2 * pair * head, 2 * (pair + 1) * head)
        mixed_ref[:, columns] = jnp.concatenate([mixed[:rows], mixed[rows:]], axis=1)
        copies.append(
            pltpu.make_async_copy(
                mixed_ref.at[:, columns], out_ref.at[:, columns], written.at[pair]
            )
        )
        copies[-1].start()
    attended = mixed_ref[...]
    low_ref[...] = times_transposed(attended, down_ref[...])
    grad_ref[...] = transposed_times(back_ref[...], attended)
    for copy in copies:
        copy.wait()


def back_kernel(grad_ref, up_ref, out_ref):
    out_ref[...] = times_transposed(grad_ref[...], up_ref[...])


def grads_kernel(low_ref, low_other_ref, grad_ref, down_ref, own_ref, sent_ref):
    low = (low_ref[...] + low_other_ref[...]).astype(BF16)
    parity = lax.axis_index("ctx") % 2
    up_step, down_step = grad_ref.shape[1] // 2, down_ref.shape[1] // 2
    for index, out in ((1 - parity, sent_ref), (parity, own_ref)):
        columns = pl.ds(pl.multiple_of(index * up_step, up_step), up_step)
        out[:, :up_step] = transposed_times(low, grad_ref[:, columns]).astype(out.dtype)
        columns = pl.ds(pl.multiple_of(index * down_step, down_step), down_step)
        out[:, up_step:] = down_ref[:, columns].astype(out.dtype)


def adapter_kernel(low_ref, low_other_ref, up_ref, out_ref):
    low = (low_ref[...] + low_other_ref[...]).astype(BF16)
    out_ref[...] = times(low, up_ref[...]).astype(BF16)


def add_kernel(own_ref, got_ref, out_ref):
    out_ref[...] = (own_ref[...].astype(F32) + got_ref[...].astype(F32)).astype(BF16)


def total_kernel(own_ref, got_ref, out_ref, square_ref):
    add_kernel(own_ref, got_ref, out_ref)
    squares = jnp.sum(jnp.square(out_ref[...].astype(F32))).reshape(1, 1)
    square_ref[...] = jnp.broadcast_to(squares, square_ref.shape)


def clip_kernel(ceiling, square_ref, other_ref, own_ref, got_ref, up_ref, down_ref):
    squares = square_ref[:1, :1] + other_ref[:1, :1]
    factor = jnp.minimum(1.0, ceiling / (jnp.sqrt(squares) + 1e-06))
    parity = lax.axis_index("ctx") % 2
    up_step, down_step = up_ref.shape[1] // 2, down_ref.shape[1] // 2
    for index, ref in ((parity, own_ref), (1 - parity, got_ref)):
        columns = pl.ds(pl.multiple_of(index * up_step, up_step), up_step)
        up_ref[:, columns] = ref[:, :up_step].astype(F32) * factor
        columns = pl.ds(pl.multiple_of(index * down_step, down_step), down_step)
        down_ref[:, columns] = ref[:, up_step:].astype(F32) * factor


def split_model_width(
    hidden, gain, queries, key_value_weight, adapt_down, adapt_up, out_grad, doc_ids
):
    place = lax.axis_index("ctx")
    rows = hidden.shape[1]
    local_width = hidden.shape[2]
    slice_width = key_value_weight.shape[1]
    kv_count, head = key_value_weight.shape[2], key_value_weight.shape[-1]
    head_count = queries.shape[2]
    local_query = head_count * head
    rank = adapt_down.shape[1]
    kv_width = kv_count * 2 * head

    half = rows // 2
    core = lax.axis_index("tp")
    mine = lax.dynamic_slice_in_dim(hidden[0], core * half, half, 0)
    theirs = lax.dynamic_slice_in_dim(hidden[0], (1 - core) * half, half, 0)
    part = ((half, slice_width), BF16)
    slices = call(
        norm_kernel,
        [part] * 4,
        mine,
        swap(theirs, "tp", 1),
        gain,
        swap(gain, "tp", 1),
        scratch=[pltpu.VMEM((3, half, slice_width), BF16), pltpu.SemaphoreType.DMA((3,))],
        loose_outs=(1, 2, 3),
    )

    def send_a(value):
        return lax.ppermute(
            value, ("ctx", "tp"), [(2 * a + t, 2 * (a ^ (2 if t else 1)) + t) for a in range(4) for t in range(2)]
        )

    def send_b(value):
        return lax.ppermute(
            value, ("ctx", "tp"), [(2 * a + t, 2 * (a ^ (1 if t else 2)) + t) for a in range(4) for t in range(2)]
        )

    even, slice_a, slice_b, slice_c = slices
    got_a, got_b, got_c = send_a(slice_a), send_b(slice_b), swap(slice_c, "ctx", 3)
    part_flops = 2 * rows * slice_width * kv_width
    packed = ((rows + rows // 8, kv_width), BF16)
    summed = ((rows, kv_width), F32)
    final = ((rows + 16, kv_width), BF16)

    def step(function, *operands):
        shapes = jax.eval_shape(function, *operands)
        return lax.cond(
            place < 4,
            function,
            lambda *_: jax.tree.map(lambda x: jnp.zeros(x.shape, x.dtype), shapes),
            *operands,
        )

    def prepare(key_value_weight):
        return key_value_weight[0].reshape(slice_width, kv_width)

    weight = step(prepare, key_value_weight)

    def prepare_attention(queries, out_grad, adapt_up, doc_ids, weight):
        docs = doc_ids.astype(F32).reshape(1, rows)
        freqs = 1000000.0 ** (-jnp.arange(head // 2, dtype=F32) * 2.0 / head)
        positions = place * rows + jnp.arange(rows, dtype=jnp.int32)
        angles = positions.astype(F32)[:, None] * freqs
        cosine, sine = jnp.cos(angles), jnp.sin(angles)
        cosine = jnp.concatenate([cosine, cosine], axis=1)
        sine = jnp.concatenate([-sine, sine], axis=1)
        (query,) = call(
            query_kernel,
            [((head_count * rows, head), BF16)],
            queries[0].reshape(rows, local_query),
            cosine,
            sine,
        )
        (back_part,) = call(
            back_kernel,
            [((rows, rank), F32)],
            out_grad[0],
            adapt_up[0],
            flops=2 * rows * local_width * rank,
        )
        return docs, cosine, sine, query, back_part, swap(back_part, "tp", 1)

    docs, cosine, sine, query, back_part, back_other = step(
        prepare_attention, queries, out_grad, adapt_up, doc_ids, weight
    )
    part_0, weight_near = call(
        functools.partial(own_kernel, head),
        [summed, (weight.shape, BF16)],
        even,
        swap(even, "tp", 1),
        weight,
        flops=part_flops,
        scratch=[pltpu.VMEM((rows, slice_width), BF16), pltpu.SemaphoreType.DMA],
        loose=(2,),
    )
    got_c, part_0, docs = lax.optimization_barrier((got_c, part_0, docs))

    def far_parts(got_c, weight):
        return call(
            functools.partial(far_kernel, head),
            [packed],
            got_c,
            swap(got_c, "tp", 1),
            weight,
            flops=part_flops,
            scratch=[pltpu.VMEM((rows, slice_width), BF16)],
        )

    (sent_c,) = step(far_parts, got_c, weight)
    arrived_c = swap(sent_c, "ctx", 3)
    got_a, got_b, sent_c = lax.optimization_barrier((got_a, got_b, sent_c))
    sent_a, sent_b = call(
        functools.partial(near_kernel, head),
        [packed, packed],
        got_a,
        swap(got_a, "tp", 1),
        got_b,
        swap(got_b, "tp", 1),
        weight_near,
        flops=2 * part_flops,
        scratch=[pltpu.VMEM((2 * rows, slice_width), BF16)],
    )
    arrived_a, arrived_b = send_a(sent_a), send_b(sent_b)
    part_0, back_rows, docs, cosine, sine, staged_down = call(
        accumulate_kernel,
        [
            summed,
            ((rows, rank), BF16),
            ((1, rows), F32),
            ((rows, head), F32),
            ((rows, head), F32),
            ((rank, local_query), BF16),
        ],
        part_0,
        arrived_c,
        back_part,
        back_other,
        docs,
        cosine,
        sine,
        adapt_down[0],
    )
    arrived_a, arrived_b, part_0 = lax.optimization_barrier((arrived_a, arrived_b, part_0))
    (block_0,) = call(finish_kernel, [final], part_0, arrived_a, arrived_b, docs, cosine, sine)

    attended, low_part, down_part = call(
        functools.partial(attention_kernel, head),
        [((rows, local_query), BF16), ((rows, rank), F32), ((rank, local_query), F32)],
        query,
        block_0,
        send_a(block_0),
        send_b(block_0),
        swap(block_0, "ctx", 3),
        staged_down,
        back_rows,
        flops=16 * rows * rows * local_query,
        scratch=[
            pltpu.VMEM((rows, local_query), BF16),
            pltpu.SemaphoreType.DMA((head_count // 2,)),
        ],
        loose_outs=(0,),
    )
    low_other = swap(low_part, "tp", 1)
    piece = (rank, (local_width + local_query) // 2)
    own, sent = call(
        grads_kernel,
        [(piece, F32), (piece, BF16)],
        low_part,
        low_other,
        out_grad[0],
        down_part,
        flops=2 * rows * rank * local_width,
    )
    (adapter_rows,) = call(
        adapter_kernel,
        [((rows, local_width), BF16)],
        low_part,
        low_other,
        adapt_up[0],
        flops=2 * rows * rank * local_width,
    )
    got_sum, adapter_rows = lax.optimization_barrier((swap(sent, "ctx", 1), adapter_rows))
    (pair_sum,) = call(add_kernel, [(piece, BF16)], own, got_sum)
    total, squares = call(
        total_kernel, [(piece, BF16), ((8, 128), F32)], pair_sum, swap(pair_sum, "ctx", 2)
    )
    total_other = swap(total, "ctx", 1)
    squares = squares + swap(squares, "tp", 1)
    beside = lax.ppermute(
        squares,
        ("section", "tp"),
        [(2 * i + t, 2 * (i ^ (2 if t else 1)) + t) for i in range(4) for t in range(2)],
    )
    across = swap(squares, "section", 3)
    squares = jnp.where(core == 0, squares + across + beside, beside)
    squares = squares + swap(squares, "ctx", 1)
    ceiling = 0.5 * math.sqrt(lax.axis_size("section") * rank * (local_query + local_width) * 2)
    grad_up, grad_down = call(
        functools.partial(clip_kernel, ceiling),
        [((rank, local_width), F32), ((rank, local_query), F32)],
        squares,
        swap(squares, "tp", 1),
        total,
        total_other,
    )
    return (attended[None], adapter_rows[None], grad_down[None], grad_up[None])


def per_device(*arrays):
    if lax.axis_size("ctx") == 4 and lax.axis_size("tp") == 2 and lax.axis_size("section") == 4:
        return split_model_width(*arrays)
    return gathered_weights(*arrays)


def solution(mesh):
    return jax.shard_map(
        per_device,
        mesh=mesh,
        in_specs=(
            P("section", "ctx", "tp"),
            P("section", "tp"),
            P("section", "ctx", "tp", None),
            P("section", "ctx", "tp", None, None),
            P("section", None, "tp"),
            P("section", None, "tp"),
            P("section", "ctx", "tp"),
            P("ctx"),
        ),
        out_specs=(
            P("section", "ctx", "tp"),
            P("section", "ctx", "tp"),
            P("section", None, "tp"),
            P("section", None, "tp"),
        ),
        check_vma=False,
    )
```

```python
import functools
import math

import jax
import jax.numpy as jnp
from jax import lax
from jax.experimental import pallas as pl
from jax.experimental.pallas import tpu as pltpu
from jax.sharding import PartitionSpec as P


def rotate(head_values, positions):
    half_width = head_values.shape[-1] // 2
    freqs = 1000000.0 ** (-jnp.arange(half_width, dtype=jnp.float32) * 2.0 / head_values.shape[-1])
    angles = positions.astype(jnp.float32)[:, None] * freqs[None, :]
    cosine = jnp.cos(angles)[:, None, :]
    sine_table = jnp.sin(angles)[:, None, :]
    first_half = head_values[..., :half_width]
    second_half = head_values[..., half_width:]
    return jnp.concatenate(
        [
            first_half * cosine - second_half * sine_table,
            second_half * cosine + first_half * sine_table,
        ],
        axis=-1,
    )


def gathered_weights(hidden, gain, queries, key_value_weight, adapt_down, adapt_up, out_grad, doc_ids):
    tp_count = lax.axis_size("tp")
    row_count = hidden.shape[1]
    local_width = hidden.shape[2]
    head_dim = key_value_weight.shape[-1]
    kv_count = key_value_weight.shape[2]
    head_count = queries.shape[2]
    group_size = head_count // kv_count
    local_query = head_count * head_dim
    rank_size = adapt_down.shape[1]
    key_block = 1024
    full_rows, full_gain = (
        lax.all_gather(hidden, "tp", axis=2, tiled=True),
        lax.all_gather(gain, "tp", axis=1, tiled=True),
    )
    widened = full_rows[0].astype(jnp.float32)
    normalized_rows = (
        widened
        * lax.rsqrt(jnp.mean(widened * widened, axis=1, keepdims=True) + 1e-06)
        * full_gain[0].astype(jnp.float32)
    ).astype(jnp.bfloat16)
    kv_local = key_value_weight.reshape(1, key_value_weight.shape[1], kv_count * 2 * head_dim)
    keyval_raw = jnp.dot(
        normalized_rows,
        lax.all_gather(kv_local, "ctx", axis=1, tiled=True)[0],
        preferred_element_type=jnp.float32,
    )
    positions = lax.axis_index("ctx") * row_count + jnp.arange(row_count, dtype=jnp.int32)
    key_value_rows = keyval_raw.reshape(row_count, kv_count, 2, head_dim)
    rotated_keys = rotate(key_value_rows[:, :, 0], positions).astype(jnp.bfloat16)
    value_rows = key_value_rows[:, :, 1].astype(jnp.bfloat16)
    rotated_query = rotate(queries[0].astype(jnp.float32), positions).astype(jnp.bfloat16)
    stacked = (
        rotated_query.reshape(row_count, kv_count, group_size, head_dim)
        .transpose(1, 2, 0, 3)
        .reshape(kv_count, group_size * row_count, head_dim)
    )
    query_pos = jnp.tile(positions, group_size)
    query_doc = jnp.tile(doc_ids, group_size).astype(jnp.float32)
    score_scale = head_dim ** (-0.5)
    start_state = (
        jnp.full((kv_count, group_size * row_count), -1e30, jnp.float32),
        jnp.zeros((kv_count, group_size * row_count), jnp.float32),
        jnp.zeros((kv_count, group_size * row_count, head_dim), jnp.float32),
    )
    carried = start_state
    first_row = jnp.int32(0)
    piece_keys = lax.all_gather(rotated_keys, "ctx", axis=0, tiled=True)
    piece_values = lax.all_gather(value_rows, "ctx", axis=0, tiled=True)
    piece_docs = lax.all_gather(doc_ids.astype(jnp.bfloat16), "ctx", axis=0, tiled=True)
    key_total = piece_keys.shape[0]
    for block_start in range(0, key_total, key_block):
        block_stop = min(key_total, block_start + key_block)
        block_keys = piece_keys[block_start:block_stop]
        block_values = piece_values[block_start:block_stop]
        key_pos = first_row + block_start + jnp.arange(block_keys.shape[0], dtype=jnp.int32)
        key_doc = piece_docs[block_start:block_stop].astype(jnp.float32)
        running_top, running_sum, running_acc = carried
        scores = (
            jnp.einsum("gqd,kgd->gqk", stacked, block_keys, preferred_element_type=jnp.float32)
            * score_scale
        )
        allowed = (
            (key_pos[None, :] <= query_pos[:, None]) & (key_doc[None, :] == query_doc[:, None])
        )[None]
        scores = jnp.where(allowed, scores, -1e30)
        new_top = jnp.maximum(running_top, jnp.max(scores, axis=2))
        weights = jnp.where(allowed, jnp.exp(scores - new_top[:, :, None]), 0.0)
        shrink = jnp.exp(running_top - new_top)
        new_acc = running_acc * shrink[:, :, None] + jnp.einsum(
            "gqk,kgd->gqd",
            weights.astype(jnp.bfloat16),
            block_values,
            preferred_element_type=jnp.float32,
        )
        carried = (new_top, running_sum * shrink + jnp.sum(weights, axis=2), new_acc)
    final_top, final_sum, final_acc = carried
    attended = (
        (final_acc / final_sum[:, :, None])
        .reshape(kv_count, group_size, row_count, head_dim)
        .transpose(2, 0, 1, 3)
        .reshape(row_count, local_query)
        .astype(jnp.bfloat16)
    )
    low_part = jnp.dot(attended, adapt_down[0].T, preferred_element_type=jnp.float32)
    back_part = jnp.dot(out_grad[0], adapt_up[0].T, preferred_element_type=jnp.float32)
    low_sum, back_sum = lax.psum((low_part, back_part), "tp")
    low_rows = low_sum.astype(jnp.bfloat16)
    back_rows = back_sum.astype(jnp.bfloat16)
    adapter_rows = jnp.dot(low_rows, adapt_up[0], preferred_element_type=jnp.float32).astype(
        jnp.bfloat16
    )
    up_part = jnp.dot(low_rows.T, out_grad[0], preferred_element_type=jnp.float32)
    down_part = jnp.dot(back_rows.T, attended, preferred_element_type=jnp.float32)
    ceiling = 0.5 * math.sqrt(
        lax.axis_size("section") * rank_size * (local_query + local_width) * tp_count
    )
    up_total, down_total = (
        lax.psum(up_part.astype(jnp.bfloat16), "ctx").astype(jnp.float32),
        lax.psum(down_part.astype(jnp.bfloat16), "ctx").astype(jnp.float32),
    )
    local_squares = jnp.sum(up_total * up_total) + jnp.sum(down_total * down_total)
    squares = lax.psum(local_squares, ("section", "tp"))
    factor = jnp.minimum(1.0, ceiling / (jnp.sqrt(squares) + 1e-06))
    grad_up = up_total * factor
    grad_down = down_total * factor
    return (attended[None], adapter_rows[None], grad_down[None], grad_up[None])


F32, BF16 = jnp.float32, jnp.bfloat16
VMEM = pl.BlockSpec(memory_space=pltpu.VMEM)
ANYWHERE = pl.BlockSpec(memory_space=pl.ANY)
LIMIT = 16 * 1024 * 1024
LEVELS = (5, 5, 5, 4)


def swap(value, axis, distance):
    count = lax.axis_size(axis)
    return lax.ppermute(value, axis, [(i, i ^ distance) for i in range(count)])


def call(kernel, outs, *operands, flops=0, scratch=(), loose=(), loose_outs=()):
    shapes = [jax.ShapeDtypeStruct(shape, dtype) for shape, dtype in outs]
    moved = sum(math.prod(x.shape) * x.dtype.itemsize for x in (*operands, *shapes))
    return pl.pallas_call(
        kernel,
        out_shape=shapes,
        in_specs=[ANYWHERE if i in loose else VMEM for i in range(len(operands))],
        out_specs=[ANYWHERE if i in loose_outs else VMEM for i in range(len(shapes))],
        scratch_shapes=scratch,
        compiler_params=pltpu.CompilerParams(vmem_limit_bytes=LIMIT),
        cost_estimate=pl.CostEstimate(flops=flops, bytes_accessed=moved, transcendentals=0),
    )(*operands)


def times(left, right):
    return lax.dot_general(left, right, (((1,), (0,)), ((), ())), preferred_element_type=F32)


def times_transposed(left, right):
    return lax.dot_general(left, right, (((1,), (1,)), ((), ())), preferred_element_type=F32)


def transposed_times(left, right):
    return lax.dot_general(left, right, (((0,), (0,)), ((), ())), preferred_element_type=F32)


def distances():
    core = lax.axis_index("tp")
    return 0, jnp.where(core == 0, 1, 2), jnp.where(core == 0, 2, 1), 3


def norm_kernel(mine_ref, other_ref, gain_ref, gain_other_ref, *refs):
    outs, (held_ref, written) = refs[:4], refs[4:]
    width = outs[0].shape[1]
    place, core = lax.axis_index("ctx"), lax.axis_index("tp")
    mine, other = mine_ref[...].astype(F32), other_ref[...].astype(F32)
    squares = [jnp.sum(rows * rows, axis=1, keepdims=True) for rows in (mine, other)]
    scale = lax.rsqrt((squares[0] + squares[1]) / (4 * width) + 1e-06)
    copies = []
    for index in (3, 1, 2, 0):
        chip = place ^ distances()[index]
        columns = pl.ds(pl.multiple_of(chip % 2 * width, width), width)
        slot = outs[0] if index == 0 else held_ref.at[index - 1]

        def write(rows_ref, weights_ref, slot=slot, columns=columns):
            rows = rows_ref[:, columns].astype(F32) * scale
            slot[...] = (rows * weights_ref[:, columns].astype(F32)).astype(BF16)

        pl.when(chip // 2 == core)(functools.partial(write, mine_ref, gain_ref))
        pl.when(chip // 2 != core)(functools.partial(write, other_ref, gain_other_ref))
        if index:
            copies.append(pltpu.make_async_copy(slot, outs[index], written.at[index - 1]))
            copies[-1].start()
    for copy in copies:
        copy.wait()


def join_rows(mine_ref, other_ref, out_ref):
    count = mine_ref.shape[0]
    core = lax.axis_index("tp")
    out_ref[pl.ds(pl.multiple_of(core * count, count), count)] = mine_ref[...]
    out_ref[pl.ds(pl.multiple_of((1 - core) * count, count), count)] = other_ref[...]


def split_heads(value, head):
    count = value.shape[1] // (2 * head)
    pieces = [value[:, i * head : (i + 1) * head] for i in range(2 * count)]
    return jnp.concatenate(pieces[0::2], axis=1), jnp.concatenate(pieces[1::2], axis=1)


def pack(value, out_ref, head):
    keys, values = split_heads(value, head)
    store_packed(keys, values, out_ref)


def store_packed(keys, values, out_ref):
    rows, width = keys.shape
    high = keys.astype(BF16)
    wide = high.astype(F32)
    size = jnp.abs(wide)
    part = (keys - wide) * 256.0 / jnp.where(size > 0, size, 1.0)
    out_ref[:rows, :width] = high
    out_ref[:rows, width:] = values.astype(BF16)
    count = rows // len(LEVELS)
    code, weight = -250.0, 1.0
    for index, levels in enumerate(LEVELS):
        level = jnp.floor((part[index * count : (index + 1) * count] + 1.0) * (levels / 2))
        code = code + jnp.clip(level, 0.0, levels - 1.0) * weight
        weight *= levels
    code = jnp.concatenate([code[: count // 2], code[count // 2 :]], axis=1)
    out_ref[rows:] = code.astype(BF16)


def unpack(ref, rows):
    width = ref.shape[1] // 2
    wide = ref[:rows, :width].astype(F32)
    code = ref[rows:].astype(F32) + 250.0
    code = jnp.concatenate([code[:, :width], code[:, width:]], axis=0)
    parts, weight = [], math.prod(LEVELS)
    for levels in reversed(LEVELS):
        weight /= levels
        level = jnp.floor((code + 0.5) / weight)
        code = code - level * weight
        parts.append((level * 2.0 + 1.0) / levels - 1.0)
    part = jnp.concatenate(parts[::-1], axis=0)
    return wide + jnp.abs(wide) * part * (1.0 / 256.0), ref[:rows, width:].astype(F32)


def store_docs(docs, out_ref):
    rows = docs.shape[1]
    out_ref[rows:, :rows] = jnp.broadcast_to(docs, (16, rows)).astype(BF16)


def load_docs(ref):
    return ref[-16:, : ref.shape[0] - 16].astype(F32)[:1]


def own_kernel(
    head, even_ref, even_other_ref, weight_ref, own_ref, weight_out_ref, rows_ref, arrived
):
    copy = pltpu.make_async_copy(weight_ref, weight_out_ref, arrived)
    copy.start()
    join_rows(even_ref, even_other_ref, rows_ref)
    copy.wait()
    product = times(rows_ref[...], weight_out_ref[...])
    own_ref[...] = jnp.concatenate(split_heads(product, head), axis=1)


def far_kernel(head, got_ref, got_other_ref, weight_ref, sent_ref, rows_ref):
    join_rows(got_ref, got_other_ref, rows_ref)
    pack(times(rows_ref[...], weight_ref[...]), sent_ref, head)


def near_kernel(
    head,
    got_a_ref,
    got_a_other_ref,
    got_b_ref,
    got_b_other_ref,
    weight_ref,
    sent_a_ref,
    sent_b_ref,
    rows_ref,
):
    count = rows_ref.shape[0] // 2
    join_rows(got_a_ref, got_b_other_ref, rows_ref.at[:count])
    join_rows(got_b_ref, got_a_other_ref, rows_ref.at[count:])
    product = times(rows_ref[...], weight_ref[...])
    pack(product[:count], sent_a_ref, head)
    pack(product[count:], sent_b_ref, head)


def turn(value, cosine, sine):
    head = cosine.shape[1]
    pieces = []
    for i in range(value.shape[1] // head):
        piece = value[:, i * head : (i + 1) * head]
        pieces.append(piece * cosine + pltpu.roll(piece, head // 2, 1) * sine)
    return jnp.concatenate(pieces, axis=1)


def query_kernel(query_ref, cosine_ref, sine_ref, out_ref):
    rows, head = cosine_ref.shape
    for index in range(query_ref.shape[1] // head):
        piece = query_ref[:, index * head : (index + 1) * head].astype(F32)
        out_ref[index * rows : (index + 1) * rows] = turn(
            piece, cosine_ref[...], sine_ref[...]
        ).astype(BF16)


def accumulate_kernel(own_ref, got_ref, back_ref, back_other_ref, *refs):
    count = len(refs) // 2
    out_ref, back_out_ref = refs[count - 1 : count + 1]
    keys, values = unpack(got_ref, own_ref.shape[0])
    width = keys.shape[1]
    out_ref[:, :width] = own_ref[:, :width] + keys
    out_ref[:, width:] = own_ref[:, width:] + values
    back_out_ref[...] = (back_ref[...] + back_other_ref[...]).astype(BF16)
    for ref, copy_ref in zip(refs[: count - 1], refs[count + 1 :]):
        copy_ref[...] = ref[...]


def finish_kernel(own_ref, got_a_ref, got_b_ref, docs_ref, cosine_ref, sine_ref, out_ref):
    rows = own_ref.shape[0]
    width = own_ref.shape[1] // 2
    keys, values = own_ref[:, :width], own_ref[:, width:]
    for ref in (got_a_ref, got_b_ref):
        more_keys, more_values = unpack(ref, rows)
        keys, values = keys + more_keys, values + more_values
    out_ref[:rows, :width] = turn(keys, cosine_ref[...], sine_ref[...]).astype(BF16)
    out_ref[:rows, width:] = values.astype(BF16)
    store_docs(docs_ref[...], out_ref)


def allowed_pairs(own_docs, key_docs, distance):
    rows = own_docs.shape[1]
    place = lax.axis_index("ctx")
    query_docs = jnp.broadcast_to(own_docs, (rows, rows)).T
    query_at = place * rows + lax.broadcasted_iota(jnp.int32, (rows, rows), 0)
    key_at = (place ^ distance) * rows + lax.broadcasted_iota(jnp.int32, (rows, rows), 1)
    return (key_at <= query_at) & (key_docs == query_docs)


def attention_kernel(
    head,
    query_ref,
    block_0_ref,
    block_a_ref,
    block_b_ref,
    block_c_ref,
    down_ref,
    back_ref,
    out_ref,
    low_ref,
    grad_ref,
    mixed_ref,
    written,
):
    rows = block_0_ref.shape[0] - 16
    width = block_0_ref.shape[1] // 2
    blocks = (block_0_ref, block_a_ref, block_b_ref, block_c_ref)
    keys = jnp.concatenate([ref[:rows, :width] for ref in blocks], axis=0)
    values = jnp.concatenate([ref[:rows, width:] for ref in blocks], axis=0)
    own_docs = load_docs(block_0_ref)
    allowed = jnp.concatenate(
        [allowed_pairs(own_docs, load_docs(ref), d) for d, ref in zip(distances(), blocks)], axis=1
    )
    scale = head ** (-0.5) * math.log2(math.e)
    ones = jnp.ones((len(blocks) * rows, head), BF16)
    groups = width // head
    pairs = query_ref.shape[0] // (2 * rows)
    copies = []
    for pair in range(pairs):
        shared = slice(pair * groups // pairs * head, (pair * groups // pairs + 1) * head)
        scores = times_transposed(
            query_ref[2 * pair * rows : 2 * (pair + 1) * rows], keys[:, shared]
        ).reshape(2, rows, keys.shape[0])
        scores = jnp.where(allowed[None], scores, -1e30).reshape(2 * rows, keys.shape[0])
        weights = jnp.exp2((scores - jnp.max(scores, axis=1, keepdims=True)) * scale)
        mixed = times(
            weights.astype(BF16), jnp.concatenate([values[:, shared], ones], axis=1)
        )
        mixed = (mixed[:, :head] / mixed[:, head:]).astype(BF16)
        columns = slice(2 * pair * head, 2 * (pair + 1) * head)
        mixed_ref[:, columns] = jnp.concatenate([mixed[:rows], mixed[rows:]], axis=1)
        copies.append(
            pltpu.make_async_copy(
                mixed_ref.at[:, columns], out_ref.at[:, columns], written.at[pair]
            )
        )
        copies[-1].start()
    attended = mixed_ref[...]
    low_ref[...] = times_transposed(attended, down_ref[...])
    grad_ref[...] = transposed_times(back_ref[...], attended)
    for copy in copies:
        copy.wait()


def back_kernel(grad_ref, up_ref, out_ref):
    out_ref[...] = times_transposed(grad_ref[...], up_ref[...])


def grads_kernel(low_ref, low_other_ref, grad_ref, down_ref, own_ref, sent_ref):
    low = (low_ref[...] + low_other_ref[...]).astype(BF16)
    parity = lax.axis_index("ctx") % 2
    up_step, down_step = grad_ref.shape[1] // 2, down_ref.shape[1] // 2
    for index, out in ((1 - parity, sent_ref), (parity, own_ref)):
        columns = pl.ds(pl.multiple_of(index * up_step, up_step), up_step)
        out[:, :up_step] = transposed_times(low, grad_ref[:, columns]).astype(out.dtype)
        columns = pl.ds(pl.multiple_of(index * down_step, down_step), down_step)
        out[:, up_step:] = down_ref[:, columns].astype(out.dtype)


def adapter_kernel(low_ref, low_other_ref, up_ref, out_ref):
    low = (low_ref[...] + low_other_ref[...]).astype(BF16)
    out_ref[...] = times(low, up_ref[...]).astype(BF16)


def add_kernel(own_ref, got_ref, out_ref):
    out_ref[...] = (own_ref[...].astype(F32) + got_ref[...].astype(F32)).astype(BF16)


def total_kernel(own_ref, got_ref, out_ref, square_ref):
    add_kernel(own_ref, got_ref, out_ref)
    squares = jnp.sum(jnp.square(out_ref[...].astype(F32))).reshape(1, 1)
    square_ref[...] = jnp.broadcast_to(squares, square_ref.shape)


def clip_kernel(ceiling, square_ref, other_ref, own_ref, got_ref, up_ref, down_ref):
    squares = square_ref[:1, :1] + other_ref[:1, :1]
    factor = jnp.minimum(1.0, ceiling / (jnp.sqrt(squares) + 1e-06))
    parity = lax.axis_index("ctx") % 2
    up_step, down_step = up_ref.shape[1] // 2, down_ref.shape[1] // 2
    for index, ref in ((parity, own_ref), (1 - parity, got_ref)):
        columns = pl.ds(pl.multiple_of(index * up_step, up_step), up_step)
        up_ref[:, columns] = ref[:, :up_step].astype(F32) * factor
        columns = pl.ds(pl.multiple_of(index * down_step, down_step), down_step)
        down_ref[:, columns] = ref[:, up_step:].astype(F32) * factor


def split_model_width(
    hidden, gain, queries, key_value_weight, adapt_down, adapt_up, out_grad, doc_ids
):
    place = lax.axis_index("ctx")
    rows = hidden.shape[1]
    local_width = hidden.shape[2]
    slice_width = key_value_weight.shape[1]
    kv_count, head = key_value_weight.shape[2], key_value_weight.shape[-1]
    head_count = queries.shape[2]
    local_query = head_count * head
    rank = adapt_down.shape[1]
    kv_width = kv_count * 2 * head

    half = rows // 2
    core = lax.axis_index("tp")
    theirs = lax.dynamic_slice_in_dim(hidden[0], (1 - core) * half, half, 0)
    hidden, theirs = lax.optimization_barrier((hidden, theirs))
    mine = lax.dynamic_slice_in_dim(hidden[0], core * half, half, 0)
    part = ((half, slice_width), BF16)
    slices = call(
        norm_kernel,
        [part] * 4,
        mine,
        swap(theirs, "tp", 1),
        gain,
        swap(gain, "tp", 1),
        scratch=[pltpu.VMEM((3, half, slice_width), BF16), pltpu.SemaphoreType.DMA((3,))],
        loose_outs=(1, 2, 3),
    )

    def send_a(value):
        return lax.ppermute(
            value, ("ctx", "tp"), [(2 * a + t, 2 * (a ^ (2 if t else 1)) + t) for a in range(4) for t in range(2)]
        )

    def send_b(value):
        return lax.ppermute(
            value, ("ctx", "tp"), [(2 * a + t, 2 * (a ^ (1 if t else 2)) + t) for a in range(4) for t in range(2)]
        )

    even, slice_a, slice_b, slice_c = slices
    got_a, got_b, got_c = send_a(slice_a), send_b(slice_b), swap(slice_c, "ctx", 3)
    part_flops = 2 * rows * slice_width * kv_width
    packed = ((rows + rows // 8, kv_width), BF16)
    summed = ((rows, kv_width), F32)
    final = ((rows + 16, kv_width), BF16)

    def step(function, *operands):
        shapes = jax.eval_shape(function, *operands)
        return lax.cond(
            place < 4,
            function,
            lambda *_: jax.tree.map(lambda x: jnp.zeros(x.shape, x.dtype), shapes),
            *operands,
        )

    key_value_weight, slice_c = lax.optimization_barrier((key_value_weight, slice_c))

    def prepare(key_value_weight):
        return key_value_weight[0].reshape(slice_width, kv_width)

    weight = step(prepare, key_value_weight)

    def prepare_attention(queries, out_grad, adapt_up, doc_ids, weight):
        docs = doc_ids.astype(F32).reshape(1, rows)
        freqs = 1000000.0 ** (-jnp.arange(head // 2, dtype=F32) * 2.0 / head)
        positions = place * rows + jnp.arange(rows, dtype=jnp.int32)
        angles = positions.astype(F32)[:, None] * freqs
        cosine, sine = jnp.cos(angles), jnp.sin(angles)
        cosine = jnp.concatenate([cosine, cosine], axis=1)
        sine = jnp.concatenate([-sine, sine], axis=1)
        (query,) = call(
            query_kernel,
            [((head_count * rows, head), BF16)],
            queries[0].reshape(rows, local_query),
            cosine,
            sine,
        )
        (back_part,) = call(
            back_kernel,
            [((rows, rank), F32)],
            out_grad[0],
            adapt_up[0],
            flops=2 * rows * local_width * rank,
        )
        return docs, cosine, sine, query, back_part, swap(back_part, "tp", 1)

    docs, cosine, sine, query, back_part, back_other = step(
        prepare_attention, queries, out_grad, adapt_up, doc_ids, weight
    )
    part_0, weight_near = call(
        functools.partial(own_kernel, head),
        [summed, (weight.shape, BF16)],
        even,
        swap(even, "tp", 1),
        weight,
        flops=part_flops,
        scratch=[pltpu.VMEM((rows, slice_width), BF16), pltpu.SemaphoreType.DMA],
        loose=(2,),
    )
    got_c, part_0, docs = lax.optimization_barrier((got_c, part_0, docs))

    def far_parts(got_c, weight):
        return call(
            functools.partial(far_kernel, head),
            [packed],
            got_c,
            swap(got_c, "tp", 1),
            weight,
            flops=part_flops,
            scratch=[pltpu.VMEM((rows, slice_width), BF16)],
        )

    (sent_c,) = step(far_parts, got_c, weight)
    arrived_c = swap(sent_c, "ctx", 3)
    got_a, got_b, sent_c = lax.optimization_barrier((got_a, got_b, sent_c))
    sent_a, sent_b = call(
        functools.partial(near_kernel, head),
        [packed, packed],
        got_a,
        swap(got_a, "tp", 1),
        got_b,
        swap(got_b, "tp", 1),
        weight_near,
        flops=2 * part_flops,
        scratch=[pltpu.VMEM((2 * rows, slice_width), BF16)],
    )
    arrived_a, arrived_b = send_a(sent_a), send_b(sent_b)
    part_0, back_rows, docs, cosine, sine, staged_down = call(
        accumulate_kernel,
        [
            summed,
            ((rows, rank), BF16),
            ((1, rows), F32),
            ((rows, head), F32),
            ((rows, head), F32),
            ((rank, local_query), BF16),
        ],
        part_0,
        arrived_c,
        back_part,
        back_other,
        docs,
        cosine,
        sine,
        adapt_down[0],
    )
    arrived_a, arrived_b, part_0 = lax.optimization_barrier((arrived_a, arrived_b, part_0))
    (block_0,) = call(finish_kernel, [final], part_0, arrived_a, arrived_b, docs, cosine, sine)

    attended, low_part, down_part = call(
        functools.partial(attention_kernel, head),
        [((rows, local_query), BF16), ((rows, rank), F32), ((rank, local_query), F32)],
        query,
        block_0,
        send_a(block_0),
        send_b(block_0),
        swap(block_0, "ctx", 3),
        staged_down,
        back_rows,
        flops=16 * rows * rows * local_query,
        scratch=[
            pltpu.VMEM((rows, local_query), BF16),
            pltpu.SemaphoreType.DMA((head_count // 2,)),
        ],
        loose_outs=(0,),
    )
    low_other = swap(low_part, "tp", 1)
    piece = (rank, (local_width + local_query) // 2)
    own, sent = call(
        grads_kernel,
        [(piece, F32), (piece, BF16)],
        low_part,
        low_other,
        out_grad[0],
        down_part,
        flops=2 * rows * rank * local_width,
    )
    (adapter_rows,) = call(
        adapter_kernel,
        [((rows, local_width), BF16)],
        low_part,
        low_other,
        adapt_up[0],
        flops=2 * rows * rank * local_width,
    )
    got_sum, adapter_rows = lax.optimization_barrier((swap(sent, "ctx", 1), adapter_rows))
    (pair_sum,) = call(add_kernel, [(piece, BF16)], own, got_sum)
    total, squares = call(
        total_kernel, [(piece, BF16), ((8, 128), F32)], pair_sum, swap(pair_sum, "ctx", 2)
    )
    total_other = swap(total, "ctx", 1)
    squares = squares + swap(squares, "tp", 1)
    beside = lax.ppermute(
        squares,
        ("section", "tp"),
        [(2 * i + t, 2 * (i ^ (2 if t else 1)) + t) for i in range(4) for t in range(2)],
    )
    across = swap(squares, "section", 3)
    squares = jnp.where(core == 0, squares + across + beside, beside)
    squares = squares + swap(squares, "ctx", 1)
    ceiling = 0.5 * math.sqrt(lax.axis_size("section") * rank * (local_query + local_width) * 2)
    grad_up, grad_down = call(
        functools.partial(clip_kernel, ceiling),
        [((rank, local_width), F32), ((rank, local_query), F32)],
        squares,
        swap(squares, "tp", 1),
        total,
        total_other,
    )
    return (attended[None], adapter_rows[None], grad_down[None], grad_up[None])


def per_device(*arrays):
    if lax.axis_size("ctx") == 4 and lax.axis_size("tp") == 2 and lax.axis_size("section") == 4:
        return split_model_width(*arrays)
    return gathered_weights(*arrays)


def solution(mesh):
    return jax.shard_map(
        per_device,
        mesh=mesh,
        in_specs=(
            P("section", "ctx", "tp"),
            P("section", "tp"),
            P("section", "ctx", "tp", None),
            P("section", "ctx", "tp", None, None),
            P("section", None, "tp"),
            P("section", None, "tp"),
            P("section", "ctx", "tp"),
            P("ctx"),
        ),
        out_specs=(
            P("section", "ctx", "tp"),
            P("section", "ctx", "tp"),
            P("section", None, "tp"),
            P("section", None, "tp"),
        ),
        check_vma=False,
    )
```

```python
import functools
import math

import jax
import jax.numpy as jnp
from jax import lax
from jax.experimental import pallas as pl
from jax.experimental.pallas import tpu as pltpu
from jax.sharding import PartitionSpec as P


def rotate(head_values, positions):
    half_width = head_values.shape[-1] // 2
    freqs = 1000000.0 ** (-jnp.arange(half_width, dtype=jnp.float32) * 2.0 / head_values.shape[-1])
    angles = positions.astype(jnp.float32)[:, None] * freqs[None, :]
    cosine = jnp.cos(angles)[:, None, :]
    sine_table = jnp.sin(angles)[:, None, :]
    first_half = head_values[..., :half_width]
    second_half = head_values[..., half_width:]
    return jnp.concatenate(
        [
            first_half * cosine - second_half * sine_table,
            second_half * cosine + first_half * sine_table,
        ],
        axis=-1,
    )


def gathered_weights(hidden, gain, queries, key_value_weight, adapt_down, adapt_up, out_grad, doc_ids):
    tp_count = lax.axis_size("tp")
    row_count = hidden.shape[1]
    local_width = hidden.shape[2]
    head_dim = key_value_weight.shape[-1]
    kv_count = key_value_weight.shape[2]
    head_count = queries.shape[2]
    group_size = head_count // kv_count
    local_query = head_count * head_dim
    rank_size = adapt_down.shape[1]
    key_block = 1024
    full_rows, full_gain = (
        lax.all_gather(hidden, "tp", axis=2, tiled=True),
        lax.all_gather(gain, "tp", axis=1, tiled=True),
    )
    widened = full_rows[0].astype(jnp.float32)
    normalized_rows = (
        widened
        * lax.rsqrt(jnp.mean(widened * widened, axis=1, keepdims=True) + 1e-06)
        * full_gain[0].astype(jnp.float32)
    ).astype(jnp.bfloat16)
    kv_local = key_value_weight.reshape(1, key_value_weight.shape[1], kv_count * 2 * head_dim)
    keyval_raw = jnp.dot(
        normalized_rows,
        lax.all_gather(kv_local, "ctx", axis=1, tiled=True)[0],
        preferred_element_type=jnp.float32,
    )
    positions = lax.axis_index("ctx") * row_count + jnp.arange(row_count, dtype=jnp.int32)
    key_value_rows = keyval_raw.reshape(row_count, kv_count, 2, head_dim)
    rotated_keys = rotate(key_value_rows[:, :, 0], positions).astype(jnp.bfloat16)
    value_rows = key_value_rows[:, :, 1].astype(jnp.bfloat16)
    rotated_query = rotate(queries[0].astype(jnp.float32), positions).astype(jnp.bfloat16)
    stacked = (
        rotated_query.reshape(row_count, kv_count, group_size, head_dim)
        .transpose(1, 2, 0, 3)
        .reshape(kv_count, group_size * row_count, head_dim)
    )
    query_pos = jnp.tile(positions, group_size)
    query_doc = jnp.tile(doc_ids, group_size).astype(jnp.float32)
    score_scale = head_dim ** (-0.5)
    start_state = (
        jnp.full((kv_count, group_size * row_count), -1e30, jnp.float32),
        jnp.zeros((kv_count, group_size * row_count), jnp.float32),
        jnp.zeros((kv_count, group_size * row_count, head_dim), jnp.float32),
    )
    carried = start_state
    first_row = jnp.int32(0)
    piece_keys = lax.all_gather(rotated_keys, "ctx", axis=0, tiled=True)
    piece_values = lax.all_gather(value_rows, "ctx", axis=0, tiled=True)
    piece_docs = lax.all_gather(doc_ids.astype(jnp.bfloat16), "ctx", axis=0, tiled=True)
    key_total = piece_keys.shape[0]
    for block_start in range(0, key_total, key_block):
        block_stop = min(key_total, block_start + key_block)
        block_keys = piece_keys[block_start:block_stop]
        block_values = piece_values[block_start:block_stop]
        key_pos = first_row + block_start + jnp.arange(block_keys.shape[0], dtype=jnp.int32)
        key_doc = piece_docs[block_start:block_stop].astype(jnp.float32)
        running_top, running_sum, running_acc = carried
        scores = (
            jnp.einsum("gqd,kgd->gqk", stacked, block_keys, preferred_element_type=jnp.float32)
            * score_scale
        )
        allowed = (
            (key_pos[None, :] <= query_pos[:, None]) & (key_doc[None, :] == query_doc[:, None])
        )[None]
        scores = jnp.where(allowed, scores, -1e30)
        new_top = jnp.maximum(running_top, jnp.max(scores, axis=2))
        weights = jnp.where(allowed, jnp.exp(scores - new_top[:, :, None]), 0.0)
        shrink = jnp.exp(running_top - new_top)
        new_acc = running_acc * shrink[:, :, None] + jnp.einsum(
            "gqk,kgd->gqd",
            weights.astype(jnp.bfloat16),
            block_values,
            preferred_element_type=jnp.float32,
        )
        carried = (new_top, running_sum * shrink + jnp.sum(weights, axis=2), new_acc)
    final_top, final_sum, final_acc = carried
    attended = (
        (final_acc / final_sum[:, :, None])
        .reshape(kv_count, group_size, row_count, head_dim)
        .transpose(2, 0, 1, 3)
        .reshape(row_count, local_query)
        .astype(jnp.bfloat16)
    )
    low_part = jnp.dot(attended, adapt_down[0].T, preferred_element_type=jnp.float32)
    back_part = jnp.dot(out_grad[0], adapt_up[0].T, preferred_element_type=jnp.float32)
    low_sum, back_sum = lax.psum((low_part, back_part), "tp")
    low_rows = low_sum.astype(jnp.bfloat16)
    back_rows = back_sum.astype(jnp.bfloat16)
    adapter_rows = jnp.dot(low_rows, adapt_up[0], preferred_element_type=jnp.float32).astype(
        jnp.bfloat16
    )
    up_part = jnp.dot(low_rows.T, out_grad[0], preferred_element_type=jnp.float32)
    down_part = jnp.dot(back_rows.T, attended, preferred_element_type=jnp.float32)
    ceiling = 0.5 * math.sqrt(
        lax.axis_size("section") * rank_size * (local_query + local_width) * tp_count
    )
    up_total, down_total = (
        lax.psum(up_part.astype(jnp.bfloat16), "ctx").astype(jnp.float32),
        lax.psum(down_part.astype(jnp.bfloat16), "ctx").astype(jnp.float32),
    )
    local_squares = jnp.sum(up_total * up_total) + jnp.sum(down_total * down_total)
    squares = lax.psum(local_squares, ("section", "tp"))
    factor = jnp.minimum(1.0, ceiling / (jnp.sqrt(squares) + 1e-06))
    grad_up = up_total * factor
    grad_down = down_total * factor
    return (attended[None], adapter_rows[None], grad_down[None], grad_up[None])


F32, BF16 = jnp.float32, jnp.bfloat16
VMEM = pl.BlockSpec(memory_space=pltpu.VMEM)
ANYWHERE = pl.BlockSpec(memory_space=pl.ANY)
LIMIT = 16 * 1024 * 1024
LEVELS = (5, 5, 5, 4)


def swap(value, axis, distance):
    count = lax.axis_size(axis)
    return lax.ppermute(value, axis, [(i, i ^ distance) for i in range(count)])


def call(kernel, outs, *operands, flops=0, scratch=(), loose=(), loose_outs=()):
    shapes = [jax.ShapeDtypeStruct(shape, dtype) for shape, dtype in outs]
    moved = sum(math.prod(x.shape) * x.dtype.itemsize for x in (*operands, *shapes))
    return pl.pallas_call(
        kernel,
        out_shape=shapes,
        in_specs=[ANYWHERE if i in loose else VMEM for i in range(len(operands))],
        out_specs=[ANYWHERE if i in loose_outs else VMEM for i in range(len(shapes))],
        scratch_shapes=scratch,
        compiler_params=pltpu.CompilerParams(vmem_limit_bytes=LIMIT),
        cost_estimate=pl.CostEstimate(flops=flops, bytes_accessed=moved, transcendentals=0),
    )(*operands)


def times(left, right):
    return lax.dot_general(left, right, (((1,), (0,)), ((), ())), preferred_element_type=F32)


def times_transposed(left, right):
    return lax.dot_general(left, right, (((1,), (1,)), ((), ())), preferred_element_type=F32)


def transposed_times(left, right):
    return lax.dot_general(left, right, (((0,), (0,)), ((), ())), preferred_element_type=F32)


def distances():
    core = lax.axis_index("tp")
    return 0, jnp.where(core == 0, 1, 2), jnp.where(core == 0, 2, 1), 3


def norm_kernel(mine_ref, other_ref, gain_ref, gain_other_ref, *refs):
    outs, (held_ref, written) = refs[:4], refs[4:]
    width = outs[0].shape[1]
    place, core = lax.axis_index("ctx"), lax.axis_index("tp")
    mine, other = mine_ref[...].astype(F32), other_ref[...].astype(F32)
    squares = [jnp.sum(rows * rows, axis=1, keepdims=True) for rows in (mine, other)]
    scale = lax.rsqrt((squares[0] + squares[1]) / (4 * width) + 1e-06)
    copies = []
    for index in (3, 1, 2, 0):
        chip = place ^ distances()[index]
        columns = pl.ds(pl.multiple_of(chip % 2 * width, width), width)
        slot = outs[0] if index == 0 else held_ref.at[index - 1]

        def write(rows_ref, weights_ref, slot=slot, columns=columns):
            rows = rows_ref[:, columns].astype(F32) * scale
            slot[...] = (rows * weights_ref[:, columns].astype(F32)).astype(BF16)

        pl.when(chip // 2 == core)(functools.partial(write, mine_ref, gain_ref))
        pl.when(chip // 2 != core)(functools.partial(write, other_ref, gain_other_ref))
        if index:
            copies.append(pltpu.make_async_copy(slot, outs[index], written.at[index - 1]))
            copies[-1].start()
    for copy in copies:
        copy.wait()


def join_rows(mine_ref, other_ref, out_ref):
    count = mine_ref.shape[0]
    core = lax.axis_index("tp")
    out_ref[pl.ds(pl.multiple_of(core * count, count), count)] = mine_ref[...]
    out_ref[pl.ds(pl.multiple_of((1 - core) * count, count), count)] = other_ref[...]


def split_heads(value, head):
    count = value.shape[1] // (2 * head)
    pieces = [value[:, i * head : (i + 1) * head] for i in range(2 * count)]
    return jnp.concatenate(pieces[0::2], axis=1), jnp.concatenate(pieces[1::2], axis=1)


def pack(value, out_ref, head):
    keys, values = split_heads(value, head)
    store_packed(keys, values, out_ref)


def store_packed(keys, values, out_ref):
    rows, width = keys.shape
    high = keys.astype(BF16)
    wide = high.astype(F32)
    size = jnp.abs(wide)
    part = (keys - wide) * 256.0 / jnp.where(size > 0, size, 1.0)
    out_ref[:rows, :width] = high
    out_ref[:rows, width:] = values.astype(BF16)
    count = rows // len(LEVELS)
    code, weight = -250.0, 1.0
    for index, levels in enumerate(LEVELS):
        level = jnp.floor((part[index * count : (index + 1) * count] + 1.0) * (levels / 2))
        code = code + jnp.clip(level, 0.0, levels - 1.0) * weight
        weight *= levels
    code = jnp.concatenate([code[: count // 2], code[count // 2 :]], axis=1)
    out_ref[rows:] = code.astype(BF16)


def unpack(ref, rows):
    width = ref.shape[1] // 2
    wide = ref[:rows, :width].astype(F32)
    code = ref[rows:].astype(F32) + 250.0
    code = jnp.concatenate([code[:, :width], code[:, width:]], axis=0)
    parts, weight = [], math.prod(LEVELS)
    for levels in reversed(LEVELS):
        weight /= levels
        level = jnp.floor((code + 0.5) / weight)
        code = code - level * weight
        parts.append((level * 2.0 + 1.0) / levels - 1.0)
    part = jnp.concatenate(parts[::-1], axis=0)
    return wide + jnp.abs(wide) * part * (1.0 / 256.0), ref[:rows, width:].astype(F32)


def store_docs(docs, out_ref):
    rows = docs.shape[1]
    out_ref[rows:, :rows] = jnp.broadcast_to(docs, (16, rows)).astype(BF16)


def load_docs(ref):
    return ref[-16:, : ref.shape[0] - 16].astype(F32)[:1]


def own_kernel(
    head, even_ref, even_other_ref, weight_ref, own_ref, weight_out_ref, rows_ref, arrived
):
    copy = pltpu.make_async_copy(weight_ref, weight_out_ref, arrived)
    copy.start()
    join_rows(even_ref, even_other_ref, rows_ref)
    copy.wait()
    product = times(rows_ref[...], weight_out_ref[...])
    own_ref[...] = jnp.concatenate(split_heads(product, head), axis=1)


def far_kernel(head, got_ref, got_other_ref, weight_ref, sent_ref, rows_ref):
    join_rows(got_ref, got_other_ref, rows_ref)
    pack(times(rows_ref[...], weight_ref[...]), sent_ref, head)


def near_kernel(
    head,
    got_a_ref,
    got_a_other_ref,
    got_b_ref,
    got_b_other_ref,
    weight_ref,
    sent_a_ref,
    sent_b_ref,
    rows_ref,
):
    count = rows_ref.shape[0] // 2
    join_rows(got_a_ref, got_b_other_ref, rows_ref.at[:count])
    join_rows(got_b_ref, got_a_other_ref, rows_ref.at[count:])
    product = times(rows_ref[...], weight_ref[...])
    pack(product[:count], sent_a_ref, head)
    pack(product[count:], sent_b_ref, head)


def turn(value, cosine, sine):
    head = cosine.shape[1]
    pieces = []
    for i in range(value.shape[1] // head):
        piece = value[:, i * head : (i + 1) * head]
        pieces.append(piece * cosine + pltpu.roll(piece, head // 2, 1) * sine)
    return jnp.concatenate(pieces, axis=1)


def query_kernel(query_ref, cosine_ref, sine_ref, out_ref):
    rows, head = cosine_ref.shape
    for index in range(query_ref.shape[1] // head):
        piece = query_ref[:, index * head : (index + 1) * head].astype(F32)
        out_ref[index * rows : (index + 1) * rows] = turn(
            piece, cosine_ref[...], sine_ref[...]
        ).astype(BF16)


def accumulate_kernel(own_ref, got_ref, back_ref, back_other_ref, *refs):
    count = len(refs) // 2
    out_ref, back_out_ref = refs[count - 1 : count + 1]
    keys, values = unpack(got_ref, own_ref.shape[0])
    width = keys.shape[1]
    out_ref[:, :width] = own_ref[:, :width] + keys
    out_ref[:, width:] = own_ref[:, width:] + values
    back_out_ref[...] = (back_ref[...] + back_other_ref[...]).astype(BF16)
    for ref, copy_ref in zip(refs[: count - 1], refs[count + 1 :]):
        copy_ref[...] = ref[...]


def finish_kernel(own_ref, got_a_ref, got_b_ref, docs_ref, cosine_ref, sine_ref, out_ref):
    rows = own_ref.shape[0]
    width = own_ref.shape[1] // 2
    keys, values = own_ref[:, :width], own_ref[:, width:]
    for ref in (got_a_ref, got_b_ref):
        more_keys, more_values = unpack(ref, rows)
        keys, values = keys + more_keys, values + more_values
    out_ref[:rows, :width] = turn(keys, cosine_ref[...], sine_ref[...]).astype(BF16)
    out_ref[:rows, width:] = values.astype(BF16)
    store_docs(docs_ref[...], out_ref)


def allowed_pairs(own_docs, key_docs, distance):
    rows = own_docs.shape[1]
    place = lax.axis_index("ctx")
    query_docs = jnp.broadcast_to(own_docs, (rows, rows)).T
    query_at = place * rows + lax.broadcasted_iota(jnp.int32, (rows, rows), 0)
    key_at = (place ^ distance) * rows + lax.broadcasted_iota(jnp.int32, (rows, rows), 1)
    return (key_at <= query_at) & (key_docs == query_docs)


def attention_kernel(
    head,
    query_ref,
    block_0_ref,
    block_a_ref,
    block_b_ref,
    block_c_ref,
    down_ref,
    back_ref,
    out_ref,
    low_ref,
    grad_ref,
    mixed_ref,
    written,
):
    rows = block_0_ref.shape[0] - 16
    width = block_0_ref.shape[1] // 2
    blocks = (block_0_ref, block_a_ref, block_b_ref, block_c_ref)
    keys = jnp.concatenate([ref[:rows, :width] for ref in blocks], axis=0)
    values = jnp.concatenate([ref[:rows, width:] for ref in blocks], axis=0)
    own_docs = load_docs(block_0_ref)
    allowed = jnp.concatenate(
        [allowed_pairs(own_docs, load_docs(ref), d) for d, ref in zip(distances(), blocks)], axis=1
    )
    scale = head ** (-0.5) * math.log2(math.e)
    ones = jnp.ones((len(blocks) * rows, head), BF16)
    excluded = -1e30 * head**0.5
    groups = width // head
    pairs = query_ref.shape[0] // (2 * rows)
    copies = []
    for pair in range(pairs):
        shared = slice(pair * groups // pairs * head, (pair * groups // pairs + 1) * head)
        scores = times_transposed(
            query_ref[2 * pair * rows : 2 * (pair + 1) * rows], keys[:, shared]
        ).reshape(2, rows, keys.shape[0])
        scores = jnp.where(allowed[None], scores, excluded).reshape(2 * rows, keys.shape[0])
        weights = jnp.exp2((scores - jnp.max(scores, axis=1, keepdims=True)) * scale)
        mixed = times(
            weights.astype(BF16), jnp.concatenate([values[:, shared], ones], axis=1)
        )
        mixed = (mixed[:, :head] / mixed[:, head:]).astype(BF16)
        columns = slice(2 * pair * head, 2 * (pair + 1) * head)
        mixed_ref[:, columns] = jnp.concatenate([mixed[:rows], mixed[rows:]], axis=1)
        copies.append(
            pltpu.make_async_copy(
                mixed_ref.at[:, columns], out_ref.at[:, columns], written.at[pair]
            )
        )
        copies[-1].start()
    attended = mixed_ref[...]
    low_ref[...] = times_transposed(attended, down_ref[...])
    grad_ref[...] = transposed_times(back_ref[...], attended)
    for copy in copies:
        copy.wait()


def back_kernel(grad_ref, up_ref, out_ref):
    out_ref[...] = times_transposed(grad_ref[...], up_ref[...])


def grads_kernel(low_ref, low_other_ref, grad_ref, down_ref, own_ref, sent_ref):
    low = (low_ref[...] + low_other_ref[...]).astype(BF16)
    parity = lax.axis_index("ctx") % 2
    up_step, down_step = grad_ref.shape[1] // 2, down_ref.shape[1] // 2
    for index, out in ((1 - parity, sent_ref), (parity, own_ref)):
        columns = pl.ds(pl.multiple_of(index * up_step, up_step), up_step)
        out[:, :up_step] = transposed_times(low, grad_ref[:, columns]).astype(out.dtype)
        columns = pl.ds(pl.multiple_of(index * down_step, down_step), down_step)
        out[:, up_step:] = down_ref[:, columns].astype(out.dtype)


def adapter_kernel(low_ref, low_other_ref, up_ref, out_ref):
    low = (low_ref[...] + low_other_ref[...]).astype(BF16)
    out_ref[...] = times(low, up_ref[...]).astype(BF16)


def add_kernel(own_ref, got_ref, out_ref):
    out_ref[...] = (own_ref[...].astype(F32) + got_ref[...].astype(F32)).astype(BF16)


def total_kernel(own_ref, got_ref, out_ref, square_ref):
    add_kernel(own_ref, got_ref, out_ref)
    squares = jnp.sum(jnp.square(out_ref[...].astype(F32))).reshape(1, 1)
    square_ref[...] = jnp.broadcast_to(squares, square_ref.shape)


def clip_kernel(ceiling, square_ref, other_ref, own_ref, got_ref, up_ref, down_ref):
    squares = square_ref[:1, :1] + other_ref[:1, :1]
    factor = jnp.minimum(1.0, ceiling / (jnp.sqrt(squares) + 1e-06))
    parity = lax.axis_index("ctx") % 2
    up_step, down_step = up_ref.shape[1] // 2, down_ref.shape[1] // 2
    for index, ref in ((parity, own_ref), (1 - parity, got_ref)):
        columns = pl.ds(pl.multiple_of(index * up_step, up_step), up_step)
        up_ref[:, columns] = ref[:, :up_step].astype(F32) * factor
        columns = pl.ds(pl.multiple_of(index * down_step, down_step), down_step)
        down_ref[:, columns] = ref[:, up_step:].astype(F32) * factor


def split_model_width(
    hidden, gain, queries, key_value_weight, adapt_down, adapt_up, out_grad, doc_ids
):
    place = lax.axis_index("ctx")
    rows = hidden.shape[1]
    local_width = hidden.shape[2]
    slice_width = key_value_weight.shape[1]
    kv_count, head = key_value_weight.shape[2], key_value_weight.shape[-1]
    head_count = queries.shape[2]
    local_query = head_count * head
    rank = adapt_down.shape[1]
    kv_width = kv_count * 2 * head

    half = rows // 2
    core = lax.axis_index("tp")
    mine = lax.dynamic_slice_in_dim(hidden[0], core * half, half, 0)
    theirs = lax.dynamic_slice_in_dim(hidden[0], (1 - core) * half, half, 0)
    part = ((half, slice_width), BF16)
    slices = call(
        norm_kernel,
        [part] * 4,
        mine,
        swap(theirs, "tp", 1),
        gain,
        swap(gain, "tp", 1),
        scratch=[pltpu.VMEM((3, half, slice_width), BF16), pltpu.SemaphoreType.DMA((3,))],
        loose_outs=(1, 2, 3),
    )

    def send_a(value):
        return lax.ppermute(
            value, ("ctx", "tp"), [(2 * a + t, 2 * (a ^ (2 if t else 1)) + t) for a in range(4) for t in range(2)]
        )

    def send_b(value):
        return lax.ppermute(
            value, ("ctx", "tp"), [(2 * a + t, 2 * (a ^ (1 if t else 2)) + t) for a in range(4) for t in range(2)]
        )

    even, slice_a, slice_b, slice_c = slices
    got_a, got_b, got_c = send_a(slice_a), send_b(slice_b), swap(slice_c, "ctx", 3)
    part_flops = 2 * rows * slice_width * kv_width
    packed = ((rows + rows // 8, kv_width), BF16)
    summed = ((rows, kv_width), F32)
    final = ((rows + 16, kv_width), BF16)

    def step(function, *operands):
        shapes = jax.eval_shape(function, *operands)
        return lax.cond(
            place < 4,
            function,
            lambda *_: jax.tree.map(lambda x: jnp.zeros(x.shape, x.dtype), shapes),
            *operands,
        )

    def prepare(key_value_weight):
        return key_value_weight[0].reshape(slice_width, kv_width)

    weight = step(prepare, key_value_weight)

    def prepare_attention(queries, out_grad, adapt_up, doc_ids, weight):
        docs = doc_ids.astype(F32).reshape(1, rows)
        freqs = 1000000.0 ** (-jnp.arange(head // 2, dtype=F32) * 2.0 / head)
        positions = place * rows + jnp.arange(rows, dtype=jnp.int32)
        angles = positions.astype(F32)[:, None] * freqs
        cosine, sine = jnp.cos(angles), jnp.sin(angles)
        cosine = jnp.concatenate([cosine, cosine], axis=1)
        sine = jnp.concatenate([-sine, sine], axis=1)
        (query,) = call(
            query_kernel,
            [((head_count * rows, head), BF16)],
            queries[0].reshape(rows, local_query),
            cosine,
            sine,
        )
        (back_part,) = call(
            back_kernel,
            [((rows, rank), F32)],
            out_grad[0],
            adapt_up[0],
            flops=2 * rows * local_width * rank,
        )
        return docs, cosine, sine, query, back_part, swap(back_part, "tp", 1)

    docs, cosine, sine, query, back_part, back_other = step(
        prepare_attention, queries, out_grad, adapt_up, doc_ids, weight
    )
    part_0, weight_near = call(
        functools.partial(own_kernel, head),
        [summed, (weight.shape, BF16)],
        even,
        swap(even, "tp", 1),
        weight,
        flops=part_flops,
        scratch=[pltpu.VMEM((rows, slice_width), BF16), pltpu.SemaphoreType.DMA],
        loose=(2,),
    )
    got_c, part_0, docs = lax.optimization_barrier((got_c, part_0, docs))

    def far_parts(got_c, weight):
        return call(
            functools.partial(far_kernel, head),
            [packed],
            got_c,
            swap(got_c, "tp", 1),
            weight,
            flops=part_flops,
            scratch=[pltpu.VMEM((rows, slice_width), BF16)],
        )

    (sent_c,) = step(far_parts, got_c, weight)
    arrived_c = swap(sent_c, "ctx", 3)
    got_a, got_b, sent_c = lax.optimization_barrier((got_a, got_b, sent_c))
    sent_a, sent_b = call(
        functools.partial(near_kernel, head),
        [packed, packed],
        got_a,
        swap(got_a, "tp", 1),
        got_b,
        swap(got_b, "tp", 1),
        weight_near,
        flops=2 * part_flops,
        scratch=[pltpu.VMEM((2 * rows, slice_width), BF16)],
    )
    arrived_a, arrived_b = send_a(sent_a), send_b(sent_b)
    part_0, back_rows, docs, cosine, sine, staged_down = call(
        accumulate_kernel,
        [
            summed,
            ((rows, rank), BF16),
            ((1, rows), F32),
            ((rows, head), F32),
            ((rows, head), F32),
            ((rank, local_query), BF16),
        ],
        part_0,
        arrived_c,
        back_part,
        back_other,
        docs,
        cosine,
        sine,
        adapt_down[0],
    )
    arrived_a, arrived_b, part_0 = lax.optimization_barrier((arrived_a, arrived_b, part_0))
    (block_0,) = call(finish_kernel, [final], part_0, arrived_a, arrived_b, docs, cosine, sine)

    attended, low_part, down_part = call(
        functools.partial(attention_kernel, head),
        [((rows, local_query), BF16), ((rows, rank), F32), ((rank, local_query), F32)],
        query,
        block_0,
        send_a(block_0),
        send_b(block_0),
        swap(block_0, "ctx", 3),
        staged_down,
        back_rows,
        flops=16 * rows * rows * local_query,
        scratch=[
            pltpu.VMEM((rows, local_query), BF16),
            pltpu.SemaphoreType.DMA((head_count // 2,)),
        ],
        loose_outs=(0,),
    )
    low_other = swap(low_part, "tp", 1)
    piece = (rank, (local_width + local_query) // 2)
    own, sent = call(
        grads_kernel,
        [(piece, F32), (piece, BF16)],
        low_part,
        low_other,
        out_grad[0],
        down_part,
        flops=2 * rows * rank * local_width,
    )
    (adapter_rows,) = call(
        adapter_kernel,
        [((rows, local_width), BF16)],
        low_part,
        low_other,
        adapt_up[0],
        flops=2 * rows * rank * local_width,
    )
    got_sum, adapter_rows = lax.optimization_barrier((swap(sent, "ctx", 1), adapter_rows))
    (pair_sum,) = call(add_kernel, [(piece, BF16)], own, got_sum)
    total, squares = call(
        total_kernel, [(piece, BF16), ((8, 128), F32)], pair_sum, swap(pair_sum, "ctx", 2)
    )
    total_other = swap(total, "ctx", 1)
    squares = squares + swap(squares, "tp", 1)
    beside = lax.ppermute(
        squares,
        ("section", "tp"),
        [(2 * i + t, 2 * (i ^ (2 if t else 1)) + t) for i in range(4) for t in range(2)],
    )
    across = swap(squares, "section", 3)
    squares = jnp.where(core == 0, squares + across + beside, beside)
    squares = squares + swap(squares, "ctx", 1)
    ceiling = 0.5 * math.sqrt(lax.axis_size("section") * rank * (local_query + local_width) * 2)
    grad_up, grad_down = call(
        functools.partial(clip_kernel, ceiling),
        [((rank, local_width), F32), ((rank, local_query), F32)],
        squares,
        swap(squares, "tp", 1),
        total,
        total_other,
    )
    return (attended[None], adapter_rows[None], grad_down[None], grad_up[None])


def per_device(*arrays):
    if lax.axis_size("ctx") == 4 and lax.axis_size("tp") == 2 and lax.axis_size("section") == 4:
        return split_model_width(*arrays)
    return gathered_weights(*arrays)


def solution(mesh):
    return jax.shard_map(
        per_device,
        mesh=mesh,
        in_specs=(
            P("section", "ctx", "tp"),
            P("section", "tp"),
            P("section", "ctx", "tp", None),
            P("section", "ctx", "tp", None, None),
            P("section", None, "tp"),
            P("section", None, "tp"),
            P("section", "ctx", "tp"),
            P("ctx"),
        ),
        out_specs=(
            P("section", "ctx", "tp"),
            P("section", "ctx", "tp"),
            P("section", None, "tp"),
            P("section", None, "tp"),
        ),
        check_vma=False,
    )
```

```python
import functools
import math

import jax
import jax.numpy as jnp
from jax import lax
from jax.experimental import pallas as pl
from jax.experimental.pallas import tpu as pltpu
from jax.sharding import PartitionSpec as P


def rotate(head_values, positions):
    half_width = head_values.shape[-1] // 2
    freqs = 1000000.0 ** (-jnp.arange(half_width, dtype=jnp.float32) * 2.0 / head_values.shape[-1])
    angles = positions.astype(jnp.float32)[:, None] * freqs[None, :]
    cosine = jnp.cos(angles)[:, None, :]
    sine_table = jnp.sin(angles)[:, None, :]
    first_half = head_values[..., :half_width]
    second_half = head_values[..., half_width:]
    return jnp.concatenate(
        [
            first_half * cosine - second_half * sine_table,
            second_half * cosine + first_half * sine_table,
        ],
        axis=-1,
    )


def gathered_weights(hidden, gain, queries, key_value_weight, adapt_down, adapt_up, out_grad, doc_ids):
    tp_count = lax.axis_size("tp")
    row_count = hidden.shape[1]
    local_width = hidden.shape[2]
    head_dim = key_value_weight.shape[-1]
    kv_count = key_value_weight.shape[2]
    head_count = queries.shape[2]
    group_size = head_count // kv_count
    local_query = head_count * head_dim
    rank_size = adapt_down.shape[1]
    key_block = 1024
    full_rows, full_gain = (
        lax.all_gather(hidden, "tp", axis=2, tiled=True),
        lax.all_gather(gain, "tp", axis=1, tiled=True),
    )
    widened = full_rows[0].astype(jnp.float32)
    normalized_rows = (
        widened
        * lax.rsqrt(jnp.mean(widened * widened, axis=1, keepdims=True) + 1e-06)
        * full_gain[0].astype(jnp.float32)
    ).astype(jnp.bfloat16)
    kv_local = key_value_weight.reshape(1, key_value_weight.shape[1], kv_count * 2 * head_dim)
    keyval_raw = jnp.dot(
        normalized_rows,
        lax.all_gather(kv_local, "ctx", axis=1, tiled=True)[0],
        preferred_element_type=jnp.float32,
    )
    positions = lax.axis_index("ctx") * row_count + jnp.arange(row_count, dtype=jnp.int32)
    key_value_rows = keyval_raw.reshape(row_count, kv_count, 2, head_dim)
    rotated_keys = rotate(key_value_rows[:, :, 0], positions).astype(jnp.bfloat16)
    value_rows = key_value_rows[:, :, 1].astype(jnp.bfloat16)
    rotated_query = rotate(queries[0].astype(jnp.float32), positions).astype(jnp.bfloat16)
    stacked = (
        rotated_query.reshape(row_count, kv_count, group_size, head_dim)
        .transpose(1, 2, 0, 3)
        .reshape(kv_count, group_size * row_count, head_dim)
    )
    query_pos = jnp.tile(positions, group_size)
    query_doc = jnp.tile(doc_ids, group_size).astype(jnp.float32)
    score_scale = head_dim ** (-0.5)
    start_state = (
        jnp.full((kv_count, group_size * row_count), -1e30, jnp.float32),
        jnp.zeros((kv_count, group_size * row_count), jnp.float32),
        jnp.zeros((kv_count, group_size * row_count, head_dim), jnp.float32),
    )
    carried = start_state
    first_row = jnp.int32(0)
    piece_keys = lax.all_gather(rotated_keys, "ctx", axis=0, tiled=True)
    piece_values = lax.all_gather(value_rows, "ctx", axis=0, tiled=True)
    piece_docs = lax.all_gather(doc_ids.astype(jnp.bfloat16), "ctx", axis=0, tiled=True)
    key_total = piece_keys.shape[0]
    for block_start in range(0, key_total, key_block):
        block_stop = min(key_total, block_start + key_block)
        block_keys = piece_keys[block_start:block_stop]
        block_values = piece_values[block_start:block_stop]
        key_pos = first_row + block_start + jnp.arange(block_keys.shape[0], dtype=jnp.int32)
        key_doc = piece_docs[block_start:block_stop].astype(jnp.float32)
        running_top, running_sum, running_acc = carried
        scores = (
            jnp.einsum("gqd,kgd->gqk", stacked, block_keys, preferred_element_type=jnp.float32)
            * score_scale
        )
        allowed = (
            (key_pos[None, :] <= query_pos[:, None]) & (key_doc[None, :] == query_doc[:, None])
        )[None]
        scores = jnp.where(allowed, scores, -1e30)
        new_top = jnp.maximum(running_top, jnp.max(scores, axis=2))
        weights = jnp.where(allowed, jnp.exp(scores - new_top[:, :, None]), 0.0)
        shrink = jnp.exp(running_top - new_top)
        new_acc = running_acc * shrink[:, :, None] + jnp.einsum(
            "gqk,kgd->gqd",
            weights.astype(jnp.bfloat16),
            block_values,
            preferred_element_type=jnp.float32,
        )
        carried = (new_top, running_sum * shrink + jnp.sum(weights, axis=2), new_acc)
    final_top, final_sum, final_acc = carried
    attended = (
        (final_acc / final_sum[:, :, None])
        .reshape(kv_count, group_size, row_count, head_dim)
        .transpose(2, 0, 1, 3)
        .reshape(row_count, local_query)
        .astype(jnp.bfloat16)
    )
    low_part = jnp.dot(attended, adapt_down[0].T, preferred_element_type=jnp.float32)
    back_part = jnp.dot(out_grad[0], adapt_up[0].T, preferred_element_type=jnp.float32)
    low_sum, back_sum = lax.psum((low_part, back_part), "tp")
    low_rows = low_sum.astype(jnp.bfloat16)
    back_rows = back_sum.astype(jnp.bfloat16)
    adapter_rows = jnp.dot(low_rows, adapt_up[0], preferred_element_type=jnp.float32).astype(
        jnp.bfloat16
    )
    up_part = jnp.dot(low_rows.T, out_grad[0], preferred_element_type=jnp.float32)
    down_part = jnp.dot(back_rows.T, attended, preferred_element_type=jnp.float32)
    ceiling = 0.5 * math.sqrt(
        lax.axis_size("section") * rank_size * (local_query + local_width) * tp_count
    )
    up_total, down_total = (
        lax.psum(up_part.astype(jnp.bfloat16), "ctx").astype(jnp.float32),
        lax.psum(down_part.astype(jnp.bfloat16), "ctx").astype(jnp.float32),
    )
    local_squares = jnp.sum(up_total * up_total) + jnp.sum(down_total * down_total)
    squares = lax.psum(local_squares, ("section", "tp"))
    factor = jnp.minimum(1.0, ceiling / (jnp.sqrt(squares) + 1e-06))
    grad_up = up_total * factor
    grad_down = down_total * factor
    return (attended[None], adapter_rows[None], grad_down[None], grad_up[None])


F32, BF16 = jnp.float32, jnp.bfloat16
VMEM = pl.BlockSpec(memory_space=pltpu.VMEM)
ANYWHERE = pl.BlockSpec(memory_space=pl.ANY)
LIMIT = 16 * 1024 * 1024
LEVELS = (5, 5, 5, 4)


def swap(value, axis, distance):
    count = lax.axis_size(axis)
    return lax.ppermute(value, axis, [(i, i ^ distance) for i in range(count)])


def call(kernel, outs, *operands, flops=0, scratch=(), loose=(), loose_outs=()):
    shapes = [jax.ShapeDtypeStruct(shape, dtype) for shape, dtype in outs]
    moved = sum(math.prod(x.shape) * x.dtype.itemsize for x in (*operands, *shapes))
    return pl.pallas_call(
        kernel,
        out_shape=shapes,
        in_specs=[ANYWHERE if i in loose else VMEM for i in range(len(operands))],
        out_specs=[ANYWHERE if i in loose_outs else VMEM for i in range(len(shapes))],
        scratch_shapes=scratch,
        compiler_params=pltpu.CompilerParams(vmem_limit_bytes=LIMIT),
        cost_estimate=pl.CostEstimate(flops=flops, bytes_accessed=moved, transcendentals=0),
    )(*operands)


def times(left, right):
    return lax.dot_general(left, right, (((1,), (0,)), ((), ())), preferred_element_type=F32)


def times_transposed(left, right):
    return lax.dot_general(left, right, (((1,), (1,)), ((), ())), preferred_element_type=F32)


def transposed_times(left, right):
    return lax.dot_general(left, right, (((0,), (0,)), ((), ())), preferred_element_type=F32)


def distances():
    core = lax.axis_index("tp")
    return 0, jnp.where(core == 0, 1, 2), jnp.where(core == 0, 2, 1), 3


def norm_kernel(mine_ref, other_ref, gain_ref, gain_other_ref, *refs):
    outs, (held_ref, written) = refs[:4], refs[4:]
    width = outs[0].shape[1]
    place, core = lax.axis_index("ctx"), lax.axis_index("tp")
    mine, other = mine_ref[...].astype(F32), other_ref[...].astype(F32)
    squares = [jnp.sum(rows * rows, axis=1, keepdims=True) for rows in (mine, other)]
    scale = lax.rsqrt((squares[0] + squares[1]) / (4 * width) + 1e-06)
    copies = []
    for index in (3, 1, 2, 0):
        chip = place ^ distances()[index]
        columns = pl.ds(pl.multiple_of(chip % 2 * width, width), width)
        slot = outs[0] if index == 0 else held_ref.at[index - 1]

        def write(rows_ref, weights_ref, slot=slot, columns=columns):
            rows = rows_ref[:, columns].astype(F32) * scale
            slot[...] = (rows * weights_ref[:, columns].astype(F32)).astype(BF16)

        pl.when(chip // 2 == core)(functools.partial(write, mine_ref, gain_ref))
        pl.when(chip // 2 != core)(functools.partial(write, other_ref, gain_other_ref))
        if index:
            copies.append(pltpu.make_async_copy(slot, outs[index], written.at[index - 1]))
            copies[-1].start()
    for copy in copies:
        copy.wait()


def join_rows(mine_ref, other_ref, out_ref):
    count = mine_ref.shape[0]
    core = lax.axis_index("tp")
    out_ref[pl.ds(pl.multiple_of(core * count, count), count)] = mine_ref[...]
    out_ref[pl.ds(pl.multiple_of((1 - core) * count, count), count)] = other_ref[...]


def split_heads(value, head):
    count = value.shape[1] // (2 * head)
    pieces = [value[:, i * head : (i + 1) * head] for i in range(2 * count)]
    return jnp.concatenate(pieces[0::2], axis=1), jnp.concatenate(pieces[1::2], axis=1)


def pack(value, out_ref, head):
    keys, values = split_heads(value, head)
    store_packed(keys, values, out_ref)


def store_packed(keys, values, out_ref):
    rows, width = keys.shape
    high = keys.astype(BF16)
    wide = high.astype(F32)
    size = jnp.abs(wide)
    part = (keys - wide) * 256.0 / jnp.where(size > 0, size, 1.0)
    out_ref[:rows, :width] = high
    out_ref[:rows, width:] = values.astype(BF16)
    count = rows // len(LEVELS)
    code, weight = -250.0, 1.0
    for index, levels in enumerate(LEVELS):
        level = jnp.floor((part[index * count : (index + 1) * count] + 1.0) * (levels / 2))
        code = code + jnp.clip(level, 0.0, levels - 1.0) * weight
        weight *= levels
    code = jnp.concatenate([code[: count // 2], code[count // 2 :]], axis=1)
    out_ref[rows:] = code.astype(BF16)


def unpack(ref, rows):
    width = ref.shape[1] // 2
    wide = ref[:rows, :width].astype(F32)
    code = ref[rows:].astype(F32) + 250.0
    code = jnp.concatenate([code[:, :width], code[:, width:]], axis=0)
    parts, weight = [], math.prod(LEVELS)
    for levels in reversed(LEVELS):
        weight /= levels
        level = jnp.floor((code + 0.5) / weight)
        code = code - level * weight
        parts.append((level * 2.0 + 1.0) / levels - 1.0)
    part = jnp.concatenate(parts[::-1], axis=0)
    return wide + jnp.abs(wide) * part * (1.0 / 256.0), ref[:rows, width:].astype(F32)


def store_docs(docs, out_ref):
    rows = docs.shape[1]
    out_ref[rows:, :rows] = jnp.broadcast_to(docs, (16, rows)).astype(BF16)


def load_docs(ref):
    return ref[-16:, : ref.shape[0] - 16].astype(F32)[:1]


def own_kernel(
    head, even_ref, even_other_ref, weight_ref, own_ref, weight_out_ref, rows_ref, arrived
):
    copy = pltpu.make_async_copy(weight_ref, weight_out_ref, arrived)
    copy.start()
    join_rows(even_ref, even_other_ref, rows_ref)
    copy.wait()
    product = times(rows_ref[...], weight_out_ref[...])
    own_ref[...] = jnp.concatenate(split_heads(product, head), axis=1)


def far_kernel(head, got_ref, got_other_ref, weight_ref, sent_ref, rows_ref):
    join_rows(got_ref, got_other_ref, rows_ref)
    pack(times(rows_ref[...], weight_ref[...]), sent_ref, head)


def near_kernel(
    head,
    got_a_ref,
    got_a_other_ref,
    got_b_ref,
    got_b_other_ref,
    weight_ref,
    sent_a_ref,
    sent_b_ref,
    rows_ref,
):
    count = rows_ref.shape[0] // 2
    join_rows(got_a_ref, got_b_other_ref, rows_ref.at[:count])
    join_rows(got_b_ref, got_a_other_ref, rows_ref.at[count:])
    product = times(rows_ref[...], weight_ref[...])
    pack(product[:count], sent_a_ref, head)
    pack(product[count:], sent_b_ref, head)


def turn(value, cosine, sine):
    head = cosine.shape[1]
    pieces = []
    for i in range(value.shape[1] // head):
        piece = value[:, i * head : (i + 1) * head]
        pieces.append(piece * cosine + pltpu.roll(piece, head // 2, 1) * sine)
    return jnp.concatenate(pieces, axis=1)


def query_kernel(query_ref, cosine_ref, sine_ref, out_ref):
    rows, head = cosine_ref.shape
    for index in range(query_ref.shape[1] // head):
        piece = query_ref[:, index * head : (index + 1) * head].astype(F32)
        out_ref[index * rows : (index + 1) * rows] = turn(
            piece, cosine_ref[...], sine_ref[...]
        ).astype(BF16)


def accumulate_kernel(own_ref, got_ref, back_ref, back_other_ref, *refs):
    count = len(refs) // 2
    out_ref, back_out_ref = refs[count - 1 : count + 1]
    keys, values = unpack(got_ref, own_ref.shape[0])
    width = keys.shape[1]
    out_ref[:, :width] = own_ref[:, :width] + keys
    out_ref[:, width:] = own_ref[:, width:] + values
    back_out_ref[...] = (back_ref[...] + back_other_ref[...]).astype(BF16)
    for ref, copy_ref in zip(refs[: count - 1], refs[count + 1 :]):
        copy_ref[...] = ref[...]


def finish_kernel(own_ref, got_a_ref, got_b_ref, docs_ref, cosine_ref, sine_ref, out_ref):
    rows = own_ref.shape[0]
    width = own_ref.shape[1] // 2
    keys, values = own_ref[:, :width], own_ref[:, width:]
    for ref in (got_a_ref, got_b_ref):
        more_keys, more_values = unpack(ref, rows)
        keys, values = keys + more_keys, values + more_values
    out_ref[:rows, :width] = turn(keys, cosine_ref[...], sine_ref[...]).astype(BF16)
    out_ref[:rows, width:] = values.astype(BF16)
    store_docs(docs_ref[...], out_ref)


def allowed_pairs(own_docs, key_docs, distance):
    rows = own_docs.shape[1]
    place = lax.axis_index("ctx")
    query_docs = jnp.broadcast_to(own_docs, (rows, rows)).T
    query_at = place * rows + lax.broadcasted_iota(jnp.int32, (rows, rows), 0)
    key_at = (place ^ distance) * rows + lax.broadcasted_iota(jnp.int32, (rows, rows), 1)
    return (key_at <= query_at) & (key_docs == query_docs)


def attention_kernel(
    head,
    query_ref,
    block_0_ref,
    block_a_ref,
    block_b_ref,
    block_c_ref,
    down_ref,
    back_ref,
    out_ref,
    low_ref,
    grad_ref,
    mixed_ref,
    written,
):
    rows = block_0_ref.shape[0] - 16
    width = block_0_ref.shape[1] // 2
    blocks = (block_0_ref, block_a_ref, block_b_ref, block_c_ref)
    keys = jnp.concatenate([ref[:rows, :width] for ref in blocks], axis=0)
    values = jnp.concatenate([ref[:rows, width:] for ref in blocks], axis=0)
    own_docs = load_docs(block_0_ref)
    allowed = jnp.concatenate(
        [allowed_pairs(own_docs, load_docs(ref), d) for d, ref in zip(distances(), blocks)], axis=1
    )
    scale = head ** (-0.5) * math.log2(math.e)
    ones = jnp.ones((len(blocks) * rows, head), BF16)
    excluded = -1e30 * head**0.5
    groups = width // head
    pairs = query_ref.shape[0] // (2 * rows)
    copies = []
    for pair in range(pairs):
        shared = slice(pair * groups // pairs * head, (pair * groups // pairs + 1) * head)
        scores = times_transposed(
            query_ref[2 * pair * rows : 2 * (pair + 1) * rows], keys[:, shared]
        ).reshape(2, rows, keys.shape[0])
        scores = jnp.where(allowed[None], scores, excluded).reshape(2 * rows, keys.shape[0])
        weights = jnp.exp2((scores - jnp.max(scores, axis=1, keepdims=True)) * scale)
        mixed = times(
            weights.astype(BF16), jnp.concatenate([values[:, shared], ones], axis=1)
        )
        mixed = (mixed[:, :head] / mixed[:, head:]).astype(BF16)
        columns = slice(2 * pair * head, 2 * (pair + 1) * head)
        mixed_ref[:, columns] = jnp.concatenate([mixed[:rows], mixed[rows:]], axis=1)
        copies.append(
            pltpu.make_async_copy(
                mixed_ref.at[:, columns], out_ref.at[:, columns], written.at[pair]
            )
        )
        copies[-1].start()
    attended = mixed_ref[...]
    low_ref[...] = times_transposed(attended, down_ref[...])
    grad_ref[...] = transposed_times(back_ref[...], attended)
    for copy in copies:
        copy.wait()


def back_kernel(grad_ref, up_ref, out_ref):
    out_ref[...] = times_transposed(grad_ref[...], up_ref[...])


def grads_kernel(low_ref, low_other_ref, grad_ref, down_ref, own_ref, sent_ref):
    low = (low_ref[...] + low_other_ref[...]).astype(BF16)
    parity = lax.axis_index("ctx") % 2
    up_step, down_step = grad_ref.shape[1] // 2, down_ref.shape[1] // 2
    for index, out in ((1 - parity, sent_ref), (parity, own_ref)):
        columns = pl.ds(pl.multiple_of(index * up_step, up_step), up_step)
        out[:, :up_step] = transposed_times(low, grad_ref[:, columns]).astype(out.dtype)
        columns = pl.ds(pl.multiple_of(index * down_step, down_step), down_step)
        out[:, up_step:] = down_ref[:, columns].astype(out.dtype)


def adapter_kernel(low_ref, low_other_ref, up_ref, out_ref):
    low = (low_ref[...] + low_other_ref[...]).astype(BF16)
    out_ref[...] = times(low, up_ref[...]).astype(BF16)


def add_kernel(own_ref, got_ref, out_ref):
    out_ref[...] = (own_ref[...].astype(F32) + got_ref[...].astype(F32)).astype(BF16)


def total_kernel(own_ref, got_ref, out_ref, square_ref):
    add_kernel(own_ref, got_ref, out_ref)
    squares = jnp.sum(jnp.square(out_ref[...].astype(F32))).reshape(1, 1)
    square_ref[...] = jnp.broadcast_to(squares, square_ref.shape)


def clip_kernel(ceiling, square_ref, other_ref, own_ref, got_ref, up_ref, down_ref):
    squares = square_ref[:1, :1] + other_ref[:1, :1]
    factor = jnp.minimum(1.0, ceiling / (jnp.sqrt(squares) + 1e-06))
    parity = lax.axis_index("ctx") % 2
    up_step, down_step = up_ref.shape[1] // 2, down_ref.shape[1] // 2
    for index, ref in ((parity, own_ref), (1 - parity, got_ref)):
        columns = pl.ds(pl.multiple_of(index * up_step, up_step), up_step)
        up_ref[:, columns] = ref[:, :up_step].astype(F32) * factor
        columns = pl.ds(pl.multiple_of(index * down_step, down_step), down_step)
        down_ref[:, columns] = ref[:, up_step:].astype(F32) * factor


def split_model_width(
    hidden, gain, queries, key_value_weight, adapt_down, adapt_up, out_grad, doc_ids
):
    place = lax.axis_index("ctx")
    rows = hidden.shape[1]
    local_width = hidden.shape[2]
    slice_width = key_value_weight.shape[1]
    kv_count, head = key_value_weight.shape[2], key_value_weight.shape[-1]
    head_count = queries.shape[2]
    local_query = head_count * head
    rank = adapt_down.shape[1]
    kv_width = kv_count * 2 * head

    half = rows // 2
    core = lax.axis_index("tp")
    mine = lax.dynamic_slice_in_dim(hidden[0], core * half, half, 0)
    theirs = lax.dynamic_slice_in_dim(hidden[0], (1 - core) * half, half, 0)
    part = ((half, slice_width), BF16)
    slices = call(
        norm_kernel,
        [part] * 4,
        mine,
        swap(theirs, "tp", 1),
        gain,
        swap(gain, "tp", 1),
        scratch=[pltpu.VMEM((3, half, slice_width), BF16), pltpu.SemaphoreType.DMA((3,))],
        loose_outs=(1, 2, 3),
    )

    def send_a(value):
        return lax.ppermute(
            value, ("ctx", "tp"), [(2 * a + t, 2 * (a ^ (2 if t else 1)) + t) for a in range(4) for t in range(2)]
        )

    def send_b(value):
        return lax.ppermute(
            value, ("ctx", "tp"), [(2 * a + t, 2 * (a ^ (1 if t else 2)) + t) for a in range(4) for t in range(2)]
        )

    even, slice_a, slice_b, slice_c = slices
    got_a, got_b, got_c = send_a(slice_a), send_b(slice_b), swap(slice_c, "ctx", 3)
    part_flops = 2 * rows * slice_width * kv_width
    packed = ((rows + rows // 8, kv_width), BF16)
    summed = ((rows, kv_width), F32)
    final = ((rows + 16, kv_width), BF16)

    def step(function, *operands):
        shapes = jax.eval_shape(function, *operands)
        return lax.cond(
            place < 4,
            function,
            lambda *_: jax.tree.map(lambda x: jnp.zeros(x.shape, x.dtype), shapes),
            *operands,
        )

    def prepare(key_value_weight):
        return key_value_weight[0].reshape(slice_width, kv_width)

    weight = step(prepare, key_value_weight)

    def prepare_attention(queries, out_grad, adapt_up, doc_ids, weight):
        docs = doc_ids.astype(F32).reshape(1, rows)
        freqs = 1000000.0 ** (-jnp.arange(head // 2, dtype=F32) * 2.0 / head)
        positions = place * rows + jnp.arange(rows, dtype=jnp.int32)
        angles = positions.astype(F32)[:, None] * freqs
        cosine, sine = jnp.cos(angles), jnp.sin(angles)
        cosine = jnp.concatenate([cosine, cosine], axis=1)
        sine = jnp.concatenate([-sine, sine], axis=1)
        (query,) = call(
            query_kernel,
            [((head_count * rows, head), BF16)],
            queries[0].reshape(rows, local_query),
            cosine,
            sine,
        )
        (back_part,) = call(
            back_kernel,
            [((rows, rank), F32)],
            out_grad[0],
            adapt_up[0],
            flops=2 * rows * local_width * rank,
        )
        return docs, cosine, sine, query, back_part, swap(back_part, "tp", 1)

    docs, cosine, sine, query, back_part, back_other = step(
        prepare_attention, queries, out_grad, adapt_up, doc_ids, weight
    )
    def swap_own(even):
        return swap(even, "tp", 1)

    even_other = step(swap_own, even)
    part_0, weight_near = call(
        functools.partial(own_kernel, head),
        [summed, (weight.shape, BF16)],
        even,
        even_other,
        weight,
        flops=part_flops,
        scratch=[pltpu.VMEM((rows, slice_width), BF16), pltpu.SemaphoreType.DMA],
        loose=(2,),
    )
    got_c, part_0, docs = lax.optimization_barrier((got_c, part_0, docs))

    def far_parts(got_c, weight):
        return call(
            functools.partial(far_kernel, head),
            [packed],
            got_c,
            swap(got_c, "tp", 1),
            weight,
            flops=part_flops,
            scratch=[pltpu.VMEM((rows, slice_width), BF16)],
        )

    (sent_c,) = step(far_parts, got_c, weight)
    arrived_c = swap(sent_c, "ctx", 3)
    got_a, got_b, sent_c = lax.optimization_barrier((got_a, got_b, sent_c))
    sent_a, sent_b = call(
        functools.partial(near_kernel, head),
        [packed, packed],
        got_a,
        swap(got_a, "tp", 1),
        got_b,
        swap(got_b, "tp", 1),
        weight_near,
        flops=2 * part_flops,
        scratch=[pltpu.VMEM((2 * rows, slice_width), BF16)],
    )
    arrived_a, arrived_b = send_a(sent_a), send_b(sent_b)
    part_0, back_rows, docs, cosine, sine, staged_down = call(
        accumulate_kernel,
        [
            summed,
            ((rows, rank), BF16),
            ((1, rows), F32),
            ((rows, head), F32),
            ((rows, head), F32),
            ((rank, local_query), BF16),
        ],
        part_0,
        arrived_c,
        back_part,
        back_other,
        docs,
        cosine,
        sine,
        adapt_down[0],
    )
    arrived_a, arrived_b, part_0 = lax.optimization_barrier((arrived_a, arrived_b, part_0))
    (block_0,) = call(finish_kernel, [final], part_0, arrived_a, arrived_b, docs, cosine, sine)

    attended, low_part, down_part = call(
        functools.partial(attention_kernel, head),
        [((rows, local_query), BF16), ((rows, rank), F32), ((rank, local_query), F32)],
        query,
        block_0,
        send_a(block_0),
        send_b(block_0),
        swap(block_0, "ctx", 3),
        staged_down,
        back_rows,
        flops=16 * rows * rows * local_query,
        scratch=[
            pltpu.VMEM((rows, local_query), BF16),
            pltpu.SemaphoreType.DMA((head_count // 2,)),
        ],
        loose_outs=(0,),
    )
    low_other = swap(low_part, "tp", 1)
    piece = (rank, (local_width + local_query) // 2)
    own, sent = call(
        grads_kernel,
        [(piece, F32), (piece, BF16)],
        low_part,
        low_other,
        out_grad[0],
        down_part,
        flops=2 * rows * rank * local_width,
    )
    (adapter_rows,) = call(
        adapter_kernel,
        [((rows, local_width), BF16)],
        low_part,
        low_other,
        adapt_up[0],
        flops=2 * rows * rank * local_width,
    )
    got_sum, adapter_rows = lax.optimization_barrier((swap(sent, "ctx", 1), adapter_rows))
    (pair_sum,) = call(add_kernel, [(piece, BF16)], own, got_sum)
    total, squares = call(
        total_kernel, [(piece, BF16), ((8, 128), F32)], pair_sum, swap(pair_sum, "ctx", 2)
    )
    total_other = swap(total, "ctx", 1)
    squares = squares + swap(squares, "tp", 1)
    beside = lax.ppermute(
        squares,
        ("section", "tp"),
        [(2 * i + t, 2 * (i ^ (2 if t else 1)) + t) for i in range(4) for t in range(2)],
    )
    across = swap(squares, "section", 3)
    squares = jnp.where(core == 0, squares + across + beside, beside)
    squares = squares + swap(squares, "ctx", 1)
    ceiling = 0.5 * math.sqrt(lax.axis_size("section") * rank * (local_query + local_width) * 2)
    grad_up, grad_down = call(
        functools.partial(clip_kernel, ceiling),
        [((rank, local_width), F32), ((rank, local_query), F32)],
        squares,
        swap(squares, "tp", 1),
        total,
        total_other,
    )
    return (attended[None], adapter_rows[None], grad_down[None], grad_up[None])


def per_device(*arrays):
    if lax.axis_size("ctx") == 4 and lax.axis_size("tp") == 2 and lax.axis_size("section") == 4:
        return split_model_width(*arrays)
    return gathered_weights(*arrays)


def solution(mesh):
    return jax.shard_map(
        per_device,
        mesh=mesh,
        in_specs=(
            P("section", "ctx", "tp"),
            P("section", "tp"),
            P("section", "ctx", "tp", None),
            P("section", "ctx", "tp", None, None),
            P("section", None, "tp"),
            P("section", None, "tp"),
            P("section", "ctx", "tp"),
            P("ctx"),
        ),
        out_specs=(
            P("section", "ctx", "tp"),
            P("section", "ctx", "tp"),
            P("section", None, "tp"),
            P("section", None, "tp"),
        ),
        check_vma=False,
    )
```

```python
import functools
import math

import jax
import jax.numpy as jnp
from jax import lax
from jax.experimental import pallas as pl
from jax.experimental.pallas import tpu as pltpu
from jax.sharding import PartitionSpec as P


def rotate(head_values, positions):
    half_width = head_values.shape[-1] // 2
    freqs = 1000000.0 ** (-jnp.arange(half_width, dtype=jnp.float32) * 2.0 / head_values.shape[-1])
    angles = positions.astype(jnp.float32)[:, None] * freqs[None, :]
    cosine = jnp.cos(angles)[:, None, :]
    sine_table = jnp.sin(angles)[:, None, :]
    first_half = head_values[..., :half_width]
    second_half = head_values[..., half_width:]
    return jnp.concatenate(
        [
            first_half * cosine - second_half * sine_table,
            second_half * cosine + first_half * sine_table,
        ],
        axis=-1,
    )


def gathered_weights(hidden, gain, queries, key_value_weight, adapt_down, adapt_up, out_grad, doc_ids):
    tp_count = lax.axis_size("tp")
    row_count = hidden.shape[1]
    local_width = hidden.shape[2]
    head_dim = key_value_weight.shape[-1]
    kv_count = key_value_weight.shape[2]
    head_count = queries.shape[2]
    group_size = head_count // kv_count
    local_query = head_count * head_dim
    rank_size = adapt_down.shape[1]
    key_block = 1024
    full_rows, full_gain = (
        lax.all_gather(hidden, "tp", axis=2, tiled=True),
        lax.all_gather(gain, "tp", axis=1, tiled=True),
    )
    widened = full_rows[0].astype(jnp.float32)
    normalized_rows = (
        widened
        * lax.rsqrt(jnp.mean(widened * widened, axis=1, keepdims=True) + 1e-06)
        * full_gain[0].astype(jnp.float32)
    ).astype(jnp.bfloat16)
    kv_local = key_value_weight.reshape(1, key_value_weight.shape[1], kv_count * 2 * head_dim)
    keyval_raw = jnp.dot(
        normalized_rows,
        lax.all_gather(kv_local, "ctx", axis=1, tiled=True)[0],
        preferred_element_type=jnp.float32,
    )
    positions = lax.axis_index("ctx") * row_count + jnp.arange(row_count, dtype=jnp.int32)
    key_value_rows = keyval_raw.reshape(row_count, kv_count, 2, head_dim)
    rotated_keys = rotate(key_value_rows[:, :, 0], positions).astype(jnp.bfloat16)
    value_rows = key_value_rows[:, :, 1].astype(jnp.bfloat16)
    rotated_query = rotate(queries[0].astype(jnp.float32), positions).astype(jnp.bfloat16)
    stacked = (
        rotated_query.reshape(row_count, kv_count, group_size, head_dim)
        .transpose(1, 2, 0, 3)
        .reshape(kv_count, group_size * row_count, head_dim)
    )
    query_pos = jnp.tile(positions, group_size)
    query_doc = jnp.tile(doc_ids, group_size).astype(jnp.float32)
    score_scale = head_dim ** (-0.5)
    start_state = (
        jnp.full((kv_count, group_size * row_count), -1e30, jnp.float32),
        jnp.zeros((kv_count, group_size * row_count), jnp.float32),
        jnp.zeros((kv_count, group_size * row_count, head_dim), jnp.float32),
    )
    carried = start_state
    first_row = jnp.int32(0)
    piece_keys = lax.all_gather(rotated_keys, "ctx", axis=0, tiled=True)
    piece_values = lax.all_gather(value_rows, "ctx", axis=0, tiled=True)
    piece_docs = lax.all_gather(doc_ids.astype(jnp.bfloat16), "ctx", axis=0, tiled=True)
    key_total = piece_keys.shape[0]
    for block_start in range(0, key_total, key_block):
        block_stop = min(key_total, block_start + key_block)
        block_keys = piece_keys[block_start:block_stop]
        block_values = piece_values[block_start:block_stop]
        key_pos = first_row + block_start + jnp.arange(block_keys.shape[0], dtype=jnp.int32)
        key_doc = piece_docs[block_start:block_stop].astype(jnp.float32)
        running_top, running_sum, running_acc = carried
        scores = (
            jnp.einsum("gqd,kgd->gqk", stacked, block_keys, preferred_element_type=jnp.float32)
            * score_scale
        )
        allowed = (
            (key_pos[None, :] <= query_pos[:, None]) & (key_doc[None, :] == query_doc[:, None])
        )[None]
        scores = jnp.where(allowed, scores, -1e30)
        new_top = jnp.maximum(running_top, jnp.max(scores, axis=2))
        weights = jnp.where(allowed, jnp.exp(scores - new_top[:, :, None]), 0.0)
        shrink = jnp.exp(running_top - new_top)
        new_acc = running_acc * shrink[:, :, None] + jnp.einsum(
            "gqk,kgd->gqd",
            weights.astype(jnp.bfloat16),
            block_values,
            preferred_element_type=jnp.float32,
        )
        carried = (new_top, running_sum * shrink + jnp.sum(weights, axis=2), new_acc)
    final_top, final_sum, final_acc = carried
    attended = (
        (final_acc / final_sum[:, :, None])
        .reshape(kv_count, group_size, row_count, head_dim)
        .transpose(2, 0, 1, 3)
        .reshape(row_count, local_query)
        .astype(jnp.bfloat16)
    )
    low_part = jnp.dot(attended, adapt_down[0].T, preferred_element_type=jnp.float32)
    back_part = jnp.dot(out_grad[0], adapt_up[0].T, preferred_element_type=jnp.float32)
    low_sum, back_sum = lax.psum((low_part, back_part), "tp")
    low_rows = low_sum.astype(jnp.bfloat16)
    back_rows = back_sum.astype(jnp.bfloat16)
    adapter_rows = jnp.dot(low_rows, adapt_up[0], preferred_element_type=jnp.float32).astype(
        jnp.bfloat16
    )
    up_part = jnp.dot(low_rows.T, out_grad[0], preferred_element_type=jnp.float32)
    down_part = jnp.dot(back_rows.T, attended, preferred_element_type=jnp.float32)
    ceiling = 0.5 * math.sqrt(
        lax.axis_size("section") * rank_size * (local_query + local_width) * tp_count
    )
    up_total, down_total = (
        lax.psum(up_part.astype(jnp.bfloat16), "ctx").astype(jnp.float32),
        lax.psum(down_part.astype(jnp.bfloat16), "ctx").astype(jnp.float32),
    )
    local_squares = jnp.sum(up_total * up_total) + jnp.sum(down_total * down_total)
    squares = lax.psum(local_squares, ("section", "tp"))
    factor = jnp.minimum(1.0, ceiling / (jnp.sqrt(squares) + 1e-06))
    grad_up = up_total * factor
    grad_down = down_total * factor
    return (attended[None], adapter_rows[None], grad_down[None], grad_up[None])


F32, BF16 = jnp.float32, jnp.bfloat16
VMEM = pl.BlockSpec(memory_space=pltpu.VMEM)
ANYWHERE = pl.BlockSpec(memory_space=pl.ANY)
LIMIT = 16 * 1024 * 1024
LEVELS = (5, 5, 5, 4)


def swap(value, axis, distance):
    count = lax.axis_size(axis)
    return lax.ppermute(value, axis, [(i, i ^ distance) for i in range(count)])


def call(kernel, outs, *operands, flops=0, scratch=(), loose=(), loose_outs=()):
    shapes = [jax.ShapeDtypeStruct(shape, dtype) for shape, dtype in outs]
    moved = sum(math.prod(x.shape) * x.dtype.itemsize for x in (*operands, *shapes))
    return pl.pallas_call(
        kernel,
        out_shape=shapes,
        in_specs=[ANYWHERE if i in loose else VMEM for i in range(len(operands))],
        out_specs=[ANYWHERE if i in loose_outs else VMEM for i in range(len(shapes))],
        scratch_shapes=scratch,
        compiler_params=pltpu.CompilerParams(vmem_limit_bytes=LIMIT),
        cost_estimate=pl.CostEstimate(flops=flops, bytes_accessed=moved, transcendentals=0),
    )(*operands)


def times(left, right):
    return lax.dot_general(left, right, (((1,), (0,)), ((), ())), preferred_element_type=F32)


def times_transposed(left, right):
    return lax.dot_general(left, right, (((1,), (1,)), ((), ())), preferred_element_type=F32)


def transposed_times(left, right):
    return lax.dot_general(left, right, (((0,), (0,)), ((), ())), preferred_element_type=F32)


def distances():
    core = lax.axis_index("tp")
    return 0, jnp.where(core == 0, 1, 2), jnp.where(core == 0, 2, 1), 3


def norm_kernel(mine_ref, other_ref, gain_ref, gain_other_ref, *refs):
    outs, (held_ref, written) = refs[:4], refs[4:]
    width = outs[0].shape[1]
    place, core = lax.axis_index("ctx"), lax.axis_index("tp")
    mine, other = mine_ref[...].astype(F32), other_ref[...].astype(F32)
    squares = [jnp.sum(rows * rows, axis=1, keepdims=True) for rows in (mine, other)]
    scale = lax.rsqrt((squares[0] + squares[1]) / (4 * width) + 1e-06)
    copies = []
    for index in (3, 1, 2, 0):
        chip = place ^ distances()[index]
        columns = pl.ds(pl.multiple_of(chip % 2 * width, width), width)
        slot = outs[0] if index == 0 else held_ref.at[index - 1]

        def write(rows_ref, weights_ref, slot=slot, columns=columns):
            rows = rows_ref[:, columns].astype(F32) * scale
            slot[...] = (rows * weights_ref[:, columns].astype(F32)).astype(BF16)

        pl.when(chip // 2 == core)(functools.partial(write, mine_ref, gain_ref))
        pl.when(chip // 2 != core)(functools.partial(write, other_ref, gain_other_ref))
        if index:
            copies.append(pltpu.make_async_copy(slot, outs[index], written.at[index - 1]))
            copies[-1].start()
    for copy in copies:
        copy.wait()


def join_rows(mine_ref, other_ref, out_ref):
    count = mine_ref.shape[0]
    core = lax.axis_index("tp")
    out_ref[pl.ds(pl.multiple_of(core * count, count), count)] = mine_ref[...]
    out_ref[pl.ds(pl.multiple_of((1 - core) * count, count), count)] = other_ref[...]


def split_heads(value, head):
    count = value.shape[1] // (2 * head)
    pieces = [value[:, i * head : (i + 1) * head] for i in range(2 * count)]
    return jnp.concatenate(pieces[0::2], axis=1), jnp.concatenate(pieces[1::2], axis=1)


def pack(value, out_ref, head):
    keys, values = split_heads(value, head)
    store_packed(keys, values, out_ref)


def store_packed(keys, values, out_ref):
    rows, width = keys.shape
    high = keys.astype(BF16)
    wide = high.astype(F32)
    size = jnp.abs(wide)
    part = (keys - wide) * 256.0 / jnp.where(size > 0, size, 1.0)
    out_ref[:rows, :width] = high
    out_ref[:rows, width:] = values.astype(BF16)
    count = rows // len(LEVELS)
    code, weight = -250.0, 1.0
    for index, levels in enumerate(LEVELS):
        level = jnp.floor((part[index * count : (index + 1) * count] + 1.0) * (levels / 2))
        code = code + jnp.clip(level, 0.0, levels - 1.0) * weight
        weight *= levels
    code = jnp.concatenate([code[: count // 2], code[count // 2 :]], axis=1)
    out_ref[rows:] = code.astype(BF16)


def unpack(ref, rows):
    width = ref.shape[1] // 2
    wide = ref[:rows, :width].astype(F32)
    code = ref[rows:].astype(F32) + 250.0
    code = jnp.concatenate([code[:, :width], code[:, width:]], axis=0)
    parts, weight = [], math.prod(LEVELS)
    for levels in reversed(LEVELS):
        weight /= levels
        level = jnp.floor((code + 0.5) / weight)
        code = code - level * weight
        parts.append((level * 2.0 + 1.0) / levels - 1.0)
    part = jnp.concatenate(parts[::-1], axis=0)
    return wide + jnp.abs(wide) * part * (1.0 / 256.0), ref[:rows, width:].astype(F32)


def store_docs(docs, out_ref):
    rows = docs.shape[1]
    out_ref[rows:, :rows] = jnp.broadcast_to(docs, (16, rows)).astype(BF16)


def load_docs(ref):
    return ref[-16:, : ref.shape[0] - 16].astype(F32)[:1]


def own_kernel(
    head, even_ref, even_other_ref, weight_ref, own_ref, weight_out_ref, rows_ref, arrived
):
    copy = pltpu.make_async_copy(weight_ref, weight_out_ref, arrived)
    copy.start()
    join_rows(even_ref, even_other_ref, rows_ref)
    copy.wait()
    product = times(rows_ref[...], weight_out_ref[...])
    own_ref[...] = jnp.concatenate(split_heads(product, head), axis=1)


def far_kernel(head, got_ref, got_other_ref, weight_ref, sent_ref, rows_ref):
    join_rows(got_ref, got_other_ref, rows_ref)
    pack(times(rows_ref[...], weight_ref[...]), sent_ref, head)


def near_kernel(
    head,
    got_a_ref,
    got_a_other_ref,
    got_b_ref,
    got_b_other_ref,
    weight_ref,
    sent_a_ref,
    sent_b_ref,
    rows_ref,
):
    count = rows_ref.shape[0] // 2
    join_rows(got_a_ref, got_b_other_ref, rows_ref.at[:count])
    join_rows(got_b_ref, got_a_other_ref, rows_ref.at[count:])
    product = times(rows_ref[...], weight_ref[...])
    pack(product[:count], sent_a_ref, head)
    pack(product[count:], sent_b_ref, head)


def turn(value, cosine, sine):
    head = cosine.shape[1]
    pieces = []
    for i in range(value.shape[1] // head):
        piece = value[:, i * head : (i + 1) * head]
        pieces.append(piece * cosine + pltpu.roll(piece, head // 2, 1) * sine)
    return jnp.concatenate(pieces, axis=1)


def query_kernel(query_ref, cosine_ref, sine_ref, out_ref):
    rows, head = cosine_ref.shape
    for index in range(query_ref.shape[1] // head):
        piece = query_ref[:, index * head : (index + 1) * head].astype(F32)
        out_ref[index * rows : (index + 1) * rows] = turn(
            piece, cosine_ref[...], sine_ref[...]
        ).astype(BF16)


def accumulate_kernel(own_ref, got_ref, back_ref, back_other_ref, *refs):
    count = len(refs) // 2
    out_ref, back_out_ref = refs[count - 1 : count + 1]
    keys, values = unpack(got_ref, own_ref.shape[0])
    width = keys.shape[1]
    out_ref[:, :width] = own_ref[:, :width] + keys
    out_ref[:, width:] = own_ref[:, width:] + values
    back_out_ref[...] = (back_ref[...] + back_other_ref[...]).astype(BF16)
    for ref, copy_ref in zip(refs[: count - 1], refs[count + 1 :]):
        copy_ref[...] = ref[...]


def finish_kernel(own_ref, got_a_ref, got_b_ref, docs_ref, cosine_ref, sine_ref, out_ref):
    rows = own_ref.shape[0]
    width = own_ref.shape[1] // 2
    keys, values = own_ref[:, :width], own_ref[:, width:]
    for ref in (got_a_ref, got_b_ref):
        more_keys, more_values = unpack(ref, rows)
        keys, values = keys + more_keys, values + more_values
    out_ref[:rows, :width] = turn(keys, cosine_ref[...], sine_ref[...]).astype(BF16)
    out_ref[:rows, width:] = values.astype(BF16)
    store_docs(docs_ref[...], out_ref)


def allowed_pairs(own_docs, key_docs, distance):
    rows = own_docs.shape[1]
    place = lax.axis_index("ctx")
    query_docs = jnp.broadcast_to(own_docs, (rows, rows)).T
    query_at = place * rows + lax.broadcasted_iota(jnp.int32, (rows, rows), 0)
    key_at = (place ^ distance) * rows + lax.broadcasted_iota(jnp.int32, (rows, rows), 1)
    return (key_at <= query_at) & (key_docs == query_docs)


def attention_kernel(
    head,
    query_ref,
    block_0_ref,
    block_a_ref,
    block_b_ref,
    block_c_ref,
    down_ref,
    back_ref,
    out_ref,
    low_ref,
    grad_ref,
    mixed_ref,
    written,
):
    rows = block_0_ref.shape[0] - 16
    width = block_0_ref.shape[1] // 2
    blocks = (block_0_ref, block_a_ref, block_b_ref, block_c_ref)
    keys = jnp.concatenate([ref[:rows, :width] for ref in blocks], axis=0)
    values = jnp.concatenate([ref[:rows, width:] for ref in blocks], axis=0)
    own_docs = load_docs(block_0_ref)
    allowed = jnp.concatenate(
        [allowed_pairs(own_docs, load_docs(ref), d) for d, ref in zip(distances(), blocks)], axis=1
    )
    scale = head ** (-0.5) * math.log2(math.e)
    ones = jnp.ones((len(blocks) * rows, head), BF16)
    excluded = -1e30 * head**0.5
    groups = width // head
    pairs = query_ref.shape[0] // (2 * rows)
    copies = []
    for pair in range(pairs):
        shared = slice(pair * groups // pairs * head, (pair * groups // pairs + 1) * head)
        scores = times_transposed(
            query_ref[2 * pair * rows : 2 * (pair + 1) * rows], keys[:, shared]
        ).reshape(2, rows, keys.shape[0])
        scores = jnp.where(allowed[None], scores, excluded).reshape(2 * rows, keys.shape[0])
        weights = jnp.exp2((scores - jnp.max(scores, axis=1, keepdims=True)) * scale)
        mixed = times(
            weights.astype(BF16), jnp.concatenate([values[:, shared], ones], axis=1)
        )
        mixed = (mixed[:, :head] / mixed[:, head:]).astype(BF16)
        columns = slice(2 * pair * head, 2 * (pair + 1) * head)
        mixed_ref[:, columns] = jnp.concatenate([mixed[:rows], mixed[rows:]], axis=1)
        copies.append(
            pltpu.make_async_copy(
                mixed_ref.at[:, columns], out_ref.at[:, columns], written.at[pair]
            )
        )
        copies[-1].start()
    attended = mixed_ref[...]
    low_ref[...] = times_transposed(attended, down_ref[...])
    grad_ref[...] = transposed_times(back_ref[...], attended)
    for copy in copies:
        copy.wait()


def back_kernel(grad_ref, up_ref, out_ref):
    out_ref[...] = times_transposed(grad_ref[...], up_ref[...])


def grads_kernel(low_ref, low_other_ref, grad_ref, down_ref, own_ref, sent_ref):
    low = (low_ref[...] + low_other_ref[...]).astype(BF16)
    parity = lax.axis_index("ctx") % 2
    up_step, down_step = grad_ref.shape[1] // 2, down_ref.shape[1] // 2
    for index, out in ((1 - parity, sent_ref), (parity, own_ref)):
        columns = pl.ds(pl.multiple_of(index * up_step, up_step), up_step)
        out[:, :up_step] = transposed_times(low, grad_ref[:, columns]).astype(out.dtype)
        columns = pl.ds(pl.multiple_of(index * down_step, down_step), down_step)
        out[:, up_step:] = down_ref[:, columns].astype(out.dtype)


def adapter_kernel(low_ref, low_other_ref, up_ref, out_ref):
    low = (low_ref[...] + low_other_ref[...]).astype(BF16)
    out_ref[...] = times(low, up_ref[...]).astype(BF16)


def add_kernel(own_ref, got_ref, out_ref):
    out_ref[...] = (own_ref[...].astype(F32) + got_ref[...].astype(F32)).astype(BF16)


def total_kernel(own_ref, got_ref, out_ref, square_ref):
    add_kernel(own_ref, got_ref, out_ref)
    squares = jnp.sum(jnp.square(out_ref[...].astype(F32))).reshape(1, 1)
    square_ref[...] = jnp.broadcast_to(squares, square_ref.shape)


def clip_kernel(ceiling, square_ref, own_ref, got_ref, up_ref, down_ref):
    squares = square_ref[:1, :1]
    factor = jnp.minimum(1.0, ceiling / (jnp.sqrt(squares) + 1e-06))
    parity = lax.axis_index("ctx") % 2
    up_step, down_step = up_ref.shape[1] // 2, down_ref.shape[1] // 2
    for index, ref in ((parity, own_ref), (1 - parity, got_ref)):
        columns = pl.ds(pl.multiple_of(index * up_step, up_step), up_step)
        up_ref[:, columns] = ref[:, :up_step].astype(F32) * factor
        columns = pl.ds(pl.multiple_of(index * down_step, down_step), down_step)
        down_ref[:, columns] = ref[:, up_step:].astype(F32) * factor


def split_model_width(
    hidden, gain, queries, key_value_weight, adapt_down, adapt_up, out_grad, doc_ids
):
    place = lax.axis_index("ctx")
    rows = hidden.shape[1]
    local_width = hidden.shape[2]
    slice_width = key_value_weight.shape[1]
    kv_count, head = key_value_weight.shape[2], key_value_weight.shape[-1]
    head_count = queries.shape[2]
    local_query = head_count * head
    rank = adapt_down.shape[1]
    kv_width = kv_count * 2 * head

    half = rows // 2
    core = lax.axis_index("tp")
    mine = lax.dynamic_slice_in_dim(hidden[0], core * half, half, 0)
    theirs = lax.dynamic_slice_in_dim(hidden[0], (1 - core) * half, half, 0)
    part = ((half, slice_width), BF16)
    slices = call(
        norm_kernel,
        [part] * 4,
        mine,
        swap(theirs, "tp", 1),
        gain,
        swap(gain, "tp", 1),
        scratch=[pltpu.VMEM((3, half, slice_width), BF16), pltpu.SemaphoreType.DMA((3,))],
        loose_outs=(1, 2, 3),
    )

    def send_a(value):
        return lax.ppermute(
            value, ("ctx", "tp"), [(2 * a + t, 2 * (a ^ (2 if t else 1)) + t) for a in range(4) for t in range(2)]
        )

    def send_b(value):
        return lax.ppermute(
            value, ("ctx", "tp"), [(2 * a + t, 2 * (a ^ (1 if t else 2)) + t) for a in range(4) for t in range(2)]
        )

    even, slice_a, slice_b, slice_c = slices
    got_a, got_b, got_c = send_a(slice_a), send_b(slice_b), swap(slice_c, "ctx", 3)
    part_flops = 2 * rows * slice_width * kv_width
    packed = ((rows + rows // 8, kv_width), BF16)
    summed = ((rows, kv_width), F32)
    final = ((rows + 16, kv_width), BF16)

    def step(function, *operands):
        shapes = jax.eval_shape(function, *operands)
        return lax.cond(
            place < 4,
            function,
            lambda *_: jax.tree.map(lambda x: jnp.zeros(x.shape, x.dtype), shapes),
            *operands,
        )

    def prepare(key_value_weight):
        return key_value_weight[0].reshape(slice_width, kv_width)

    weight = step(prepare, key_value_weight)

    def prepare_attention(queries, out_grad, adapt_up, doc_ids, weight):
        docs = doc_ids.astype(F32).reshape(1, rows)
        freqs = 1000000.0 ** (-jnp.arange(head // 2, dtype=F32) * 2.0 / head)
        positions = place * rows + jnp.arange(rows, dtype=jnp.int32)
        angles = positions.astype(F32)[:, None] * freqs
        cosine, sine = jnp.cos(angles), jnp.sin(angles)
        cosine = jnp.concatenate([cosine, cosine], axis=1)
        sine = jnp.concatenate([-sine, sine], axis=1)
        (query,) = call(
            query_kernel,
            [((head_count * rows, head), BF16)],
            queries[0].reshape(rows, local_query),
            cosine,
            sine,
        )
        (back_part,) = call(
            back_kernel,
            [((rows, rank), F32)],
            out_grad[0],
            adapt_up[0],
            flops=2 * rows * local_width * rank,
        )
        return docs, cosine, sine, query, back_part, swap(back_part, "tp", 1)

    docs, cosine, sine, query, back_part, back_other = step(
        prepare_attention, queries, out_grad, adapt_up, doc_ids, weight
    )
    def swap_own(even):
        return swap(even, "tp", 1)

    even_other = step(swap_own, even)
    part_0, weight_near = call(
        functools.partial(own_kernel, head),
        [summed, (weight.shape, BF16)],
        even,
        even_other,
        weight,
        flops=part_flops,
        scratch=[pltpu.VMEM((rows, slice_width), BF16), pltpu.SemaphoreType.DMA],
        loose=(2,),
    )
    got_c, part_0, docs = lax.optimization_barrier((got_c, part_0, docs))

    def far_parts(got_c, weight):
        return call(
            functools.partial(far_kernel, head),
            [packed],
            got_c,
            swap(got_c, "tp", 1),
            weight,
            flops=part_flops,
            scratch=[pltpu.VMEM((rows, slice_width), BF16)],
        )

    (sent_c,) = step(far_parts, got_c, weight)
    arrived_c = swap(sent_c, "ctx", 3)
    got_a, got_b, sent_c = lax.optimization_barrier((got_a, got_b, sent_c))
    sent_a, sent_b = call(
        functools.partial(near_kernel, head),
        [packed, packed],
        got_a,
        swap(got_a, "tp", 1),
        got_b,
        swap(got_b, "tp", 1),
        weight_near,
        flops=2 * part_flops,
        scratch=[pltpu.VMEM((2 * rows, slice_width), BF16)],
    )
    arrived_a, arrived_b = send_a(sent_a), send_b(sent_b)
    part_0, back_rows, docs, cosine, sine, staged_down = call(
        accumulate_kernel,
        [
            summed,
            ((rows, rank), BF16),
            ((1, rows), F32),
            ((rows, head), F32),
            ((rows, head), F32),
            ((rank, local_query), BF16),
        ],
        part_0,
        arrived_c,
        back_part,
        back_other,
        docs,
        cosine,
        sine,
        adapt_down[0],
    )
    arrived_a, arrived_b, part_0 = lax.optimization_barrier((arrived_a, arrived_b, part_0))
    (block_0,) = call(finish_kernel, [final], part_0, arrived_a, arrived_b, docs, cosine, sine)

    attended, low_part, down_part = call(
        functools.partial(attention_kernel, head),
        [((rows, local_query), BF16), ((rows, rank), F32), ((rank, local_query), F32)],
        query,
        block_0,
        send_a(block_0),
        send_b(block_0),
        swap(block_0, "ctx", 3),
        staged_down,
        back_rows,
        flops=16 * rows * rows * local_query,
        scratch=[
            pltpu.VMEM((rows, local_query), BF16),
            pltpu.SemaphoreType.DMA((head_count // 2,)),
        ],
        loose_outs=(0,),
    )
    low_other = swap(low_part, "tp", 1)
    piece = (rank, (local_width + local_query) // 2)
    own, sent = call(
        grads_kernel,
        [(piece, F32), (piece, BF16)],
        low_part,
        low_other,
        out_grad[0],
        down_part,
        flops=2 * rows * rank * local_width,
    )
    (adapter_rows,) = call(
        adapter_kernel,
        [((rows, local_width), BF16)],
        low_part,
        low_other,
        adapt_up[0],
        flops=2 * rows * rank * local_width,
    )
    got_sum, adapter_rows = lax.optimization_barrier((swap(sent, "ctx", 1), adapter_rows))
    (pair_sum,) = call(add_kernel, [(piece, BF16)], own, got_sum)
    total, squares = call(
        total_kernel, [(piece, BF16), ((8, 128), F32)], pair_sum, swap(pair_sum, "ctx", 2)
    )
    total_other = swap(total, "ctx", 1)
    squares = squares + swap(squares, "tp", 1)
    squares = squares + swap(squares, "section", 1)
    squares = squares + swap(squares, "section", 2)
    squares = squares + swap(squares, "ctx", 1)
    ceiling = 0.5 * math.sqrt(lax.axis_size("section") * rank * (local_query + local_width) * 2)
    grad_up, grad_down = call(
        functools.partial(clip_kernel, ceiling),
        [((rank, local_width), F32), ((rank, local_query), F32)],
        squares,
        total,
        total_other,
    )
    return (attended[None], adapter_rows[None], grad_down[None], grad_up[None])


def per_device(*arrays):
    if lax.axis_size("ctx") == 4 and lax.axis_size("tp") == 2 and lax.axis_size("section") == 4:
        return split_model_width(*arrays)
    return gathered_weights(*arrays)


def solution(mesh):
    return jax.shard_map(
        per_device,
        mesh=mesh,
        in_specs=(
            P("section", "ctx", "tp"),
            P("section", "tp"),
            P("section", "ctx", "tp", None),
            P("section", "ctx", "tp", None, None),
            P("section", None, "tp"),
            P("section", None, "tp"),
            P("section", "ctx", "tp"),
            P("ctx"),
        ),
        out_specs=(
            P("section", "ctx", "tp"),
            P("section", "ctx", "tp"),
            P("section", None, "tp"),
            P("section", None, "tp"),
        ),
        check_vma=False,
    )
```
